128 devices in a mesh: bl: 16 (over x, y_hi, core), ch: 8 (over z, y_lo).
Axes of the slice: x: 4, y: 4 (y_hi: 2, y_lo: 2; y = y_hi * 2 + y_lo), z: 4, core: 2. Of those that a mesh axis runs over, the one named last changes fastest.
Arguments:
- uvw_index: int32 [2048], P('bl'), may hold values from 0 to 4095
- row_baseline: int32 [2048], P('bl'), may hold values from 0 to 2015
- flags: int32 [2048, 256], P('bl', 'ch'), may hold values 0 or 1
- uvw_table: bfloat16 [64, 4096], replicated, may hold values from -6 to 6
- baseline_features: bfloat16 [64, 2016], replicated, may hold values from -6 to 6
- w_in: bfloat16 [64, 64], replicated, may hold values from -0.75 to 0.75
- w_out: bfloat16 [64, 2, 65536], P(None, None, 'ch'), may hold values from -0.75 to 0.75
- observed: bfloat16 [2, 65536, 2048], P(None, 'ch', 'bl'), may hold values from -6 to 6
- delay_weight: float32 [65536], replicated, may hold values from 0.25 to 4
Outputs:
- grad_out: float32 [64, 2, 65536], P('bl', None, 'ch')
- grad_in: float32 [64, 64], replicated
- grad_uvw: float32 [64, 4096], replicated
- grad_base: float32 [64, 2016], replicated
The draws below stay inside these ranges and needn't reach their ends.
All inputs are finite; a program needn't handle non-finite values. No bound on the sum of `flags` on one device may be relied on, other than what follows from the above.
Results may differ from the reference program's by a relative error of at most 0.00035.
The reference program's roundings to bfloat16 on the way (of `inputs`, `hidden` and `grad_field`) count: a program that leaves them out, or rounds other values in their place, can miss the bound.
Values sent between devices are 32-bit elements; how exact they have to be, the bound alone decides.
No kernel may reach another device: no remote copies, remote signals or barrier semaphores. Data moves between devices by JAX's collectives and lax.ppermute only.
A program may use at most 128 MiB of HBM per device.

```python
import math
import jax
import jax.numpy as jnp
import numpy as np
from jax import lax

R_DEV = 128
TOTAL_ROWS = 2048
BLOCK = 256
NBLOCKS = 256
CHANNELS = 65536
HIDDEN_SIZE = 64
GRID_CELLS = 4096
BASELINE_COUNT = 2016
N_BL = 16


def place_ends(values, own_key, smallest, high):
    extent = values.shape
    index_at = [jax.random.randint(jax.random.fold_in(own_key, axis), (), 0, extent[axis]) for axis in range(len(extent))]
    values = values.at[tuple(index_at)].set(smallest)
    longest = extent.index(max(extent))
    index_at[longest] = (index_at[longest] + 1) % extent[longest]
    return values.at[tuple(index_at)].set(high)


def block_scale(own_key, shape, split, least, largest):
    gain, own = 1.0, jax.random.fold_in(own_key, 6)
    for position, shards_of in split:
        draws = jnp.exp(jax.random.uniform(jax.random.fold_in(own, position), (shards_of,), jnp.float32, least / len(split), largest / len(split)))
        gain = gain * jnp.repeat(draws, shape[position] // shards_of).reshape([-1 if axis == position else 1 for axis in range(len(shape))])
    return gain


def cumulative_ranks(number_of, skew):
    weights = [(1 << 20) // math.isqrt(rank ** skew) + 1 for rank in range(1, number_of + 1)]
    scale = 1 + sum(weights) // (1 << 30)
    return np.cumsum(np.array([max(1, weight // scale) for weight in weights]))


def ranked_ids(rng, shape, amount, lean):
    listing = cumulative_ranks(amount, lean)
    lot = jax.random.randint(jax.random.fold_in(rng, 1), shape, 0, int(listing[amount - 1]))
    rank = jnp.searchsorted(jnp.asarray(listing, jnp.int32), lot, side="right")
    return jax.random.permutation(jax.random.fold_in(rng, 2), amount)[rank].astype(jnp.int32)


def bell_draw(own_key, extent, width, most, shards=(), held_as=jnp.bfloat16):
    array = jax.random.normal(own_key, extent, jnp.float32) * width
    if len(shards) > 0:
        array = block_scale(own_key, extent, shards, -0.22, 0.18) * array
    return jnp.clip(array, min=-most, max=most).astype(held_as)


def setup_inputs(seed: int = 0) -> dict:
    seeds = jax.random.split(jax.random.key(seed), 10)
    uvw_index = place_ends(ranked_ids(seeds[0], (TOTAL_ROWS,), GRID_CELLS, 2), jax.random.fold_in(seeds[0], 3), 0, GRID_CELLS - 1).astype(jnp.int32)
    row_baseline = place_ends(jax.random.randint(seeds[1], (TOTAL_ROWS,), 0, BASELINE_COUNT), jax.random.fold_in(seeds[1], 1), 0, BASELINE_COUNT - 1).astype(jnp.int32)
    flags = place_ends((jax.random.randint(seeds[2], (TOTAL_ROWS, NBLOCKS), 0, 8) < 1).astype(jnp.int32), jax.random.fold_in(seeds[2], 1), 0, 1)
    uvw_table = bell_draw(seeds[3], (HIDDEN_SIZE, GRID_CELLS), 0.7, 6.0)
    baseline_features = bell_draw(seeds[4], (HIDDEN_SIZE, BASELINE_COUNT), 0.7, 6.0)
    w_in = bell_draw(seeds[5], (HIDDEN_SIZE, HIDDEN_SIZE), HIDDEN_SIZE ** -0.5, 0.75)
    w_out = bell_draw(seeds[6], (HIDDEN_SIZE, 2, CHANNELS), HIDDEN_SIZE ** -0.5, 0.75, ((2, 8),))
    observed = bell_draw(seeds[7], (2, CHANNELS, TOTAL_ROWS), 1.0, 6.0, ((1, 8), (2, 16)))
    delay_weight = jnp.clip(jnp.exp(jax.random.uniform(seeds[8], (CHANNELS,), jnp.float32, math.log(0.25), math.log(4.0))), 0.25, 4.0)
    return {"uvw_index": uvw_index, "row_baseline": row_baseline, "flags": flags, "uvw_table": uvw_table, "baseline_features": baseline_features, "w_in": w_in, "w_out": w_out, "observed": observed, "delay_weight": delay_weight}


loss_scale = 0.0625
highest = lax.Precision.HIGHEST


def angle_of(product, period):
    return (product % period).astype(jnp.float32) * (2.0 * math.pi / period)


def taper_values(length):
    channel_number = jnp.arange(length, dtype=jnp.int32)
    window = jnp.full((length,), 0.35875, jnp.float32)
    for harmonic, weight_term in ((1, -0.48829), (2, 0.14128), (3, -0.01168)):
        window = window + weight_term * jnp.cos(angle_of(channel_number * harmonic, CHANNELS))
    return window


def reference(uvw_index, row_baseline, flags, uvw_table, baseline_features, w_in, w_out, observed, delay_weight):
    taper = taper_values(CHANNELS)
    w_in_wide = w_in.astype(jnp.float32)
    w_out_wide = w_out.astype(jnp.float32)

    def block_step(running, block_number):
        grad_out, grad_in, grad_uvw, grad_base = running
        row_start = block_number * R_DEV
        cells = lax.dynamic_slice_in_dim(uvw_index, row_start, R_DEV, 0)
        bases = lax.dynamic_slice_in_dim(row_baseline, row_start, R_DEV, 0)
        kept_share = 1.0 - lax.dynamic_slice_in_dim(flags, row_start, R_DEV, 0).astype(jnp.float32)
        seen = lax.dynamic_slice_in_dim(observed, row_start, R_DEV, 2).astype(jnp.float32)
        summed = jnp.take(uvw_table, cells, axis=1).astype(jnp.float32) + jnp.take(baseline_features, bases, axis=1).astype(jnp.float32)
        inputs = summed.astype(jnp.bfloat16)
        pre_act = jnp.dot(w_in.T, inputs, preferred_element_type=jnp.float32)
        hidden = jax.nn.silu(pre_act).astype(jnp.bfloat16)
        hidden_wide = hidden.astype(jnp.float32)
        field = jnp.einsum("jqc,jr->qcr", w_out_wide, hidden_wide)
        weight = (kept_share.T[:, None, :] * taper.reshape(NBLOCKS, BLOCK)[:, :, None]).reshape(CHANNELS, R_DEV)
        residual_vis = (field - seen) * weight[None]
        delay_spectrum = jnp.fft.fft(residual_vis[0] + 1j * residual_vis[1], axis=0)
        back = jnp.fft.ifft(delay_spectrum * delay_weight[:, None], axis=0) * loss_scale
        grad_field = (jnp.stack([jnp.real(back), jnp.imag(back)]) * weight[None]).astype(jnp.bfloat16)
        field_wide = grad_field.astype(jnp.float32)
        grad_out = grad_out + jnp.einsum("jr,qcr->jqc", hidden_wide, field_wide)
        hidden_grad = jnp.einsum("jqc,qcr->jr", w_out_wide, field_wide)
        sigmoid_part = jax.nn.sigmoid(pre_act)
        pre_grad = hidden_grad * sigmoid_part * (1.0 + pre_act * (1.0 - sigmoid_part))
        grad_in = grad_in + jnp.dot(inputs.astype(jnp.float32), pre_grad.T, precision=highest)
        input_grad = jnp.dot(w_in_wide, pre_grad, precision=highest)
        grad_uvw = grad_uvw.at[:, cells].add(input_grad)
        grad_base = grad_base.at[:, bases].add(input_grad)
        return (grad_out, grad_in, grad_uvw, grad_base), None

    start_state = (jnp.zeros((HIDDEN_SIZE, 2, CHANNELS), jnp.float32), jnp.zeros((HIDDEN_SIZE, HIDDEN_SIZE), jnp.float32),
                   jnp.zeros((HIDDEN_SIZE, GRID_CELLS), jnp.float32), jnp.zeros((HIDDEN_SIZE, BASELINE_COUNT), jnp.float32))
    final_state, _ = lax.scan(block_step, start_state, jnp.arange(N_BL, dtype=jnp.int32))
    grad_out, grad_in, grad_uvw, grad_base = final_state
    return (grad_out, grad_in, grad_uvw, grad_base)
```

```python
import functools
import math

import jax
import jax.numpy as jnp
import ml_dtypes
import numpy as np
from jax import lax
from jax.experimental import pallas as pl
from jax.experimental.pallas import tpu as pltpu
from jax.sharding import PartitionSpec as P

BLOCK = 256
NBLOCKS = 256
CHANNELS = 65536
LOSS_SCALE = 0.0625
HIGHEST = lax.Precision.HIGHEST
F32 = jnp.float32
BF16 = jnp.bfloat16
STEP = 8
WIDE = STEP * BLOCK
LANES = 128
PLANES = 4
VMEM = 56 * 2**20


def split_matrix(matrix):
    high = matrix.astype(ml_dtypes.bfloat16)
    low = (matrix - high.astype(np.float64)).astype(ml_dtypes.bfloat16)
    return high, low


def tables():
    n = np.arange(BLOCK)
    product = np.outer(n, n)
    cosine = np.cos(2 * math.pi * (product % BLOCK) / BLOCK)
    sine = np.sin(2 * math.pi * (product % BLOCK) / BLOCK)
    forward = np.block([[cosine, sine], [-sine, cosine]])
    backward = np.block([[cosine, -sine], [sine, cosine]])
    twiddle = 2 * math.pi * product / CHANNELS
    return (
        *split_matrix(forward),
        *split_matrix(backward),
        np.cos(twiddle).astype(np.float32),
        np.sin(twiddle).astype(np.float32),
    )


def taper_table():
    c = np.arange(CHANNELS)
    window = np.full((CHANNELS,), 0.35875)
    for harmonic, term in ((1, -0.48829), (2, 0.14128), (3, -0.01168)):
        window = window + term * np.cos(2 * math.pi * ((c * harmonic) % CHANNELS) / CHANNELS)
    return window.astype(np.float32).reshape(1, CHANNELS)


def dot(a, b, dims=(((1,), (0,)), ((), ())), precision=None):
    return lax.dot_general(a, b, dims, precision=precision, preferred_element_type=F32)


NT = (((1,), (1,)), ((), ()))
TN = (((0,), (0,)), ((), ()))


def params(**more):
    return pltpu.CompilerParams(vmem_limit_bytes=VMEM, **more)


def one_hot_rows(index_row, count):
    cells = lax.broadcasted_iota(jnp.int32, (count, index_row.shape[1]), 0)
    return jnp.where(cells == index_row, 1.0, 0.0).astype(BF16)


def trunk_kernel(uvw_ref, base_ref, flags_ref, table_ref, features_ref, w_in_ref,
                 inputs_ref, hidden_ref, hidden_t_ref, keep_ref):
    summed = dot(table_ref[...], one_hot_rows(uvw_ref[...], table_ref.shape[1]))
    summed = summed + dot(features_ref[...], one_hot_rows(base_ref[...], features_ref.shape[1]))
    inputs = summed.astype(BF16)
    inputs_ref[...] = inputs.astype(F32)
    pre_act = dot(w_in_ref[...], inputs, TN)
    hidden = pre_act / (1.0 + jnp.exp(-pre_act))
    hidden_ref[...] = hidden.astype(BF16)
    hidden_t_ref[...] = hidden.T.astype(BF16)
    keep_ref[...] = (1.0 - flags_ref[...].astype(F32)).T.astype(BF16)


def trunk(uvw_index, row_baseline, flags, uvw_table, baseline_features, w_in):
    rows = uvw_index.shape[0]
    units = w_in.shape[1]
    return pl.pallas_call(
        trunk_kernel,
        out_shape=(
            jax.ShapeDtypeStruct((w_in.shape[0], rows), F32),
            jax.ShapeDtypeStruct((units, rows), BF16),
            jax.ShapeDtypeStruct((rows, units), BF16),
            jax.ShapeDtypeStruct(flags.shape, BF16),
        ),
        compiler_params=params(),
        name="trunk",
    )(uvw_index[None], row_baseline[None], flags.T, uvw_table, baseline_features, w_in)


def weight_of(keep, taper_row, first_block):
    blocks = keep.shape[1]
    block = lax.broadcasted_iota(jnp.int32, (blocks, WIDE), 0)
    lane = lax.broadcasted_iota(jnp.int32, (blocks, WIDE), 1)
    expand = jnp.where(block == first_block + (lane >> 8), 1.0, 0.0).astype(BF16)
    return dot(keep, expand) * taper_row


def residual_kernel(half, hidden_ref, w_ref, observed_ref, keep_ref, taper_ref, out_ref):
    rows = hidden_ref.shape[0]
    total = observed_ref.shape[2]
    weight = weight_of(keep_ref[...], taper_ref[...], pl.program_id(0) * STEP)
    row = lax.broadcasted_iota(jnp.int32, (rows, total), 0)
    column = lax.broadcasted_iota(jnp.int32, (rows, total), 1)
    pick = jnp.where(column == row + half * rows, -1.0, 0.0).astype(BF16)
    flat = out_ref.reshape(rows * PLANES * STEP, LANES)
    for q in range(2):
        residual = dot(hidden_ref[...], w_ref[q]) + dot(pick, observed_ref[q], NT)
        residual = residual * weight
        for b in range(STEP):
            for side in range(2):
                start = b * BLOCK + side * LANES
                flat[pl.ds((q * 2 + side) * STEP + b, rows, stride=PLANES * STEP), :] = residual[
                    :, start : start + LANES
                ]


def residual_part(half, halves, hidden_t, w, observed, keep, taper):
    rows = hidden_t.shape[0] // halves
    blocks = keep.shape[1]
    return pl.pallas_call(
        functools.partial(residual_kernel, half),
        grid=(blocks // STEP,),
        in_specs=[
            pl.BlockSpec((rows, hidden_t.shape[1]), lambda g: (half, 0)),
            pl.BlockSpec((2, w.shape[1], WIDE), lambda g: (0, 0, g)),
            pl.BlockSpec((2, WIDE, observed.shape[2]), lambda g: (0, g, 0)),
            pl.BlockSpec((rows, blocks), lambda g: (half, 0)),
            pl.BlockSpec((1, WIDE), lambda g: (0, g)),
        ],
        out_specs=pl.BlockSpec((rows, PLANES, STEP, LANES), lambda g: (0, 0, g, 0)),
        out_shape=jax.ShapeDtypeStruct((rows, PLANES, blocks, LANES), F32),
        compiler_params=params(),
        cost_estimate=pl.CostEstimate(
            flops=2 * rows * 2 * blocks * BLOCK * 192, bytes_accessed=10 * 2**20, transcendentals=0
        ),
        name=f"residual_{half}",
    )(hidden_t, w, observed, keep, taper)


def halves_of(values):
    high = values.astype(BF16)
    return high, (values - high.astype(F32)).astype(BF16)


def dot_three(a, b):
    return dot(a[0], b[0]) + (dot(a[0], b[1]) + dot(a[1], b[0]))


def delay_kernel(pieces, x_ref, fh_ref, fl_ref, bh_ref, bl_ref, cos_ref, sin_ref, weight_ref, *outs):
    forward = (fh_ref[...], fl_ref[...])
    backward = (bh_ref[...], bl_ref[...])
    cosine, sine = cos_ref[...], sin_ref[...]
    count = x_ref.shape[1]
    members, local = x_ref.shape[0], x_ref.shape[3]
    turned = []
    for i in range(count):
        values = jnp.concatenate(
            [
                jnp.concatenate(
                    [x_ref[:, i, q * 2 + side].reshape(NBLOCKS, LANES) for side in range(2)], axis=1
                )
                for q in range(2)
            ],
            axis=0,
        )
        first = dot_three(forward, halves_of(values))
        real, imag = first[:NBLOCKS], first[NBLOCKS:]
        turned.append(
            jnp.concatenate([real * cosine + imag * sine, imag * cosine - real * sine], axis=1)
        )
    second = dot_three(halves_of(jnp.concatenate(turned, axis=0)), backward)
    factor = weight_ref[...] * (LOSS_SCALE / CHANNELS)
    factor = jnp.concatenate([jnp.concatenate([factor, factor], axis=1)] * count, axis=0)
    third = dot_three(halves_of(second * factor), forward)
    for i in range(count):
        part = third[i * NBLOCKS : (i + 1) * NBLOCKS]
        real, imag = part[:, :BLOCK], part[:, BLOCK:]
        back = jnp.concatenate([real * cosine - imag * sine, imag * cosine + real * sine], axis=0)
        fourth = dot_three(backward, halves_of(back))
        for q in range(2):
            for member in range(members):
                start = q * NBLOCKS + member * local
                for out_ref, size in zip(outs, pieces):
                    for side in range(2):
                        out_ref[member, i, q * 2 + side] = fourth[
                            start : start + size, side * LANES : (side + 1) * LANES
                        ]
                    start += size


def delay_filter(pieces, arrived, constants, weight, count=2):
    members, rows, _, local, _ = arrived.shape
    whole = lambda array: pl.BlockSpec(array.shape, lambda g: (0, 0))
    flops = rows * 4 * 3 * 2 * 512 * 512 * 256
    return pl.pallas_call(
        functools.partial(delay_kernel, pieces),
        grid=(rows // count,),
        in_specs=[
            pl.BlockSpec((members, count, PLANES, local, LANES), lambda g: (0, g, 0, 0, 0)),
            *[whole(array) for array in constants],
            whole(weight),
        ],
        out_specs=[
            pl.BlockSpec((members, count, PLANES, size, LANES), lambda g: (0, g, 0, 0, 0))
            for size in pieces
        ],
        out_shape=[
            jax.ShapeDtypeStruct((members, rows, PLANES, size, LANES), F32) for size in pieces
        ],
        compiler_params=params(),
        cost_estimate=pl.CostEstimate(flops=flops, bytes_accessed=12 * 2**20, transcendentals=0),
        name=f"delay_{len(pieces)}",
    )(arrived, *constants, weight)


def tail_kernel(first, g1_ref, g2_ref, hidden_ref, w_ref, keep_ref, taper_ref,
                mine_ref, other_ref, hidden_grad_ref):
    step = pl.program_id(0)
    weight = weight_of(keep_ref[...], taper_ref[...], (first + step) * STEP)
    rows = g1_ref.shape[0]
    flats = [ref.reshape(rows * PLANES * STEP, LANES) for ref in (g1_ref, g2_ref)]

    @pl.when(step == 0)
    def _():
        hidden_grad_ref[...] = jnp.zeros_like(hidden_grad_ref)

    total = hidden_grad_ref[...]
    for q in range(2):
        values = jnp.concatenate(
            [
                jnp.concatenate(
                    [
                        flat[pl.ds((q * 2 + side) * STEP + b, rows, stride=PLANES * STEP), :]
                        for b in range(STEP)
                        for side in range(2)
                    ],
                    axis=1,
                )
                for flat in flats
            ],
            axis=0,
        )
        grad_field = (values * weight).astype(BF16)
        grad_out = dot(hidden_ref[...], grad_field)
        units = grad_out.shape[0] // 2
        for d in range(4):
            mine_ref[d, q] = grad_out[d * 8 : (d + 1) * 8]
            other_ref[d, q] = grad_out[units + d * 8 : units + (d + 1) * 8]
        total = total + dot(w_ref[q], grad_field, NT)
    hidden_grad_ref[...] = total


def tail_part(first, count, g1, g2, hidden_order, w, keep, taper):
    rows = g1.shape[0]
    units, total_rows = hidden_order.shape
    return pl.pallas_call(
        functools.partial(tail_kernel, first),
        grid=(count,),
        in_specs=[
            pl.BlockSpec((rows, PLANES, STEP, LANES), lambda g: (0, 0, first + g, 0)),
            pl.BlockSpec((rows, PLANES, STEP, LANES), lambda g: (0, 0, g, 0)),
            pl.BlockSpec((units, total_rows), lambda g: (0, 0)),
            pl.BlockSpec((2, units, WIDE), lambda g: (0, 0, first + g)),
            pl.BlockSpec(keep.shape, lambda g: (0, 0)),
            pl.BlockSpec((1, WIDE), lambda g: (0, first + g)),
        ],
        out_specs=[
            pl.BlockSpec((4, 2, 8, WIDE), lambda g: (0, 0, 0, g)),
            pl.BlockSpec((4, 2, 8, WIDE), lambda g: (0, 0, 0, g)),
            pl.BlockSpec((units, total_rows), lambda g: (0, 0)),
        ],
        out_shape=[
            jax.ShapeDtypeStruct((4, 2, 8, count * WIDE), F32),
            jax.ShapeDtypeStruct((4, 2, 8, count * WIDE), F32),
            jax.ShapeDtypeStruct((units, total_rows), F32),
        ],
        compiler_params=params(),
        cost_estimate=pl.CostEstimate(
            flops=count * 2 * 2 * 2 * 64 * 128 * WIDE, bytes_accessed=count * 4 * 2**20, transcendentals=0
        ),
        name=f"tail_{first}",
    )(g1, g2, hidden_order, w, keep, taper)


def terms_of(values, count):
    out = []
    for _ in range(count):
        term = values.astype(BF16)
        out.append(term)
        values = values - term.astype(F32)
    return out


def scatter_kernel(hidden_grad_ref, inputs_ref, index_ref, w_in_ref, w_in_t_ref,
                   grad_in_ref, grad_uvw_ref, grad_base_ref, terms_ref):
    inputs = inputs_ref[...].astype(BF16)
    pre_act = dot(w_in_t_ref[...], inputs)
    sigmoid = 1.0 / (1.0 + jnp.exp(-pre_act))
    pre_grad = hidden_grad_ref[...] * sigmoid * (1.0 + pre_act * (1.0 - sigmoid))
    grad_terms = jnp.concatenate(terms_of(pre_grad, 3), axis=0)
    units = pre_grad.shape[0]
    parts = dot(inputs, grad_terms, NT)
    grad_in_ref[...] = parts[:, :units] + (parts[:, units : 2 * units] + parts[:, 2 * units :])
    input_grad = jnp.zeros_like(pre_grad)
    for k in (2, 1, 0):
        input_grad = input_grad + dot(w_in_ref[...], grad_terms[k * units : (k + 1) * units])
    terms_ref[...] = jnp.concatenate(terms_of(input_grad, 3), axis=0)
    for which, out_ref in ((0, grad_uvw_ref), (1, grad_base_ref)):
        index = index_ref[which : which + 1, :].astype(jnp.int32)
        cells = out_ref.shape[1]
        for start in range(0, cells, 512):
            size = min(512, cells - start)
            picked = one_hot_rows(index - start, size)
            sums = dot(terms_ref[...], picked, NT)
            out_ref[:, start : start + size] = sums[:units] + (
                sums[units : 2 * units] + sums[2 * units :]
            )


def scatter(hidden_grad, inputs, index, w_in, cells, baselines):
    units, rows = hidden_grad.shape
    return pl.pallas_call(
        scatter_kernel,
        out_shape=[
            jax.ShapeDtypeStruct(w_in.shape, F32),
            jax.ShapeDtypeStruct((w_in.shape[0], cells), F32),
            jax.ShapeDtypeStruct((w_in.shape[0], baselines), F32),
        ],
        scratch_shapes=[pltpu.VMEM((3 * units, rows), BF16)],
        compiler_params=params(),
        name="scatter",
    )(hidden_grad, inputs, index, w_in, w_in.T)


def swap(values, axis, distance):
    size = lax.axis_size(axis)
    return lax.ppermute(values, axis, [(i, i ^ distance) for i in range(size)])


def gather_rows(values):
    me = lax.axis_index("bl")
    values = values[None]
    for distance in (8, 4, 2, 1):
        got = swap(values, "bl", distance)
        mine_first = (me & distance) == 0
        low = jnp.where(mine_first, values, got)
        high = jnp.where(mine_first, got, values)
        values = jnp.stack([low, high], axis=1).reshape(-1, *values.shape[1:])
    members, height, width = values.shape
    return values.transpose(1, 0, 2).reshape(height, members * width)


def sum_over_rows(mine, other):
    ring = lambda d: [(i, (i + 4 * d) % 16) for i in range(16)]
    both = mine + swap(other, "bl", 1)
    got = [lax.ppermute(both[d], "bl", ring(d)) for d in (1, 2, 3)]
    total = both[0] + got[0] + got[1] + got[2]
    return total[:, :4] + swap(total[:, 4:], "bl", 2)


def body(
    uvw_index, row_baseline, flags, uvw_table, baseline_features, w_in, w_out, observed, delay_weight
):
    members = lax.axis_size("ch")
    rows = uvw_index.shape[0]
    local_blocks = flags.shape[1]
    local_channels = w_out.shape[2]
    half_rows = rows // 2
    per = half_rows // members

    inputs, hidden, hidden_t, keep = trunk(
        uvw_index, row_baseline, flags, uvw_table, baseline_features, w_in
    )
    w = w_out.transpose(1, 0, 2)
    taper = lax.dynamic_slice_in_dim(
        jnp.asarray(taper_table()), lax.axis_index("ch") * local_channels, local_channels, 1
    )
    constants = [jnp.asarray(table) for table in tables()]
    weight = delay_weight.reshape(BLOCK, NBLOCKS).T

    def exchange(values):
        size = values.shape[-2]
        got = lax.all_to_all(
            values.reshape(members, per, PLANES, size, LANES), "ch", 0, 0, tiled=True
        )
        return got

    sent = [
        exchange(residual_part(half, 2, hidden_t, w, observed, keep, taper)) for half in range(2)
    ]
    (out_0,) = delay_filter((local_blocks,), sent[0], constants, weight)
    back_0 = exchange(out_0).reshape(half_rows, PLANES, local_blocks, LANES)
    pieces = (local_blocks // 2, local_blocks // 2)
    back_1 = [
        exchange(out).reshape(half_rows, PLANES, size, LANES)
        for out, size in zip(delay_filter(pieces, sent[1], constants, weight), pieces)
    ]

    me = lax.axis_index("bl")
    order = lax.broadcasted_iota(jnp.int32, hidden.shape[:1], 0)
    core, x_far, y_far, unit = order // 32, (order // 8) % 4, (order // 4) % 2, order % 4
    owner = ((me // 4 + x_far) % 4) * 4 + ((me // 2) % 2 ^ y_far) * 2 + (me % 2 ^ core)
    units = lax.broadcasted_iota(jnp.int32, (hidden.shape[0],) * 2, 1)
    turn = (units == (owner * 4 + unit)[:, None]).astype(BF16)
    hidden_order = dot(turn, hidden).astype(BF16)

    index_rows = jnp.stack([uvw_index, row_baseline]).astype(F32)
    early = jnp.concatenate([inputs, index_rows, jnp.zeros((6, rows), F32)], axis=0)
    early = gather_rows(early)

    first = 0
    grad_out = []
    hidden_grad = 0.0
    for piece, size in zip(back_1, pieces):
        count = size // STEP
        mine, other, grad = tail_part(
            first, count, back_0, piece, hidden_order, w, keep, taper
        )
        hidden_grad = hidden_grad + grad
        grad_out.append(sum_over_rows(mine, other))
        first += count
    grad_out = jnp.concatenate(grad_out, axis=2).transpose(1, 0, 2)

    for distance in (1, 2, 4):
        hidden_grad = hidden_grad + swap(hidden_grad, "ch", distance)
    hidden_grad = gather_rows(hidden_grad)
    inputs_all, index_all = early[: w_in.shape[0]], early[w_in.shape[0] :]
    grad_in, grad_uvw, grad_base = scatter(
        hidden_grad, inputs_all, index_all, w_in, uvw_table.shape[1], baseline_features.shape[1]
    )
    return (grad_out, grad_in, grad_uvw, grad_base)


def solution(mesh):
    return jax.shard_map(
        body,
        mesh=mesh,
        in_specs=(
            P("bl"),
            P("bl"),
            P("bl", "ch"),
            P(),
            P(),
            P(),
            P(None, None, "ch"),
            P(None, "ch", "bl"),
            P(),
        ),
        out_specs=(P("bl", None, "ch"), P(), P(), P()),
        check_vma=False,
    )
```

```python
import functools
import math

import jax
import jax.numpy as jnp
import ml_dtypes
import numpy as np
from jax import lax
from jax.experimental import pallas as pl
from jax.experimental.pallas import tpu as pltpu
from jax.sharding import PartitionSpec as P

BLOCK = 256
NBLOCKS = 256
CHANNELS = 65536
LOSS_SCALE = 0.0625
HIGHEST = lax.Precision.HIGHEST
F32 = jnp.float32
BF16 = jnp.bfloat16
STEP = 8
WIDE = STEP * BLOCK
LANES = 128
PLANES = 4
VMEM = 56 * 2**20


def split_matrix(matrix):
    high = matrix.astype(ml_dtypes.bfloat16)
    low = (matrix - high.astype(np.float64)).astype(ml_dtypes.bfloat16)
    return high, low


def tables():
    n = np.arange(BLOCK)
    product = np.outer(n, n)
    cosine = np.cos(2 * math.pi * (product % BLOCK) / BLOCK)
    sine = np.sin(2 * math.pi * (product % BLOCK) / BLOCK)
    forward = np.block([[cosine, sine], [-sine, cosine]])
    backward = np.block([[cosine, -sine], [sine, cosine]])
    twiddle = 2 * math.pi * product / CHANNELS
    return (
        *split_matrix(forward),
        *split_matrix(backward),
        np.cos(twiddle).astype(np.float32),
        np.sin(twiddle).astype(np.float32),
    )


def taper_table():
    c = np.arange(CHANNELS)
    window = np.full((CHANNELS,), 0.35875)
    for harmonic, term in ((1, -0.48829), (2, 0.14128), (3, -0.01168)):
        window = window + term * np.cos(2 * math.pi * ((c * harmonic) % CHANNELS) / CHANNELS)
    return window.astype(np.float32)


def dot(a, b, dims=(((1,), (0,)), ((), ())), precision=None):
    return lax.dot_general(a, b, dims, precision=precision, preferred_element_type=F32)


NT = (((1,), (1,)), ((), ()))
TN = (((0,), (0,)), ((), ()))


def params(**more):
    return pltpu.CompilerParams(vmem_limit_bytes=VMEM, **more)


def one_hot_rows(index_row, count):
    cells = lax.broadcasted_iota(jnp.int32, (count, index_row.shape[1]), 0)
    return jnp.where(cells == index_row, 1.0, 0.0).astype(BF16)


def trunk_kernel(uvw_ref, base_ref, flags_ref, table_ref, features_ref, w_in_ref, taper_ref,
                 inputs_ref, hidden_ref, hidden_t_ref, keep_ref, taper_here_ref):
    taper_here_ref[...] = taper_ref[pl.ds(lax.axis_index("ch"), 1), :]
    summed = dot(table_ref[...], one_hot_rows(uvw_ref[...], table_ref.shape[1]))
    summed = summed + dot(features_ref[...], one_hot_rows(base_ref[...], features_ref.shape[1]))
    inputs = summed.astype(BF16)
    inputs_ref[...] = inputs.astype(F32)
    pre_act = dot(w_in_ref[...], inputs, TN)
    hidden = pre_act / (1.0 + jnp.exp(-pre_act))
    hidden_ref[...] = hidden.astype(BF16)
    hidden_t_ref[...] = hidden.T.astype(BF16)
    keep_ref[...] = (1.0 - flags_ref[...].astype(F32)).T.astype(BF16)


def trunk(uvw_index, row_baseline, flags, uvw_table, baseline_features, w_in, taper):
    rows = uvw_index.shape[0]
    units = w_in.shape[1]
    return pl.pallas_call(
        trunk_kernel,
        out_shape=(
            jax.ShapeDtypeStruct((w_in.shape[0], rows), F32),
            jax.ShapeDtypeStruct((units, rows), BF16),
            jax.ShapeDtypeStruct((rows, units), BF16),
            jax.ShapeDtypeStruct(flags.shape, BF16),
            jax.ShapeDtypeStruct((1, taper.shape[1]), F32),
        ),
        compiler_params=params(),
        name="trunk",
    )(uvw_index[None], row_baseline[None], flags.T, uvw_table, baseline_features, w_in, taper)


def weight_of(keep, taper_row, first_block):
    blocks = keep.shape[1]
    block = lax.broadcasted_iota(jnp.int32, (blocks, WIDE), 0)
    lane = lax.broadcasted_iota(jnp.int32, (blocks, WIDE), 1)
    expand = jnp.where(block == first_block + (lane >> 8), 1.0, 0.0).astype(BF16)
    return dot(keep, expand) * taper_row


def residual_kernel(half, hidden_ref, w_ref, observed_ref, keep_ref, taper_ref, out_ref):
    rows = hidden_ref.shape[0]
    total = observed_ref.shape[2]
    weight = weight_of(keep_ref[...], taper_ref[...], pl.program_id(0) * STEP)
    row = lax.broadcasted_iota(jnp.int32, (rows, total), 0)
    column = lax.broadcasted_iota(jnp.int32, (rows, total), 1)
    pick = jnp.where(column == row + half * rows, -1.0, 0.0).astype(BF16)
    flat = out_ref.reshape(rows * PLANES * STEP, LANES)
    units = w_ref.shape[0]
    pairs = w_ref[...].reshape(2 * units, WIDE)
    unit = lax.broadcasted_iota(jnp.int32, (units, 2 * units), 0)
    place = lax.broadcasted_iota(jnp.int32, (units, 2 * units), 1)
    for q in range(2):
        spread = jnp.where(place == unit * 2 + q, 1.0, 0.0).astype(BF16)
        own = dot(hidden_ref[...], spread).astype(BF16)
        residual = dot(own, pairs) + dot(pick, observed_ref[q], NT)
        residual = residual * weight
        for b in range(STEP):
            for side in range(2):
                start = b * BLOCK + side * LANES
                flat[pl.ds((q * 2 + side) * STEP + b, rows, stride=PLANES * STEP), :] = residual[
                    :, start : start + LANES
                ]


def residual_part(half, halves, hidden_t, w, observed, keep, taper):
    rows = hidden_t.shape[0] // halves
    blocks = keep.shape[1]
    return pl.pallas_call(
        functools.partial(residual_kernel, half),
        grid=(blocks // STEP,),
        in_specs=[
            pl.BlockSpec((rows, hidden_t.shape[1]), lambda g: (half, 0)),
            pl.BlockSpec((w.shape[0], 2, WIDE), lambda g: (0, 0, g)),
            pl.BlockSpec((2, WIDE, observed.shape[2]), lambda g: (0, g, 0)),
            pl.BlockSpec((rows, blocks), lambda g: (half, 0)),
            pl.BlockSpec((1, WIDE), lambda g: (0, g)),
        ],
        out_specs=pl.BlockSpec((rows, PLANES, STEP, LANES), lambda g: (0, 0, g, 0)),
        out_shape=jax.ShapeDtypeStruct((rows, PLANES, blocks, LANES), F32),
        compiler_params=params(),
        cost_estimate=pl.CostEstimate(
            flops=2 * rows * 2 * blocks * BLOCK * 192, bytes_accessed=10 * 2**20, transcendentals=0
        ),
        name=f"residual_{half}",
    )(hidden_t, w, observed, keep, taper)


def halves_of(values):
    high = values.astype(BF16)
    return high, (values - high.astype(F32)).astype(BF16)


def dot_three(a, b):
    return dot(a[0], b[0]) + (dot(a[0], b[1]) + dot(a[1], b[0]))


def delay_kernel(pieces, x_ref, fh_ref, fl_ref, bh_ref, bl_ref, cos_ref, sin_ref, weight_ref, *outs):
    forward = (fh_ref[...], fl_ref[...])
    backward = (bh_ref[...], bl_ref[...])
    cosine, sine = cos_ref[...], sin_ref[...]
    count = x_ref.shape[1]
    members, local = x_ref.shape[0], x_ref.shape[3]
    turned = []
    for i in range(count):
        values = jnp.concatenate(
            [
                jnp.concatenate(
                    [x_ref[:, i, q * 2 + side].reshape(NBLOCKS, LANES) for side in range(2)], axis=1
                )
                for q in range(2)
            ],
            axis=0,
        )
        first = dot_three(forward, halves_of(values))
        real, imag = first[:NBLOCKS], first[NBLOCKS:]
        turned.append(
            jnp.concatenate([real * cosine + imag * sine, imag * cosine - real * sine], axis=1)
        )
    second = dot_three(halves_of(jnp.concatenate(turned, axis=0)), backward)
    factor = weight_ref[...] * (LOSS_SCALE / CHANNELS)
    factor = jnp.concatenate([jnp.concatenate([factor, factor], axis=1)] * count, axis=0)
    third = dot_three(halves_of(second * factor), forward)
    for i in range(count):
        part = third[i * NBLOCKS : (i + 1) * NBLOCKS]
        real, imag = part[:, :BLOCK], part[:, BLOCK:]
        back = jnp.concatenate([real * cosine - imag * sine, imag * cosine + real * sine], axis=0)
        fourth = dot_three(backward, halves_of(back))
        for q in range(2):
            for member in range(members):
                start = q * NBLOCKS + member * local
                for out_ref, size in zip(outs, pieces):
                    for side in range(2):
                        out_ref[member, i, q * 2 + side] = fourth[
                            start : start + size, side * LANES : (side + 1) * LANES
                        ]
                    start += size


def delay_filter(pieces, arrived, constants, weight, count=2):
    members, rows, _, local, _ = arrived.shape
    whole = lambda array: pl.BlockSpec(array.shape, lambda g: (0, 0))
    flops = rows * 4 * 3 * 2 * 512 * 512 * 256
    return pl.pallas_call(
        functools.partial(delay_kernel, pieces),
        grid=(rows // count,),
        in_specs=[
            pl.BlockSpec((members, count, PLANES, local, LANES), lambda g: (0, g, 0, 0, 0)),
            *[whole(array) for array in constants],
            whole(weight),
        ],
        out_specs=[
            pl.BlockSpec((members, count, PLANES, size, LANES), lambda g: (0, g, 0, 0, 0))
            for size in pieces
        ],
        out_shape=[
            jax.ShapeDtypeStruct((members, rows, PLANES, size, LANES), F32) for size in pieces
        ],
        compiler_params=params(),
        cost_estimate=pl.CostEstimate(flops=flops, bytes_accessed=12 * 2**20, transcendentals=0),
        name=f"delay_{len(pieces)}",
    )(arrived, *constants, weight)


def tail_kernel(first, g1_ref, g2_ref, hidden_ref, w_ref, keep_ref, taper_ref, before_ref,
                mine_ref, other_ref, hidden_grad_ref):
    step = pl.program_id(0)
    weight = weight_of(keep_ref[...], taper_ref[...], (first + step) * STEP)
    rows = g1_ref.shape[0]
    flats = [ref.reshape(rows * PLANES * STEP, LANES) for ref in (g1_ref, g2_ref)]

    @pl.when(step == 0)
    def _():
        hidden_grad_ref[...] = before_ref[...]

    total = hidden_grad_ref[...]
    for q in range(2):
        values = jnp.concatenate(
            [
                jnp.concatenate(
                    [
                        flat[pl.ds((q * 2 + side) * STEP + b, rows, stride=PLANES * STEP), :]
                        for b in range(STEP)
                        for side in range(2)
                    ],
                    axis=1,
                )
                for flat in flats
            ],
            axis=0,
        )
        grad_field = (values * weight).astype(BF16)
        grad_out = dot(hidden_ref[...], grad_field)
        units = grad_out.shape[0] // 2
        for d in range(4):
            mine_ref[d, q] = grad_out[d * 8 : (d + 1) * 8]
            other_ref[d, q] = grad_out[units + d * 8 : units + (d + 1) * 8]
        total = total + dot(w_ref[q], grad_field, NT)
    hidden_grad_ref[...] = total


def tail_part(first, count, g1, g2, hidden_order, w, keep, taper, before):
    rows = g1.shape[0]
    units, total_rows = hidden_order.shape
    return pl.pallas_call(
        functools.partial(tail_kernel, first),
        grid=(count,),
        in_specs=[
            pl.BlockSpec((rows, PLANES, STEP, LANES), lambda g: (0, 0, first + g, 0)),
            pl.BlockSpec((rows, PLANES, STEP, LANES), lambda g: (0, 0, g, 0)),
            pl.BlockSpec((units, total_rows), lambda g: (0, 0)),
            pl.BlockSpec((2, units, WIDE), lambda g: (0, 0, first + g)),
            pl.BlockSpec(keep.shape, lambda g: (0, 0)),
            pl.BlockSpec((1, WIDE), lambda g: (0, first + g)),
            pl.BlockSpec((units, total_rows), lambda g: (0, 0)),
        ],
        out_specs=[
            pl.BlockSpec((4, 2, 8, WIDE), lambda g: (0, 0, 0, g)),
            pl.BlockSpec((4, 2, 8, WIDE), lambda g: (0, 0, 0, g)),
            pl.BlockSpec((units, total_rows), lambda g: (0, 0)),
        ],
        out_shape=[
            jax.ShapeDtypeStruct((4, 2, 8, count * WIDE), F32),
            jax.ShapeDtypeStruct((4, 2, 8, count * WIDE), F32),
            jax.ShapeDtypeStruct((units, total_rows), F32),
        ],
        compiler_params=params(),
        cost_estimate=pl.CostEstimate(
            flops=count * 2 * 2 * 2 * 64 * 128 * WIDE, bytes_accessed=count * 4 * 2**20, transcendentals=0
        ),
        name=f"tail_{first}",
    )(g1, g2, hidden_order, w, keep, taper, before)


def terms_of(values, count):
    out = []
    for _ in range(count):
        term = values.astype(BF16)
        out.append(term)
        values = values - term.astype(F32)
    return out


def scatter_kernel(near_ref, far_ref, early_ref, w_in_ref, w_in_t_ref,
                   grad_in_ref, grad_uvw_ref, grad_base_ref, terms_ref):
    units = w_in_ref.shape[0]
    members = early_ref.shape[0]
    apart = [lax.axis_index("bl") ^ m for m in range(members)]
    spot = [((a >> 3) & 1) + ((a >> 2) & 1) * 2 + ((a >> 1) & 1) * 4 for a in apart]
    side = [a & 1 for a in apart]
    early_at = [spot[m] + 8 * side[m] for m in range(members)]
    inputs = jnp.concatenate([early_ref[e, :units] for e in early_at], axis=1).astype(BF16)
    hidden_grad = jnp.concatenate(
        [jnp.where(side[m] == 0, near_ref[spot[m]], far_ref[spot[m]]) for m in range(members)],
        axis=1,
    )
    pre_act = dot(w_in_t_ref[...], inputs)
    sigmoid = 1.0 / (1.0 + jnp.exp(-pre_act))
    pre_grad = hidden_grad * sigmoid * (1.0 + pre_act * (1.0 - sigmoid))
    grad_terms = jnp.concatenate(terms_of(pre_grad, 2), axis=0)
    parts = dot(inputs, grad_terms, NT)
    grad_in_ref[...] = parts[:, :units] + parts[:, units:]
    input_grad = dot(w_in_ref[...], grad_terms[:units]) + dot(w_in_ref[...], grad_terms[units:])
    terms_ref[...] = jnp.concatenate(terms_of(input_grad, 2), axis=0)
    for which, out_ref in ((0, grad_uvw_ref), (1, grad_base_ref)):
        row = units + which
        index = jnp.concatenate([early_ref[e, row : row + 1] for e in early_at], axis=1)
        index = index.astype(jnp.int32)
        cells = out_ref.shape[1]
        for start in range(0, cells, 512):
            size = min(512, cells - start)
            picked = one_hot_rows(index - start, size)
            sums = dot(terms_ref[...], picked, NT)
            out_ref[:, start : start + size] = sums[:units] + sums[units:]


def scatter(near, far, early, w_in, cells, baselines):
    members, _, rows = early.shape
    units = near.shape[1]
    return pl.pallas_call(
        scatter_kernel,
        out_shape=[
            jax.ShapeDtypeStruct(w_in.shape, F32),
            jax.ShapeDtypeStruct((w_in.shape[0], cells), F32),
            jax.ShapeDtypeStruct((w_in.shape[0], baselines), F32),
        ],
        scratch_shapes=[pltpu.VMEM((2 * units, members * rows), BF16)],
        compiler_params=params(),
        cost_estimate=pl.CostEstimate(
            flops=6 * 10**9, bytes_accessed=4 * 2**20, transcendentals=0
        ),
        name="scatter",
    )(near, far, early, w_in, w_in.T)


def swap(values, axis, distance):
    size = lax.axis_size(axis)
    return lax.ppermute(values, axis, [(i, i ^ distance) for i in range(size)])


def gather_step(values, distance):
    return jnp.concatenate([values, swap(values, "bl", distance)], axis=0)


def sum_cores(mine, other):
    return mine + swap(other, "bl", 1)


def sum_far(both):
    ring = lambda d: [(i, (i + 4 * d) % 16) for i in range(16)]
    got = [lax.ppermute(both[d], "bl", ring(d)) for d in (1, 2, 3)]
    return both[0] + got[0] + got[1] + got[2]


def sum_near(total):
    return total[:, :4] + swap(total[:, 4:], "bl", 2)


def together(*values):
    return lax.optimization_barrier(values)


def body(
    uvw_index, row_baseline, flags, uvw_table, baseline_features, w_in, w_out, observed, delay_weight
):
    members = lax.axis_size("ch")
    rows = uvw_index.shape[0]
    local_blocks = flags.shape[1]
    local_channels = w_out.shape[2]
    half_rows = rows // 2
    per = half_rows // members

    taper = jnp.asarray(taper_table()).reshape(members, local_channels)
    inputs, hidden, hidden_t, keep, taper = trunk(
        uvw_index, row_baseline, flags, uvw_table, baseline_features, w_in, taper
    )
    constants = [jnp.asarray(table) for table in tables()]
    weight = delay_weight.reshape(BLOCK, NBLOCKS).T

    def exchange(values):
        size = values.shape[-2]
        return lax.all_to_all(
            values.reshape(members, per, PLANES, size, LANES), "ch", 0, 0, tiled=True
        )

    sent = [
        exchange(residual_part(half, 2, hidden_t, w_out, observed, keep, taper))
        for half in range(2)
    ]

    index_rows = jnp.stack([uvw_index, row_baseline]).astype(F32)
    early = jnp.concatenate([inputs, index_rows, jnp.zeros((6, rows), F32)], axis=0)[None]
    for distance in (8, 4, 2, 1):
        early = gather_step(early, distance)
    me = lax.axis_index("bl")
    order = lax.broadcasted_iota(jnp.int32, hidden.shape[:1], 0)
    core, x_far, y_far, unit = order // 32, (order // 8) % 4, (order // 4) % 2, order % 4
    owner = ((me // 4 + x_far) % 4) * 4 + ((me // 2) % 2 ^ y_far) * 2 + (me % 2 ^ core)
    units = lax.broadcasted_iota(jnp.int32, (hidden.shape[0],) * 2, 1)
    turn = (units == (owner * 4 + unit)[:, None]).astype(BF16)
    hidden_order = dot(turn, hidden).astype(BF16)
    w = w_out.transpose(1, 0, 2)
    sent[0], early, hidden_order, w, weight = together(sent[0], early, hidden_order, w, weight)

    (out_0,) = delay_filter((local_blocks,), sent[0], constants, weight)
    back_0 = exchange(out_0).reshape(half_rows, PLANES, local_blocks, LANES)
    sizes = (local_blocks * 3 // 4, local_blocks // 4)
    parts = delay_filter(sizes, sent[1], constants, weight)
    piece_0, piece_1 = [
        exchange(part).reshape(half_rows, PLANES, size, LANES) for part, size in zip(parts, sizes)
    ]
    counts = [size // STEP for size in sizes]

    mine, other, hidden_grad = tail_part(
        0, counts[0], back_0, piece_0, hidden_order, w, keep, taper, jnp.zeros(hidden.shape, F32)
    )
    first = sum_cores(mine, other)
    piece_1, first = together(piece_1, first)
    first = sum_far(first)
    mine, other, hidden_grad = tail_part(
        counts[0], counts[1], back_0, piece_1, hidden_order, w, keep, taper, hidden_grad
    )
    second = sum_cores(mine, other)
    hidden_grad = hidden_grad + swap(hidden_grad, "ch", 1)
    hidden_grad, second = together(hidden_grad, second)
    second = sum_far(second)
    hidden_grad = hidden_grad + swap(hidden_grad, "ch", 2)
    hidden_grad = hidden_grad + swap(hidden_grad, "ch", 4)
    hidden_grad, first = together(hidden_grad, first)
    first = sum_near(first)
    gathered = gather_step(hidden_grad[None], 8)
    gathered, first = together(gathered, first)
    gathered = gather_step(gathered, 4)
    gathered, second = together(gathered, second)
    second = sum_near(second)
    gathered = gather_step(gathered, 2)
    far = swap(gathered, "bl", 1)
    grad_out = jnp.concatenate([first, second], axis=2).transpose(1, 0, 2)
    grad_in, grad_uvw, grad_base = scatter(
        gathered, far, early, w_in, uvw_table.shape[1], baseline_features.shape[1]
    )
    return (grad_out, grad_in, grad_uvw, grad_base)


def solution(mesh):
    return jax.shard_map(
        body,
        mesh=mesh,
        in_specs=(
            P("bl"),
            P("bl"),
            P("bl", "ch"),
            P(),
            P(),
            P(),
            P(None, None, "ch"),
            P(None, "ch", "bl"),
            P(),
        ),
        out_specs=(P("bl", None, "ch"), P(), P(), P()),
        check_vma=False,
    )
```

```python
import functools
import math

import jax
import jax.numpy as jnp
import ml_dtypes
import numpy as np
from jax import lax
from jax.experimental import pallas as pl
from jax.experimental.pallas import tpu as pltpu
from jax.sharding import PartitionSpec as P

BLOCK = 256
NBLOCKS = 256
CHANNELS = 65536
LOSS_SCALE = 0.0625
HIGHEST = lax.Precision.HIGHEST
F32 = jnp.float32
BF16 = jnp.bfloat16
STEP = 8
WIDE = STEP * BLOCK
LANES = 128
PLANES = 4
VMEM = 56 * 2**20


def split_matrix(matrix):
    high = matrix.astype(ml_dtypes.bfloat16)
    low = (matrix - high.astype(np.float64)).astype(ml_dtypes.bfloat16)
    return high, low


def tables():
    n = np.arange(BLOCK)
    product = np.outer(n, n)
    cosine = np.cos(2 * math.pi * (product % BLOCK) / BLOCK)
    sine = np.sin(2 * math.pi * (product % BLOCK) / BLOCK)
    forward = np.block([[cosine, sine], [-sine, cosine]])
    backward = np.block([[cosine, -sine], [sine, cosine]])
    twiddle = 2 * math.pi * product / CHANNELS
    return (
        *split_matrix(forward),
        *split_matrix(backward),
        np.cos(twiddle).astype(np.float32),
        np.sin(twiddle).astype(np.float32),
    )


def taper_table():
    c = np.arange(CHANNELS)
    window = np.full((CHANNELS,), 0.35875)
    for harmonic, term in ((1, -0.48829), (2, 0.14128), (3, -0.01168)):
        window = window + term * np.cos(2 * math.pi * ((c * harmonic) % CHANNELS) / CHANNELS)
    return window.astype(np.float32)


def dot(a, b, dims=(((1,), (0,)), ((), ())), precision=None):
    return lax.dot_general(a, b, dims, precision=precision, preferred_element_type=F32)


NT = (((1,), (1,)), ((), ()))
TN = (((0,), (0,)), ((), ()))


def params(**more):
    return pltpu.CompilerParams(vmem_limit_bytes=VMEM, **more)


def one_hot_rows(index_row, count):
    cells = lax.broadcasted_iota(jnp.int32, (count, index_row.shape[1]), 0)
    return jnp.where(cells == index_row, 1.0, 0.0).astype(BF16)


def trunk_kernel(uvw_ref, base_ref, flags_ref, table_ref, features_ref, w_in_ref, taper_ref,
                 inputs_ref, hidden_ref, hidden_t_ref, keep_ref, taper_here_ref):
    taper_here_ref[...] = taper_ref[pl.ds(lax.axis_index("ch"), 1), :]
    summed = dot(table_ref[...], one_hot_rows(uvw_ref[...], table_ref.shape[1]))
    summed = summed + dot(features_ref[...], one_hot_rows(base_ref[...], features_ref.shape[1]))
    inputs = summed.astype(BF16)
    inputs_ref[...] = inputs.astype(F32)
    pre_act = dot(w_in_ref[...], inputs, TN)
    hidden = pre_act / (1.0 + jnp.exp(-pre_act))
    hidden_ref[...] = hidden.astype(BF16)
    hidden_t_ref[...] = hidden.T.astype(BF16)
    keep_ref[...] = (1.0 - flags_ref[...].astype(F32)).T.astype(BF16)


def trunk(uvw_index, row_baseline, flags, uvw_table, baseline_features, w_in, taper):
    rows = uvw_index.shape[0]
    units = w_in.shape[1]
    return pl.pallas_call(
        trunk_kernel,
        out_shape=(
            jax.ShapeDtypeStruct((w_in.shape[0], rows), F32),
            jax.ShapeDtypeStruct((units, rows), BF16),
            jax.ShapeDtypeStruct((rows, units), BF16),
            jax.ShapeDtypeStruct(flags.shape, BF16),
            jax.ShapeDtypeStruct((1, taper.shape[1]), F32),
        ),
        compiler_params=params(),
        name="trunk",
    )(uvw_index[None], row_baseline[None], flags.T, uvw_table, baseline_features, w_in, taper)


def weight_of(keep, taper_row, first_block):
    blocks = keep.shape[1]
    block = lax.broadcasted_iota(jnp.int32, (blocks, WIDE), 0)
    lane = lax.broadcasted_iota(jnp.int32, (blocks, WIDE), 1)
    expand = jnp.where(block == first_block + (lane >> 8), 1.0, 0.0).astype(BF16)
    return dot(keep, expand) * taper_row


def residual_kernel(half, hidden_ref, w_ref, observed_ref, keep_ref, taper_ref, out_ref):
    rows = hidden_ref.shape[0]
    total = observed_ref.shape[2]
    weight = weight_of(keep_ref[...], taper_ref[...], pl.program_id(0) * STEP)
    row = lax.broadcasted_iota(jnp.int32, (rows, total), 0)
    column = lax.broadcasted_iota(jnp.int32, (rows, total), 1)
    pick = jnp.where(column == row + half * rows, -1.0, 0.0).astype(BF16)
    flat = out_ref.reshape(rows * PLANES * STEP, LANES)
    units = w_ref.shape[0]
    pairs = w_ref[...].reshape(2 * units, WIDE)
    unit = lax.broadcasted_iota(jnp.int32, (units, 2 * units), 0)
    place = lax.broadcasted_iota(jnp.int32, (units, 2 * units), 1)
    for q in range(2):
        spread = jnp.where(place == unit * 2 + q, 1.0, 0.0).astype(BF16)
        own = dot(hidden_ref[...], spread).astype(BF16)
        residual = dot(own, pairs) + dot(pick, observed_ref[q], NT)
        residual = residual * weight
        for b in range(STEP):
            for side in range(2):
                start = b * BLOCK + side * LANES
                flat[pl.ds((q * 2 + side) * STEP + b, rows, stride=PLANES * STEP), :] = residual[
                    :, start : start + LANES
                ]


def residual_part(half, halves, hidden_t, w, observed, keep, taper):
    rows = hidden_t.shape[0] // halves
    blocks = keep.shape[1]
    return pl.pallas_call(
        functools.partial(residual_kernel, half),
        grid=(blocks // STEP,),
        in_specs=[
            pl.BlockSpec((rows, hidden_t.shape[1]), lambda g: (half, 0)),
            pl.BlockSpec((w.shape[0], 2, WIDE), lambda g: (0, 0, g)),
            pl.BlockSpec((2, WIDE, observed.shape[2]), lambda g: (0, g, 0)),
            pl.BlockSpec((rows, blocks), lambda g: (half, 0)),
            pl.BlockSpec((1, WIDE), lambda g: (0, g)),
        ],
        out_specs=pl.BlockSpec((rows, PLANES, STEP, LANES), lambda g: (0, 0, g, 0)),
        out_shape=jax.ShapeDtypeStruct((rows, PLANES, blocks, LANES), F32),
        compiler_params=params(),
        cost_estimate=pl.CostEstimate(
            flops=2 * rows * 2 * blocks * BLOCK * 192, bytes_accessed=10 * 2**20, transcendentals=0
        ),
        name=f"residual_{half}",
    )(hidden_t, w, observed, keep, taper)


def halves_of(values):
    high = values.astype(BF16)
    return high, (values - high.astype(F32)).astype(BF16)


def dot_three(a, b):
    return dot(a[0], b[0]) + (dot(a[0], b[1]) + dot(a[1], b[0]))


def delay_kernel(pieces, x_ref, fh_ref, fl_ref, bh_ref, bl_ref, cos_ref, sin_ref, weight_ref, *outs):
    forward = (fh_ref[...], fl_ref[...])
    backward = (bh_ref[...], bl_ref[...])
    cosine, sine = cos_ref[...], sin_ref[...]
    count = x_ref.shape[1]
    members, local = x_ref.shape[0], x_ref.shape[3]
    turned = []
    for i in range(count):
        values = jnp.concatenate(
            [
                jnp.concatenate(
                    [x_ref[:, i, q * 2 + side].reshape(NBLOCKS, LANES) for side in range(2)], axis=1
                )
                for q in range(2)
            ],
            axis=0,
        )
        first = dot_three(forward, halves_of(values))
        real, imag = first[:NBLOCKS], first[NBLOCKS:]
        turned.append(
            jnp.concatenate([real * cosine + imag * sine, imag * cosine - real * sine], axis=1)
        )
    second = dot_three(halves_of(jnp.concatenate(turned, axis=0)), backward)
    factor = weight_ref[...] * (LOSS_SCALE / CHANNELS)
    factor = jnp.concatenate([jnp.concatenate([factor, factor], axis=1)] * count, axis=0)
    third = dot_three(halves_of(second * factor), forward)
    for i in range(count):
        part = third[i * NBLOCKS : (i + 1) * NBLOCKS]
        real, imag = part[:, :BLOCK], part[:, BLOCK:]
        back = jnp.concatenate([real * cosine - imag * sine, imag * cosine + real * sine], axis=0)
        fourth = dot_three(backward, halves_of(back))
        for q in range(2):
            for member in range(members):
                start = q * NBLOCKS + member * local
                for out_ref, size in zip(outs, pieces):
                    for side in range(2):
                        out_ref[member, i, q * 2 + side] = fourth[
                            start : start + size, side * LANES : (side + 1) * LANES
                        ]
                    start += size


def delay_filter(pieces, arrived, constants, weight, count=2):
    members, rows, _, local, _ = arrived.shape
    whole = lambda array: pl.BlockSpec(array.shape, lambda g: (0, 0))
    flops = rows * 4 * 3 * 2 * 512 * 512 * 256
    return pl.pallas_call(
        functools.partial(delay_kernel, pieces),
        grid=(rows // count,),
        in_specs=[
            pl.BlockSpec((members, count, PLANES, local, LANES), lambda g: (0, g, 0, 0, 0)),
            *[whole(array) for array in constants],
            whole(weight),
        ],
        out_specs=[
            pl.BlockSpec((members, count, PLANES, size, LANES), lambda g: (0, g, 0, 0, 0))
            for size in pieces
        ],
        out_shape=[
            jax.ShapeDtypeStruct((members, rows, PLANES, size, LANES), F32) for size in pieces
        ],
        compiler_params=params(),
        cost_estimate=pl.CostEstimate(flops=flops, bytes_accessed=12 * 2**20, transcendentals=0),
        name=f"delay_{len(pieces)}",
    )(arrived, *constants, weight)


def tail_kernel(first, g1_ref, g2_ref, hidden_ref, w_ref, keep_ref, taper_ref, before_ref,
                mine_ref, other_ref, hidden_grad_ref):
    step = pl.program_id(0)
    weight = weight_of(keep_ref[...], taper_ref[...], (first + step) * STEP)
    rows = g1_ref.shape[0]
    flats = [ref.reshape(rows * PLANES * STEP, LANES) for ref in (g1_ref, g2_ref)]

    @pl.when(step == 0)
    def _():
        hidden_grad_ref[...] = before_ref[...]

    total = hidden_grad_ref[...]
    for q in range(2):
        values = jnp.concatenate(
            [
                jnp.concatenate(
                    [
                        flat[pl.ds((q * 2 + side) * STEP + b, rows, stride=PLANES * STEP), :]
                        for b in range(STEP)
                        for side in range(2)
                    ],
                    axis=1,
                )
                for flat in flats
            ],
            axis=0,
        )
        grad_field = (values * weight).astype(BF16)
        grad_out = dot(hidden_ref[...], grad_field)
        units = grad_out.shape[0] // 2
        for d in range(4):
            mine_ref[d, q] = grad_out[d * 8 : (d + 1) * 8]
            other_ref[d, q] = grad_out[units + d * 8 : units + (d + 1) * 8]
        total = total + dot(w_ref[q], grad_field, NT)
    hidden_grad_ref[...] = total


def tail_part(first, count, g1, g2, hidden_order, w, keep, taper, before):
    rows = g1.shape[0]
    units, total_rows = hidden_order.shape
    return pl.pallas_call(
        functools.partial(tail_kernel, first),
        grid=(count,),
        in_specs=[
            pl.BlockSpec((rows, PLANES, STEP, LANES), lambda g: (0, 0, first + g, 0)),
            pl.BlockSpec((rows, PLANES, STEP, LANES), lambda g: (0, 0, g, 0)),
            pl.BlockSpec((units, total_rows), lambda g: (0, 0)),
            pl.BlockSpec((2, units, WIDE), lambda g: (0, 0, first + g)),
            pl.BlockSpec(keep.shape, lambda g: (0, 0)),
            pl.BlockSpec((1, WIDE), lambda g: (0, first + g)),
            pl.BlockSpec((units, total_rows), lambda g: (0, 0)),
        ],
        out_specs=[
            pl.BlockSpec((4, 2, 8, WIDE), lambda g: (0, 0, 0, g)),
            pl.BlockSpec((4, 2, 8, WIDE), lambda g: (0, 0, 0, g)),
            pl.BlockSpec((units, total_rows), lambda g: (0, 0)),
        ],
        out_shape=[
            jax.ShapeDtypeStruct((4, 2, 8, count * WIDE), F32),
            jax.ShapeDtypeStruct((4, 2, 8, count * WIDE), F32),
            jax.ShapeDtypeStruct((units, total_rows), F32),
        ],
        compiler_params=params(),
        cost_estimate=pl.CostEstimate(
            flops=count * 2 * 2 * 2 * 64 * 128 * WIDE, bytes_accessed=count * 4 * 2**20, transcendentals=0
        ),
        name=f"tail_{first}",
    )(g1, g2, hidden_order, w, keep, taper, before)


def terms_of(values, count):
    out = []
    for _ in range(count):
        term = values.astype(BF16)
        out.append(term)
        values = values - term.astype(F32)
    return out


def scatter_kernel(own_ref, one_ref, two_ref, three_ref, early_ref, w_in_ref, w_in_t_ref,
                   grad_in_ref, grad_uvw_ref, grad_base_ref):
    units = w_in_ref.shape[0]
    spread, near = early_ref.shape[:2]
    members = spread * near
    apart = [lax.axis_index("bl") ^ m for m in range(members)]
    spots = [(a // near, a % near) for a in apart]
    inputs = jnp.concatenate([early_ref[f, n, :units] for f, n in spots], axis=1).astype(BF16)
    blocks = []
    for far, n in spots:
        block = own_ref[n]
        for k, ref in ((1, one_ref), (2, two_ref), (3, three_ref)):
            block = jnp.where(far == k, ref[n], block)
        blocks.append(block)
    hidden_grad = jnp.concatenate(blocks, axis=1)
    pre_act = dot(w_in_t_ref[...], inputs)
    sigmoid = 1.0 / (1.0 + jnp.exp(-pre_act))
    pre_grad = hidden_grad * sigmoid * (1.0 + pre_act * (1.0 - sigmoid))
    grad_terms = jnp.concatenate(terms_of(pre_grad, 2), axis=0)
    parts = dot(inputs, grad_terms, NT)
    grad_in_ref[...] = parts[:, :units] + parts[:, units:]
    input_grad = dot(w_in_ref[...], grad_terms[:units]) + dot(w_in_ref[...], grad_terms[units:])
    terms = jnp.concatenate(terms_of(input_grad, 2), axis=0)
    for which, out_ref in ((0, grad_uvw_ref), (1, grad_base_ref)):
        row = units + which
        index = jnp.concatenate([early_ref[f, n, row : row + 1] for f, n in spots], axis=1)
        index = index.astype(jnp.int32)
        cells = out_ref.shape[1]
        for start in range(0, cells, 512):
            size = min(512, cells - start)
            sums = dot(one_hot_rows(index - start, size), terms, NT).T
            out_ref[:, start : start + size] = sums[:units] + sums[units:]


def scatter(blocks, early, w_in, cells, baselines):
    return pl.pallas_call(
        scatter_kernel,
        out_shape=[
            jax.ShapeDtypeStruct(w_in.shape, F32),
            jax.ShapeDtypeStruct((w_in.shape[0], cells), F32),
            jax.ShapeDtypeStruct((w_in.shape[0], baselines), F32),
        ],
        compiler_params=params(),
        cost_estimate=pl.CostEstimate(
            flops=6 * 10**9, bytes_accessed=4 * 2**20, transcendentals=0
        ),
        name="scatter",
    )(*blocks, early, w_in, w_in.T)


def swap(values, axis, distance):
    size = lax.axis_size(axis)
    return lax.ppermute(values, axis, [(i, i ^ distance) for i in range(size)])


def met(values, axis, distances):
    return [values, *[swap(values, axis, distance) for distance in distances]]


def sum_over_ch(values):
    a, b, c, d = met(values, "ch", (2, 4, 6))
    total = (a + b) + (c + d)
    return total + swap(total, "ch", 1)


def sum_cores(mine, other):
    return mine + swap(other, "bl", 1)


def sum_far(both):
    ring = lambda d: [(i, (i + 4 * d) % 16) for i in range(16)]
    got = [lax.ppermute(both[d], "bl", ring(d)) for d in (1, 2, 3)]
    return both[0] + got[0] + got[1] + got[2]


def sum_near(total):
    return total[:, :4] + swap(total[:, 4:], "bl", 2)


def together(*values):
    return lax.optimization_barrier(values)


def after(value, *others):
    return lax.optimization_barrier((value, *others))[0]


def body(
    uvw_index, row_baseline, flags, uvw_table, baseline_features, w_in, w_out, observed, delay_weight
):
    members = lax.axis_size("ch")
    rows = uvw_index.shape[0]
    local_blocks = flags.shape[1]
    local_channels = w_out.shape[2]
    half_rows = rows // 2
    per = half_rows // members

    taper = jnp.asarray(taper_table()).reshape(members, local_channels)
    inputs, hidden, hidden_t, keep, taper = trunk(
        uvw_index, row_baseline, flags, uvw_table, baseline_features, w_in, taper
    )
    constants = [jnp.asarray(table) for table in tables()]
    weight = delay_weight.reshape(BLOCK, NBLOCKS).T

    def exchange(values):
        size = values.shape[-2]
        return lax.all_to_all(
            values.reshape(members, per, PLANES, size, LANES), "ch", 0, 0, tiled=True
        )

    part = residual_part(0, 2, hidden_t, w_out, observed, keep, taper)
    hidden_t = after(hidden_t, part)
    sent = [exchange(part), exchange(residual_part(1, 2, hidden_t, w_out, observed, keep, taper))]

    index_rows = jnp.stack([uvw_index, row_baseline]).astype(F32)
    early = jnp.concatenate([inputs, index_rows, jnp.zeros((6, rows), F32)], axis=0)[None]
    early = jnp.concatenate(met(early, "bl", (4, 8, 12)), axis=0)
    early = jnp.stack(met(early, "bl", (1, 2, 3)), axis=1)
    me = lax.axis_index("bl")
    order = lax.broadcasted_iota(jnp.int32, hidden.shape[:1], 0)
    core, x_far, y_far, unit = order // 32, (order // 8) % 4, (order // 4) % 2, order % 4
    owner = ((me // 4 + x_far) % 4) * 4 + ((me // 2) % 2 ^ y_far) * 2 + (me % 2 ^ core)
    units = lax.broadcasted_iota(jnp.int32, (hidden.shape[0],) * 2, 1)
    turn = (units == (owner * 4 + unit)[:, None]).astype(BF16)
    hidden_order = dot(turn, hidden).astype(BF16)
    w = w_out.transpose(1, 0, 2)

    (part,) = delay_filter((local_blocks,), sent[0], constants, weight)
    back_0 = exchange(part).reshape(half_rows, PLANES, local_blocks, LANES)
    sizes = (local_blocks // 2, local_blocks // 2)
    counts = [size // STEP for size in sizes]
    parts = delay_filter(sizes, after(sent[1], part), constants, weight)

    def arrive(part):
        return exchange(part).reshape(half_rows, PLANES, part.shape[-2], LANES)

    piece = arrive(after(parts[0], back_0, hidden_order, w, early))
    late = after(parts[1], piece)
    mine, other, hidden_grad = tail_part(
        0, counts[0], back_0, piece, hidden_order, w, keep, taper, jnp.zeros(hidden.shape, F32)
    )
    first = sum_far(sum_cores(mine, other))
    piece = after(arrive(late), first)
    mine, other, hidden_grad = tail_part(
        counts[0], counts[1], back_0, piece, hidden_order, w, keep, taper, hidden_grad
    )
    both = sum_cores(mine, other)
    hidden_grad, both = together(sum_over_ch(hidden_grad), both)
    second = sum_far(both)
    near = jnp.stack(met(hidden_grad, "bl", (1, 2, 3)))
    near, first, second = together(near, first, second)
    blocks = met(near, "bl", (4, 8, 12))
    total = jnp.concatenate([first, second], axis=2)
    grad_out = sum_near(total).transpose(1, 0, 2)
    grad_in, grad_uvw, grad_base = scatter(
        blocks, early, w_in, uvw_table.shape[1], baseline_features.shape[1]
    )
    return (grad_out, grad_in, grad_uvw, grad_base)


def solution(mesh):
    return jax.shard_map(
        body,
        mesh=mesh,
        in_specs=(
            P("bl"),
            P("bl"),
            P("bl", "ch"),
            P(),
            P(),
            P(),
            P(None, None, "ch"),
            P(None, "ch", "bl"),
            P(),
        ),
        out_specs=(P("bl", None, "ch"), P(), P(), P()),
        check_vma=False,
    )
```

```python
import functools
import math

import jax
import jax.numpy as jnp
import ml_dtypes
import numpy as np
from jax import lax
from jax.experimental import pallas as pl
from jax.experimental.pallas import tpu as pltpu
from jax.sharding import PartitionSpec as P

BLOCK = 256
NBLOCKS = 256
CHANNELS = 65536
LOSS_SCALE = 0.0625
HIGHEST = lax.Precision.HIGHEST
F32 = jnp.float32
BF16 = jnp.bfloat16
STEP = 8
WIDE = STEP * BLOCK
LANES = 128
PLANES = 4
VMEM = 56 * 2**20


def split_matrix(matrix):
    high = matrix.astype(ml_dtypes.bfloat16)
    low = (matrix - high.astype(np.float64)).astype(ml_dtypes.bfloat16)
    return high, low


def tables():
    n = np.arange(BLOCK)
    product = np.outer(n, n)
    cosine = np.cos(2 * math.pi * (product % BLOCK) / BLOCK)
    sine = np.sin(2 * math.pi * (product % BLOCK) / BLOCK)
    forward = np.block([[cosine, sine], [-sine, cosine]])
    backward = np.block([[cosine, -sine], [sine, cosine]])
    twiddle = 2 * math.pi * product / CHANNELS
    return (
        *split_matrix(forward),
        *split_matrix(backward),
        np.cos(twiddle).astype(np.float32),
        np.sin(twiddle).astype(np.float32),
    )


def taper_table():
    c = np.arange(CHANNELS)
    window = np.full((CHANNELS,), 0.35875)
    for harmonic, term in ((1, -0.48829), (2, 0.14128), (3, -0.01168)):
        window = window + term * np.cos(2 * math.pi * ((c * harmonic) % CHANNELS) / CHANNELS)
    return window.astype(np.float32)


def dot(a, b, dims=(((1,), (0,)), ((), ())), precision=None):
    return lax.dot_general(a, b, dims, precision=precision, preferred_element_type=F32)


NT = (((1,), (1,)), ((), ()))
TN = (((0,), (0,)), ((), ()))


def params(**more):
    return pltpu.CompilerParams(vmem_limit_bytes=VMEM, **more)


def one_hot_rows(index_row, count):
    cells = lax.broadcasted_iota(jnp.int32, (count, index_row.shape[1]), 0)
    return jnp.where(cells == index_row, 1.0, 0.0).astype(BF16)


def trunk_kernel(uvw_ref, base_ref, flags_ref, table_ref, features_ref, w_in_ref, taper_ref,
                 inputs_ref, hidden_ref, hidden_t_ref, keep_ref, taper_here_ref):
    taper_here_ref[...] = taper_ref[pl.ds(lax.axis_index("ch"), 1), :]
    summed = dot(table_ref[...], one_hot_rows(uvw_ref[...], table_ref.shape[1]))
    summed = summed + dot(features_ref[...], one_hot_rows(base_ref[...], features_ref.shape[1]))
    inputs = summed.astype(BF16)
    inputs_ref[...] = inputs.astype(F32)
    pre_act = dot(w_in_ref[...], inputs, TN)
    hidden = pre_act / (1.0 + jnp.exp(-pre_act))
    hidden_ref[...] = hidden.astype(BF16)
    hidden_t_ref[...] = hidden.T.astype(BF16)
    keep_ref[...] = (1.0 - flags_ref[...].astype(F32)).T.astype(BF16)


def trunk(uvw_index, row_baseline, flags, uvw_table, baseline_features, w_in, taper):
    rows = uvw_index.shape[0]
    units = w_in.shape[1]
    return pl.pallas_call(
        trunk_kernel,
        out_shape=(
            jax.ShapeDtypeStruct((w_in.shape[0], rows), F32),
            jax.ShapeDtypeStruct((units, rows), BF16),
            jax.ShapeDtypeStruct((rows, units), BF16),
            jax.ShapeDtypeStruct(flags.shape, BF16),
            jax.ShapeDtypeStruct((1, taper.shape[1]), F32),
        ),
        compiler_params=params(),
        name="trunk",
    )(uvw_index[None], row_baseline[None], flags.T, uvw_table, baseline_features, w_in, taper)


def weight_of(keep, taper_row, first_block):
    blocks = keep.shape[1]
    block = lax.broadcasted_iota(jnp.int32, (blocks, WIDE), 0)
    lane = lax.broadcasted_iota(jnp.int32, (blocks, WIDE), 1)
    expand = jnp.where(block == first_block + (lane >> 8), 1.0, 0.0).astype(BF16)
    return dot(keep, expand) * taper_row


def residual_kernel(half, hidden_ref, w_ref, observed_ref, keep_ref, taper_ref, out_ref):
    rows = hidden_ref.shape[0]
    total = observed_ref.shape[2]
    weight = weight_of(keep_ref[...], taper_ref[...], pl.program_id(0) * STEP)
    row = lax.broadcasted_iota(jnp.int32, (rows, total), 0)
    column = lax.broadcasted_iota(jnp.int32, (rows, total), 1)
    pick = jnp.where(column == row + half * rows, -1.0, 0.0).astype(BF16)
    flat = out_ref.reshape(rows * PLANES * STEP, LANES)
    units = w_ref.shape[0]
    pairs = w_ref[...].reshape(2 * units, WIDE)
    unit = lax.broadcasted_iota(jnp.int32, (units, 2 * units), 0)
    place = lax.broadcasted_iota(jnp.int32, (units, 2 * units), 1)
    for q in range(2):
        spread = jnp.where(place == unit * 2 + q, 1.0, 0.0).astype(BF16)
        own = dot(hidden_ref[...], spread).astype(BF16)
        residual = dot(own, pairs) + dot(pick, observed_ref[q], NT)
        residual = residual * weight
        for b in range(STEP):
            for side in range(2):
                start = b * BLOCK + side * LANES
                flat[pl.ds((q * 2 + side) * STEP + b, rows, stride=PLANES * STEP), :] = residual[
                    :, start : start + LANES
                ]


def residual_part(half, halves, hidden_t, w, observed, keep, taper):
    rows = hidden_t.shape[0] // halves
    blocks = keep.shape[1]
    return pl.pallas_call(
        functools.partial(residual_kernel, half),
        grid=(blocks // STEP,),
        in_specs=[
            pl.BlockSpec((rows, hidden_t.shape[1]), lambda g: (half, 0)),
            pl.BlockSpec((w.shape[0], 2, WIDE), lambda g: (0, 0, g)),
            pl.BlockSpec((2, WIDE, observed.shape[2]), lambda g: (0, g, 0)),
            pl.BlockSpec((rows, blocks), lambda g: (half, 0)),
            pl.BlockSpec((1, WIDE), lambda g: (0, g)),
        ],
        out_specs=pl.BlockSpec((rows, PLANES, STEP, LANES), lambda g: (0, 0, g, 0)),
        out_shape=jax.ShapeDtypeStruct((rows, PLANES, blocks, LANES), F32),
        compiler_params=params(),
        cost_estimate=pl.CostEstimate(
            flops=2 * rows * 2 * blocks * BLOCK * 192, bytes_accessed=10 * 2**20, transcendentals=0
        ),
        name=f"residual_{half}",
    )(hidden_t, w, observed, keep, taper)


def halves_of(values):
    high = values.astype(BF16)
    return high, (values - high.astype(F32)).astype(BF16)


def dot_three(a, b):
    return dot(a[0], b[0]) + (dot(a[0], b[1]) + dot(a[1], b[0]))


def delay_kernel(pieces, x_ref, fh_ref, fl_ref, bh_ref, bl_ref, cos_ref, sin_ref, weight_ref, *outs):
    forward = (fh_ref[...], fl_ref[...])
    backward = (bh_ref[...], bl_ref[...])
    cosine, sine = cos_ref[...], sin_ref[...]
    count = x_ref.shape[1]
    members, local = x_ref.shape[0], x_ref.shape[3]
    turned = []
    for i in range(count):
        values = jnp.concatenate(
            [
                jnp.concatenate(
                    [x_ref[:, i, q * 2 + side].reshape(NBLOCKS, LANES) for side in range(2)], axis=1
                )
                for q in range(2)
            ],
            axis=0,
        )
        first = dot_three(forward, halves_of(values))
        real, imag = first[:NBLOCKS], first[NBLOCKS:]
        turned.append(
            jnp.concatenate([real * cosine + imag * sine, imag * cosine - real * sine], axis=1)
        )
    second = dot_three(halves_of(jnp.concatenate(turned, axis=0)), backward)
    factor = weight_ref[...] * (LOSS_SCALE / CHANNELS)
    factor = jnp.concatenate([jnp.concatenate([factor, factor], axis=1)] * count, axis=0)
    third = dot_three(halves_of(second * factor), forward)
    for i in range(count):
        part = third[i * NBLOCKS : (i + 1) * NBLOCKS]
        real, imag = part[:, :BLOCK], part[:, BLOCK:]
        back = jnp.concatenate([real * cosine - imag * sine, imag * cosine + real * sine], axis=0)
        fourth = dot_three(backward, halves_of(back))
        for q in range(2):
            for member in range(members):
                start = q * NBLOCKS + member * local
                for out_ref, size in zip(outs, pieces):
                    for side in range(2):
                        out_ref[member, i, q * 2 + side] = fourth[
                            start : start + size, side * LANES : (side + 1) * LANES
                        ]
                    start += size


def delay_filter(pieces, arrived, constants, weight, count=2):
    members, rows, _, local, _ = arrived.shape
    whole = lambda array: pl.BlockSpec(array.shape, lambda g: (0, 0))
    flops = rows * 4 * 3 * 2 * 512 * 512 * 256
    return pl.pallas_call(
        functools.partial(delay_kernel, pieces),
        grid=(rows // count,),
        in_specs=[
            pl.BlockSpec((members, count, PLANES, local, LANES), lambda g: (0, g, 0, 0, 0)),
            *[whole(array) for array in constants],
            whole(weight),
        ],
        out_specs=[
            pl.BlockSpec((members, count, PLANES, size, LANES), lambda g: (0, g, 0, 0, 0))
            for size in pieces
        ],
        out_shape=[
            jax.ShapeDtypeStruct((members, rows, PLANES, size, LANES), F32) for size in pieces
        ],
        compiler_params=params(),
        cost_estimate=pl.CostEstimate(flops=flops, bytes_accessed=12 * 2**20, transcendentals=0),
        name=f"delay_{len(pieces)}",
    )(arrived, *constants, weight)


def tail_kernel(first, g1_ref, g2_ref, hidden_ref, w_ref, keep_ref, taper_ref, before_ref,
                mine_ref, other_ref, hidden_grad_ref):
    step = pl.program_id(0)
    weight = weight_of(keep_ref[...], taper_ref[...], (first + step) * STEP)
    rows = g1_ref.shape[0]
    flats = [ref.reshape(rows * PLANES * STEP, LANES) for ref in (g1_ref, g2_ref)]

    @pl.when(step == 0)
    def _():
        hidden_grad_ref[...] = before_ref[...]

    total = hidden_grad_ref[...]
    for q in range(2):
        values = jnp.concatenate(
            [
                jnp.concatenate(
                    [
                        flat[pl.ds((q * 2 + side) * STEP + b, rows, stride=PLANES * STEP), :]
                        for b in range(STEP)
                        for side in range(2)
                    ],
                    axis=1,
                )
                for flat in flats
            ],
            axis=0,
        )
        grad_field = (values * weight).astype(BF16)
        grad_out = dot(hidden_ref[...], grad_field)
        units = grad_out.shape[0] // 2
        for d in range(4):
            mine_ref[d, q] = grad_out[d * 8 : (d + 1) * 8]
            other_ref[d, q] = grad_out[units + d * 8 : units + (d + 1) * 8]
        total = total + dot(w_ref[q], grad_field, NT)
    hidden_grad_ref[...] = total


def tail_part(first, count, g1, g2, hidden_order, w, keep, taper, before):
    rows = g1.shape[0]
    units, total_rows = hidden_order.shape
    return pl.pallas_call(
        functools.partial(tail_kernel, first),
        grid=(count,),
        in_specs=[
            pl.BlockSpec((rows, PLANES, STEP, LANES), lambda g: (0, 0, first + g, 0)),
            pl.BlockSpec((rows, PLANES, STEP, LANES), lambda g: (0, 0, g, 0)),
            pl.BlockSpec((units, total_rows), lambda g: (0, 0)),
            pl.BlockSpec((2, units, WIDE), lambda g: (0, 0, first + g)),
            pl.BlockSpec(keep.shape, lambda g: (0, 0)),
            pl.BlockSpec((1, WIDE), lambda g: (0, first + g)),
            pl.BlockSpec((units, total_rows), lambda g: (0, 0)),
        ],
        out_specs=[
            pl.BlockSpec((4, 2, 8, WIDE), lambda g: (0, 0, 0, g)),
            pl.BlockSpec((4, 2, 8, WIDE), lambda g: (0, 0, 0, g)),
            pl.BlockSpec((units, total_rows), lambda g: (0, 0)),
        ],
        out_shape=[
            jax.ShapeDtypeStruct((4, 2, 8, count * WIDE), F32),
            jax.ShapeDtypeStruct((4, 2, 8, count * WIDE), F32),
            jax.ShapeDtypeStruct((units, total_rows), F32),
        ],
        compiler_params=params(),
        cost_estimate=pl.CostEstimate(
            flops=count * 2 * 2 * 2 * 64 * 128 * WIDE, bytes_accessed=count * 4 * 2**20, transcendentals=0
        ),
        name=f"tail_{first}",
    )(g1, g2, hidden_order, w, keep, taper, before)


def terms_of(values, count):
    out = []
    for _ in range(count):
        term = values.astype(BF16)
        out.append(term)
        values = values - term.astype(F32)
    return out


def scatter_kernel(own_ref, one_ref, two_ref, three_ref, early_ref, w_in_ref, w_in_t_ref,
                   grad_in_ref, grad_uvw_ref, grad_base_ref):
    units = w_in_ref.shape[0]
    spread, near = early_ref.shape[:2]
    members = spread * near
    apart = [lax.axis_index("bl") ^ m for m in range(members)]
    spots = [(a // near, a % near) for a in apart]
    inputs = jnp.concatenate([early_ref[f, n, :units] for f, n in spots], axis=1).astype(BF16)
    blocks = []
    for far, n in spots:
        block = own_ref[far]
        for k, ref in ((1, one_ref), (2, two_ref), (3, three_ref)):
            block = jnp.where(n == k, ref[far], block)
        blocks.append(block)
    hidden_grad = jnp.concatenate(blocks, axis=1)
    pre_act = dot(w_in_t_ref[...], inputs)
    sigmoid = 1.0 / (1.0 + jnp.exp(-pre_act))
    pre_grad = hidden_grad * sigmoid * (1.0 + pre_act * (1.0 - sigmoid))
    grad_terms = jnp.concatenate(terms_of(pre_grad, 2), axis=0)
    parts = dot(inputs, grad_terms, NT)
    grad_in_ref[...] = parts[:, :units] + parts[:, units:]
    input_grad = dot(w_in_ref[...], grad_terms[:units]) + dot(w_in_ref[...], grad_terms[units:])
    terms = jnp.concatenate(terms_of(input_grad, 2), axis=0)
    for which, out_ref in ((0, grad_uvw_ref), (1, grad_base_ref)):
        row = units + which
        index = jnp.concatenate([early_ref[f, n, row : row + 1] for f, n in spots], axis=1)
        index = index.astype(jnp.int32)
        cells = out_ref.shape[1]
        for start in range(0, cells, 512):
            size = min(512, cells - start)
            sums = dot(one_hot_rows(index - start, size), terms, NT).T
            out_ref[:, start : start + size] = sums[:units] + sums[units:]


def scatter(blocks, early, w_in, cells, baselines):
    return pl.pallas_call(
        scatter_kernel,
        out_shape=[
            jax.ShapeDtypeStruct(w_in.shape, F32),
            jax.ShapeDtypeStruct((w_in.shape[0], cells), F32),
            jax.ShapeDtypeStruct((w_in.shape[0], baselines), F32),
        ],
        compiler_params=params(),
        cost_estimate=pl.CostEstimate(
            flops=6 * 10**9, bytes_accessed=4 * 2**20, transcendentals=0
        ),
        name="scatter",
    )(*blocks, early, w_in, w_in.T)


def swap(values, axis, distance):
    size = lax.axis_size(axis)
    return lax.ppermute(values, axis, [(i, i ^ distance) for i in range(size)])


def met(values, axis, distances):
    return [values, *[swap(values, axis, distance) for distance in distances]]


def sum_over_ch(values):
    a, b, c, d = met(values, "ch", (2, 4, 6))
    total = (a + b) + (c + d)
    return total + swap(total, "ch", 1)


def sum_cores(mine, other):
    return mine + swap(other, "bl", 1)


def sum_far(both):
    ring = lambda d: [(i, (i + 4 * d) % 16) for i in range(16)]
    got = [lax.ppermute(both[d], "bl", ring(d)) for d in (1, 2, 3)]
    return both[0] + got[0] + got[1] + got[2]


def sum_near(total):
    return total[:, :4] + swap(total[:, 4:], "bl", 2)


def together(*values):
    return lax.optimization_barrier(values)


def after(value, *others):
    return lax.optimization_barrier((value, *others))[0]


def body(
    uvw_index, row_baseline, flags, uvw_table, baseline_features, w_in, w_out, observed, delay_weight
):
    members = lax.axis_size("ch")
    rows = uvw_index.shape[0]
    local_blocks = flags.shape[1]
    local_channels = w_out.shape[2]
    half_rows = rows // 2
    per = half_rows // members

    taper = jnp.asarray(taper_table()).reshape(members, local_channels)
    inputs, hidden, hidden_t, keep, taper = trunk(
        uvw_index, row_baseline, flags, uvw_table, baseline_features, w_in, taper
    )
    constants = [jnp.asarray(table) for table in tables()]
    weight = delay_weight.reshape(BLOCK, NBLOCKS).T

    def exchange(values):
        size = values.shape[-2]
        return lax.all_to_all(
            values.reshape(members, per, PLANES, size, LANES), "ch", 0, 0, tiled=True
        )

    part = residual_part(0, 2, hidden_t, w_out, observed, keep, taper)
    hidden_t = after(hidden_t, part)
    sent = [exchange(part), exchange(residual_part(1, 2, hidden_t, w_out, observed, keep, taper))]

    me = lax.axis_index("bl")
    order = lax.broadcasted_iota(jnp.int32, hidden.shape[:1], 0)
    core, x_far, y_far, unit = order // 32, (order // 8) % 4, (order // 4) % 2, order % 4
    owner = ((me // 4 + x_far) % 4) * 4 + ((me // 2) % 2 ^ y_far) * 2 + (me % 2 ^ core)
    units = lax.broadcasted_iota(jnp.int32, (hidden.shape[0],) * 2, 1)
    turn = (units == (owner * 4 + unit)[:, None]).astype(BF16)
    hidden_order = dot(turn, hidden).astype(BF16)
    w = w_out.transpose(1, 0, 2)

    (part,) = delay_filter((local_blocks,), sent[0], constants, weight)
    back_0 = exchange(part).reshape(half_rows, PLANES, local_blocks, LANES)
    sizes = (local_blocks // 2, local_blocks // 2)
    counts = [size // STEP for size in sizes]
    parts = delay_filter(sizes, after(sent[1], part), constants, weight)

    def arrive(part):
        return exchange(part).reshape(half_rows, PLANES, part.shape[-2], LANES)

    index_rows = jnp.stack([uvw_index, row_baseline]).astype(F32)
    early = jnp.concatenate([inputs, index_rows, jnp.zeros((6, rows), F32)], axis=0)[None]
    early = after(early, parts[0])
    early = jnp.concatenate(met(early, "bl", (4, 8, 12)), axis=0)
    early = jnp.stack(met(early, "bl", (1, 2, 3)), axis=1)

    piece = arrive(after(parts[0], back_0, hidden_order, w))
    late = after(parts[1], piece)
    piece = after(piece, early)
    mine, other, hidden_grad = tail_part(
        0, counts[0], back_0, piece, hidden_order, w, keep, taper, jnp.zeros(hidden.shape, F32)
    )
    first = sum_far(sum_cores(mine, other))
    piece = after(arrive(late), first)
    mine, other, hidden_grad = tail_part(
        counts[0], counts[1], back_0, piece, hidden_order, w, keep, taper, hidden_grad
    )
    hidden_grad, both = together(sum_over_ch(hidden_grad), sum_cores(mine, other))
    far = jnp.stack(met(hidden_grad, "bl", (4, 8, 12)))
    second = sum_far(after(both, far))
    blocks = met(far, "bl", (1, 2, 3))
    blocks[0] = after(blocks[0], second)
    grad_out = sum_near(jnp.concatenate([first, second], axis=2)).transpose(1, 0, 2)
    grad_in, grad_uvw, grad_base = scatter(
        blocks, early, w_in, uvw_table.shape[1], baseline_features.shape[1]
    )
    return (grad_out, grad_in, grad_uvw, grad_base)


def solution(mesh):
    return jax.shard_map(
        body,
        mesh=mesh,
        in_specs=(
            P("bl"),
            P("bl"),
            P("bl", "ch"),
            P(),
            P(),
            P(),
            P(None, None, "ch"),
            P(None, "ch", "bl"),
            P(),
        ),
        out_specs=(P("bl", None, "ch"), P(), P(), P()),
        check_vma=False,
    )
```

```python
import functools
import math

import jax
import jax.numpy as jnp
import ml_dtypes
import numpy as np
from jax import lax
from jax.experimental import pallas as pl
from jax.experimental.pallas import tpu as pltpu
from jax.sharding import PartitionSpec as P

BLOCK = 256
NBLOCKS = 256
CHANNELS = 65536
LOSS_SCALE = 0.0625
HIGHEST = lax.Precision.HIGHEST
F32 = jnp.float32
BF16 = jnp.bfloat16
STEP = 8
WIDE = STEP * BLOCK
LANES = 128
PLANES = 4
VMEM = 56 * 2**20


def split_matrix(matrix):
    high = matrix.astype(ml_dtypes.bfloat16)
    low = (matrix - high.astype(np.float64)).astype(ml_dtypes.bfloat16)
    return high, low


def tables():
    n = np.arange(BLOCK)
    product = np.outer(n, n)
    cosine = np.cos(2 * math.pi * (product % BLOCK) / BLOCK)
    sine = np.sin(2 * math.pi * (product % BLOCK) / BLOCK)
    forward = np.block([[cosine, sine], [-sine, cosine]])
    backward = np.block([[cosine, -sine], [sine, cosine]])
    twiddle = 2 * math.pi * product / CHANNELS
    return (
        *split_matrix(forward),
        *split_matrix(backward),
        np.cos(twiddle).astype(np.float32),
        np.sin(twiddle).astype(np.float32),
    )


def taper_table():
    c = np.arange(CHANNELS)
    window = np.full((CHANNELS,), 0.35875)
    for harmonic, term in ((1, -0.48829), (2, 0.14128), (3, -0.01168)):
        window = window + term * np.cos(2 * math.pi * ((c * harmonic) % CHANNELS) / CHANNELS)
    return window.astype(np.float32)


def dot(a, b, dims=(((1,), (0,)), ((), ())), precision=None):
    return lax.dot_general(a, b, dims, precision=precision, preferred_element_type=F32)


NT = (((1,), (1,)), ((), ()))
TN = (((0,), (0,)), ((), ()))


def params(**more):
    return pltpu.CompilerParams(vmem_limit_bytes=VMEM, **more)


def one_hot_rows(index_row, count):
    cells = lax.broadcasted_iota(jnp.int32, (count, index_row.shape[1]), 0)
    return jnp.where(cells == index_row, 1.0, 0.0).astype(BF16)


def trunk_kernel(uvw_ref, base_ref, flags_ref, table_ref, features_ref, w_in_ref, taper_ref,
                 hidden_ref, hidden_t_ref, keep_ref, taper_here_ref):
    taper_here_ref[...] = taper_ref[pl.ds(lax.axis_index("ch"), 1), :]
    summed = dot(table_ref[...], one_hot_rows(uvw_ref[...], table_ref.shape[1]))
    summed = summed + dot(features_ref[...], one_hot_rows(base_ref[...], features_ref.shape[1]))
    inputs = summed.astype(BF16)
    pre_act = dot(w_in_ref[...], inputs, TN)
    hidden = pre_act / (1.0 + jnp.exp(-pre_act))
    hidden_ref[...] = hidden.astype(BF16)
    hidden_t_ref[...] = hidden.T.astype(BF16)
    keep_ref[...] = (1.0 - flags_ref[...].astype(F32)).T.astype(BF16)


def trunk(uvw_index, row_baseline, flags, uvw_table, baseline_features, w_in, taper):
    rows = uvw_index.shape[0]
    units = w_in.shape[1]
    return pl.pallas_call(
        trunk_kernel,
        out_shape=(
            jax.ShapeDtypeStruct((units, rows), BF16),
            jax.ShapeDtypeStruct((rows, units), BF16),
            jax.ShapeDtypeStruct(flags.shape, BF16),
            jax.ShapeDtypeStruct((1, taper.shape[1]), F32),
        ),
        compiler_params=params(),
        name="trunk",
    )(uvw_index[None], row_baseline[None], flags.T, uvw_table, baseline_features, w_in, taper)


def weight_of(keep, taper_row, first_block):
    blocks = keep.shape[1]
    block = lax.broadcasted_iota(jnp.int32, (blocks, WIDE), 0)
    lane = lax.broadcasted_iota(jnp.int32, (blocks, WIDE), 1)
    expand = jnp.where(block == first_block + (lane >> 8), 1.0, 0.0).astype(BF16)
    return dot(keep, expand) * taper_row


def residual_kernel(half, hidden_ref, w_ref, observed_ref, keep_ref, taper_ref, out_ref):
    rows = hidden_ref.shape[0]
    total = observed_ref.shape[2]
    weight = weight_of(keep_ref[...], taper_ref[...], pl.program_id(0) * STEP)
    row = lax.broadcasted_iota(jnp.int32, (rows, total), 0)
    column = lax.broadcasted_iota(jnp.int32, (rows, total), 1)
    pick = jnp.where(column == row + half * rows, -1.0, 0.0).astype(BF16)
    flat = out_ref.reshape(rows * PLANES * STEP, LANES)
    units = w_ref.shape[0]
    pairs = w_ref[...].reshape(2 * units, WIDE)
    unit = lax.broadcasted_iota(jnp.int32, (units, 2 * units), 0)
    place = lax.broadcasted_iota(jnp.int32, (units, 2 * units), 1)
    for q in range(2):
        spread = jnp.where(place == unit * 2 + q, 1.0, 0.0).astype(BF16)
        own = dot(hidden_ref[...], spread).astype(BF16)
        residual = dot(own, pairs) + dot(pick, observed_ref[q], NT)
        residual = residual * weight
        for b in range(STEP):
            for side in range(2):
                start = b * BLOCK + side * LANES
                flat[pl.ds((q * 2 + side) * STEP + b, rows, stride=PLANES * STEP), :] = residual[
                    :, start : start + LANES
                ]


def residual_part(half, halves, hidden_t, w, observed, keep, taper):
    rows = hidden_t.shape[0] // halves
    blocks = keep.shape[1]
    return pl.pallas_call(
        functools.partial(residual_kernel, half),
        grid=(blocks // STEP,),
        in_specs=[
            pl.BlockSpec((rows, hidden_t.shape[1]), lambda g: (half, 0)),
            pl.BlockSpec((w.shape[0], 2, WIDE), lambda g: (0, 0, g)),
            pl.BlockSpec((2, WIDE, observed.shape[2]), lambda g: (0, g, 0)),
            pl.BlockSpec((rows, blocks), lambda g: (half, 0)),
            pl.BlockSpec((1, WIDE), lambda g: (0, g)),
        ],
        out_specs=pl.BlockSpec((rows, PLANES, STEP, LANES), lambda g: (0, 0, g, 0)),
        out_shape=jax.ShapeDtypeStruct((rows, PLANES, blocks, LANES), F32),
        compiler_params=params(),
        cost_estimate=pl.CostEstimate(
            flops=2 * rows * 2 * blocks * BLOCK * 192, bytes_accessed=10 * 2**20, transcendentals=0
        ),
        name=f"residual_{half}",
    )(hidden_t, w, observed, keep, taper)


def halves_of(values):
    high = values.astype(BF16)
    return high, (values - high.astype(F32)).astype(BF16)


def dot_three(a, b):
    return dot(a[0], b[0]) + (dot(a[0], b[1]) + dot(a[1], b[0]))


def delay_kernel(pieces, x_ref, fh_ref, fl_ref, bh_ref, bl_ref, cos_ref, sin_ref, weight_ref, *outs):
    forward = (fh_ref[...], fl_ref[...])
    backward = (bh_ref[...], bl_ref[...])
    cosine, sine = cos_ref[...], sin_ref[...]
    count = x_ref.shape[1]
    members, local = x_ref.shape[0], x_ref.shape[3]
    turned = []
    for i in range(count):
        values = jnp.concatenate(
            [
                jnp.concatenate(
                    [x_ref[:, i, q * 2 + side].reshape(NBLOCKS, LANES) for side in range(2)], axis=1
                )
                for q in range(2)
            ],
            axis=0,
        )
        first = dot_three(forward, halves_of(values))
        real, imag = first[:NBLOCKS], first[NBLOCKS:]
        turned.append(
            jnp.concatenate([real * cosine + imag * sine, imag * cosine - real * sine], axis=1)
        )
    second = dot_three(halves_of(jnp.concatenate(turned, axis=0)), backward)
    factor = weight_ref[...] * (LOSS_SCALE / CHANNELS)
    factor = jnp.concatenate([jnp.concatenate([factor, factor], axis=1)] * count, axis=0)
    third = dot_three(halves_of(second * factor), forward)
    for i in range(count):
        part = third[i * NBLOCKS : (i + 1) * NBLOCKS]
        real, imag = part[:, :BLOCK], part[:, BLOCK:]
        back = jnp.concatenate([real * cosine - imag * sine, imag * cosine + real * sine], axis=0)
        fourth = dot_three(backward, halves_of(back))
        for q in range(2):
            for member in range(members):
                start = q * NBLOCKS + member * local
                for out_ref, size in zip(outs, pieces):
                    for side in range(2):
                        out_ref[member, i, q * 2 + side] = fourth[
                            start : start + size, side * LANES : (side + 1) * LANES
                        ]
                    start += size


def delay_filter(pieces, arrived, constants, weight, count=2):
    members, rows, _, local, _ = arrived.shape
    whole = lambda array: pl.BlockSpec(array.shape, lambda g: (0, 0))
    flops = rows * 4 * 3 * 2 * 512 * 512 * 256
    return pl.pallas_call(
        functools.partial(delay_kernel, pieces),
        grid=(rows // count,),
        in_specs=[
            pl.BlockSpec((members, count, PLANES, local, LANES), lambda g: (0, g, 0, 0, 0)),
            *[whole(array) for array in constants],
            whole(weight),
        ],
        out_specs=[
            pl.BlockSpec((members, count, PLANES, size, LANES), lambda g: (0, g, 0, 0, 0))
            for size in pieces
        ],
        out_shape=[
            jax.ShapeDtypeStruct((members, rows, PLANES, size, LANES), F32) for size in pieces
        ],
        compiler_params=params(),
        cost_estimate=pl.CostEstimate(flops=flops, bytes_accessed=12 * 2**20, transcendentals=0),
        name=f"delay_{len(pieces)}",
    )(arrived, *constants, weight)


def tail_kernel(first, g1_ref, g2_ref, hidden_ref, w_ref, keep_ref, taper_ref, before_ref,
                mine_ref, other_ref, hidden_grad_ref):
    step = pl.program_id(0)
    weight = weight_of(keep_ref[...], taper_ref[...], (first + step) * STEP)
    rows = g1_ref.shape[0]
    flats = [ref.reshape(rows * PLANES * STEP, LANES) for ref in (g1_ref, g2_ref)]

    @pl.when(step == 0)
    def _():
        hidden_grad_ref[...] = before_ref[...]

    total = hidden_grad_ref[...]
    for q in range(2):
        values = jnp.concatenate(
            [
                jnp.concatenate(
                    [
                        flat[pl.ds((q * 2 + side) * STEP + b, rows, stride=PLANES * STEP), :]
                        for b in range(STEP)
                        for side in range(2)
                    ],
                    axis=1,
                )
                for flat in flats
            ],
            axis=0,
        )
        grad_field = (values * weight).astype(BF16)
        grad_out = dot(hidden_ref[...], grad_field)
        units = grad_out.shape[0] // 2
        for d in range(4):
            mine_ref[d, q] = grad_out[d * 8 : (d + 1) * 8]
            other_ref[d, q] = grad_out[units + d * 8 : units + (d + 1) * 8]
        total = total + dot(w_ref[q], grad_field, NT)
    hidden_grad_ref[...] = total


def tail_part(first, count, g1, g2, hidden_order, w, keep, taper, before):
    rows = g1.shape[0]
    units, total_rows = hidden_order.shape
    return pl.pallas_call(
        functools.partial(tail_kernel, first),
        grid=(count,),
        in_specs=[
            pl.BlockSpec((rows, PLANES, STEP, LANES), lambda g: (0, 0, first + g, 0)),
            pl.BlockSpec((rows, PLANES, STEP, LANES), lambda g: (0, 0, g, 0)),
            pl.BlockSpec((units, total_rows), lambda g: (0, 0)),
            pl.BlockSpec((2, units, WIDE), lambda g: (0, 0, first + g)),
            pl.BlockSpec(keep.shape, lambda g: (0, 0)),
            pl.BlockSpec((1, WIDE), lambda g: (0, first + g)),
            pl.BlockSpec((units, total_rows), lambda g: (0, 0)),
        ],
        out_specs=[
            pl.BlockSpec((4, 2, 8, WIDE), lambda g: (0, 0, 0, g)),
            pl.BlockSpec((4, 2, 8, WIDE), lambda g: (0, 0, 0, g)),
            pl.BlockSpec((units, total_rows), lambda g: (0, 0)),
        ],
        out_shape=[
            jax.ShapeDtypeStruct((4, 2, 8, count * WIDE), F32),
            jax.ShapeDtypeStruct((4, 2, 8, count * WIDE), F32),
            jax.ShapeDtypeStruct((units, total_rows), F32),
        ],
        compiler_params=params(),
        cost_estimate=pl.CostEstimate(
            flops=count * 2 * 2 * 2 * 64 * 128 * WIDE, bytes_accessed=count * 4 * 2**20, transcendentals=0
        ),
        name=f"tail_{first}",
    )(g1, g2, hidden_order, w, keep, taper, before)


def terms_of(values, count):
    out = []
    for _ in range(count):
        term = values.astype(BF16)
        out.append(term)
        values = values - term.astype(F32)
    return out


def member_blocks(count):
    apart = [lax.axis_index("bl") ^ m for m in range(count)]
    return [(a // 4, a % 4) for a in apart]


def rows_kernel(index_ref, table_ref, features_ref, w_in_ref, inputs_ref, slope_ref, cells_ref):
    spots = member_blocks(index_ref.shape[0] * index_ref.shape[1])
    cells = jnp.concatenate([index_ref[f, n] for f, n in spots], axis=1).astype(jnp.int32)
    cells_ref[...] = cells
    summed = []
    for which, ref in ((0, table_ref), (1, features_ref)):
        total = 0.0
        for start in range(0, ref.shape[1], 512):
            size = min(512, ref.shape[1] - start)
            picked = one_hot_rows(cells[which : which + 1] - start, size)
            total = total + dot(ref[:, start : start + size], picked)
        summed.append(total)
    inputs = (summed[0] + summed[1]).astype(BF16)
    inputs_ref[...] = inputs
    pre_act = dot(w_in_ref[...], inputs, TN)
    sigmoid = 1.0 / (1.0 + jnp.exp(-pre_act))
    slope_ref[...] = sigmoid * (1.0 + pre_act * (1.0 - sigmoid))


def all_rows(index, uvw_table, baseline_features, w_in):
    rows = index.shape[0] * index.shape[1] * index.shape[3]
    return pl.pallas_call(
        rows_kernel,
        out_shape=[
            jax.ShapeDtypeStruct((w_in.shape[0], rows), BF16),
            jax.ShapeDtypeStruct((w_in.shape[1], rows), F32),
            jax.ShapeDtypeStruct((index.shape[2], rows), jnp.int32),
        ],
        compiler_params=params(),
        cost_estimate=pl.CostEstimate(flops=6 * 10**9, bytes_accessed=2**20, transcendentals=0),
        name="all_rows",
    )(index, uvw_table, baseline_features, w_in)


def scatter_kernel(own_ref, one_ref, two_ref, three_ref, inputs_ref, slope_ref, cells_ref, w_in_ref,
                   grad_in_ref, grad_uvw_ref, grad_base_ref):
    units = w_in_ref.shape[0]
    blocks = []
    for far, n in member_blocks(16):
        block = own_ref[n]
        for k, ref in ((1, one_ref), (2, two_ref), (3, three_ref)):
            block = jnp.where(far == k, ref[n], block)
        blocks.append(block)
    pre_grad = jnp.concatenate(blocks, axis=1) * slope_ref[...]
    grad_terms = jnp.concatenate(terms_of(pre_grad, 2), axis=0)
    parts = dot(inputs_ref[...], grad_terms, NT)
    grad_in_ref[...] = parts[:, :units] + parts[:, units:]
    input_grad = dot(w_in_ref[...], grad_terms[:units]) + dot(w_in_ref[...], grad_terms[units:])
    terms = jnp.concatenate(terms_of(input_grad, 2), axis=0)
    for which, out_ref in ((0, grad_uvw_ref), (1, grad_base_ref)):
        index = cells_ref[which : which + 1, :]
        cells = out_ref.shape[1]
        half = -(-cells // 2 // LANES) * LANES
        upper = index >= half
        index = jnp.where(upper, index - half, index)
        zero = jnp.zeros_like(terms)
        sides = jnp.concatenate(
            [jnp.where(upper, zero, terms), jnp.where(upper, terms, zero)], axis=0
        )
        for start in range(0, half, 512):
            size = min(512, half - start)
            sums = dot(one_hot_rows(index - start, size), sides, NT).T
            for side in range(2):
                first = side * half + start
                wide = min(size, cells - first)
                part = sums[side * 2 * units : (side + 1) * 2 * units, :wide]
                out_ref[:, first : first + wide] = part[:units] + part[units:]


def scatter(blocks, known, w_in, cells, baselines):
    return pl.pallas_call(
        scatter_kernel,
        out_shape=[
            jax.ShapeDtypeStruct(w_in.shape, F32),
            jax.ShapeDtypeStruct((w_in.shape[0], cells), F32),
            jax.ShapeDtypeStruct((w_in.shape[0], baselines), F32),
        ],
        compiler_params=params(),
        cost_estimate=pl.CostEstimate(
            flops=6 * 10**9, bytes_accessed=4 * 2**20, transcendentals=0
        ),
        name="scatter",
    )(*blocks, *known, w_in)


def swap(values, axis, distance):
    size = lax.axis_size(axis)
    return lax.ppermute(values, axis, [(i, i ^ distance) for i in range(size)])


def met(values, axis, distances):
    return [values, *[swap(values, axis, distance) for distance in distances]]


def sum_over_ch(values, *others):
    a, b, c, d = met(values, "ch", (2, 4, 6))
    total = after((a + b) + (c + d), *others)
    return total + swap(total, "ch", 1)


def sum_cores(mine, other, parts):
    return mine + swap(other, "bl", 1)


def sum_far(both):
    ring = lambda d: [(i, (i + 4 * d) % 16) for i in range(16)]
    got = [lax.ppermute(both[d], "bl", ring(d)) for d in (1, 2, 3)]
    return both[0] + got[0] + got[1] + got[2]


def sum_near(total):
    return total[:, :4] + swap(total[:, 4:], "bl", 2)


def together(*values):
    return lax.optimization_barrier(values)


def after(value, *others):
    return lax.optimization_barrier((value, *others))[0]


def body(
    uvw_index, row_baseline, flags, uvw_table, baseline_features, w_in, w_out, observed, delay_weight
):
    members = lax.axis_size("ch")
    rows = uvw_index.shape[0]
    local_blocks = flags.shape[1]
    local_channels = w_out.shape[2]
    half_rows = rows // 2
    per = half_rows // members

    taper = jnp.asarray(taper_table()).reshape(members, local_channels)
    hidden, hidden_t, keep, taper = trunk(
        uvw_index, row_baseline, flags, uvw_table, baseline_features, w_in, taper
    )
    constants = [jnp.asarray(table) for table in tables()]
    weight = delay_weight.reshape(BLOCK, NBLOCKS).T

    def exchange(values):
        size = values.shape[-2]
        return lax.all_to_all(
            values.reshape(members, per, PLANES, size, LANES), "ch", 0, 0, tiled=True
        )

    part = residual_part(0, 2, hidden_t, w_out, observed, keep, taper)
    hidden_t = after(hidden_t, part)
    sent_0 = exchange(part)
    index = jnp.stack([uvw_index, row_baseline]).astype(F32)
    index = jnp.concatenate([index, jnp.zeros((6, rows), F32)], axis=0)
    index = after(index, part)
    index = jnp.stack(met(index, "bl", (4, 8, 12)))
    index = jnp.stack(met(index, "bl", (1, 2, 3)), axis=1)
    part = residual_part(1, 2, hidden_t, w_out, observed, keep, taper)
    sent_1 = exchange(after(part, index))

    me = lax.axis_index("bl")
    order = lax.broadcasted_iota(jnp.int32, hidden.shape[:1], 0)
    core, x_far, y_far, unit = order // 32, (order // 8) % 4, (order // 4) % 2, order % 4
    owner = ((me // 4 + x_far) % 4) * 4 + ((me // 2) % 2 ^ y_far) * 2 + (me % 2 ^ core)
    units = lax.broadcasted_iota(jnp.int32, (hidden.shape[0],) * 2, 1)
    turn = (units == (owner * 4 + unit)[:, None]).astype(BF16)
    hidden_order = dot(turn, hidden).astype(BF16)
    w = w_out.transpose(1, 0, 2)

    (part,) = delay_filter((local_blocks,), sent_0, constants, weight)
    back_0 = exchange(part).reshape(half_rows, PLANES, local_blocks, LANES)
    known = all_rows(after(index, part), uvw_table, baseline_features, w_in)
    sizes = (local_blocks // 2, local_blocks // 2)
    counts = [size // STEP for size in sizes]
    parts = delay_filter(sizes, after(sent_1, part, *known), constants, weight)

    def arrive(part):
        return exchange(part).reshape(half_rows, PLANES, part.shape[-2], LANES)

    piece = arrive(after(parts[0], back_0, hidden_order, w))
    late = after(parts[1], piece)
    mine, other, hidden_grad = tail_part(
        0, counts[0], back_0, piece, hidden_order, w, keep, taper, jnp.zeros(hidden.shape, F32)
    )
    early = sum_cores(mine, other, 1)
    piece = after(arrive(late), early)
    mine, other, hidden_grad = tail_part(
        counts[0], counts[1], back_0, piece, hidden_order, w, keep, taper, hidden_grad
    )
    both = sum_cores(mine, other, 1)
    hidden_grad = sum_over_ch(hidden_grad, both)
    total = sum_far(jnp.concatenate([early, both], axis=3))
    near = jnp.stack(met(hidden_grad, "bl", (1, 2, 3)))
    blocks = met(near, "bl", (4, 8, 12))
    blocks[0] = after(blocks[0], total)
    grad_out = sum_near(total).transpose(1, 0, 2)
    grad_in, grad_uvw, grad_base = scatter(
        blocks, known, w_in, uvw_table.shape[1], baseline_features.shape[1]
    )
    return (grad_out, grad_in, grad_uvw, grad_base)


def solution(mesh):
    return jax.shard_map(
        body,
        mesh=mesh,
        in_specs=(
            P("bl"),
            P("bl"),
            P("bl", "ch"),
            P(),
            P(),
            P(),
            P(None, None, "ch"),
            P(None, "ch", "bl"),
            P(),
        ),
        out_specs=(P("bl", None, "ch"), P(), P(), P()),
        check_vma=False,
    )
```

```python
import functools
import math

import jax
import jax.numpy as jnp
import ml_dtypes
import numpy as np
from jax import lax
from jax.experimental import pallas as pl
from jax.experimental.pallas import tpu as pltpu
from jax.sharding import PartitionSpec as P

BLOCK = 256
NBLOCKS = 256
CHANNELS = 65536
LOSS_SCALE = 0.0625
HIGHEST = lax.Precision.HIGHEST
F32 = jnp.float32
BF16 = jnp.bfloat16
STEP = 8
WIDE = STEP * BLOCK
LANES = 128
PLANES = 4
VMEM = 63 * 2**20


def split_matrix(matrix):
    high = matrix.astype(ml_dtypes.bfloat16)
    low = (matrix - high.astype(np.float64)).astype(ml_dtypes.bfloat16)
    return high, low


def tables():
    n = np.arange(BLOCK)
    product = np.outer(n, n)
    cosine = np.cos(2 * math.pi * (product % BLOCK) / BLOCK)
    sine = np.sin(2 * math.pi * (product % BLOCK) / BLOCK)
    forward = np.block([[cosine, sine], [-sine, cosine]])
    backward = np.block([[cosine, -sine], [sine, cosine]])
    twiddle = 2 * math.pi * product / CHANNELS
    return (
        *split_matrix(forward),
        *split_matrix(backward),
        np.cos(twiddle).astype(np.float32),
        np.sin(twiddle).astype(np.float32),
    )


def taper_table():
    c = np.arange(CHANNELS)
    window = np.full((CHANNELS,), 0.35875)
    for harmonic, term in ((1, -0.48829), (2, 0.14128), (3, -0.01168)):
        window = window + term * np.cos(2 * math.pi * ((c * harmonic) % CHANNELS) / CHANNELS)
    return window.astype(np.float32)


def dot(a, b, dims=(((1,), (0,)), ((), ())), precision=None):
    return lax.dot_general(a, b, dims, precision=precision, preferred_element_type=F32)


NT = (((1,), (1,)), ((), ()))
TN = (((0,), (0,)), ((), ()))


def params(vmem=VMEM):
    return pltpu.CompilerParams(vmem_limit_bytes=vmem)


def one_hot_rows(index_row, count):
    cells = lax.broadcasted_iota(jnp.int32, (count, index_row.shape[1]), 0)
    return jnp.where(cells == index_row, 1.0, 0.0).astype(BF16)


def trunk_kernel(uvw_ref, base_ref, flags_ref, table_ref, features_ref, w_in_ref, taper_ref,
                 hidden_ref, hidden_t_ref, keep_ref, taper_here_ref):
    taper_here_ref[...] = taper_ref[pl.ds(lax.axis_index("ch"), 1), :]
    summed = dot(table_ref[...], one_hot_rows(uvw_ref[...], table_ref.shape[1]))
    summed = summed + dot(features_ref[...], one_hot_rows(base_ref[...], features_ref.shape[1]))
    inputs = summed.astype(BF16)
    pre_act = dot(w_in_ref[...], inputs, TN)
    hidden = pre_act / (1.0 + jnp.exp(-pre_act))
    hidden_ref[...] = hidden.astype(BF16)
    hidden_t_ref[...] = hidden.T.astype(BF16)
    keep_ref[...] = (1.0 - flags_ref[...].astype(F32)).T.astype(BF16)


def trunk(uvw_index, row_baseline, flags, uvw_table, baseline_features, w_in, taper):
    rows = uvw_index.shape[0]
    units = w_in.shape[1]
    return pl.pallas_call(
        trunk_kernel,
        out_shape=(
            jax.ShapeDtypeStruct((units, rows), BF16),
            jax.ShapeDtypeStruct((rows, units), BF16),
            jax.ShapeDtypeStruct(flags.shape, BF16),
            jax.ShapeDtypeStruct((1, taper.shape[1]), F32),
        ),
        compiler_params=params(),
        name="trunk",
    )(uvw_index[None], row_baseline[None], flags.T, uvw_table, baseline_features, w_in, taper)


def weight_of(keep, taper_row, first_block):
    blocks = keep.shape[1]
    block = lax.broadcasted_iota(jnp.int32, (blocks, WIDE), 0)
    lane = lax.broadcasted_iota(jnp.int32, (blocks, WIDE), 1)
    expand = jnp.where(block == first_block + (lane >> 8), 1.0, 0.0).astype(BF16)
    return dot(keep, expand) * taper_row


def residual_kernel(first_row, rows, hidden_ref, w_ref, observed_ref, keep_ref, taper_ref, out_ref):
    total = observed_ref.shape[2]
    own_rows = slice(first_row, first_row + rows)
    weight = weight_of(keep_ref[own_rows], taper_ref[...], pl.program_id(0) * STEP)
    row = lax.broadcasted_iota(jnp.int32, (rows, total), 0)
    column = lax.broadcasted_iota(jnp.int32, (rows, total), 1)
    pick = jnp.where(column == row + first_row, -1.0, 0.0).astype(BF16)
    flat = out_ref.reshape(rows * PLANES * STEP, LANES)
    units = w_ref.shape[0]
    pairs = w_ref[...].reshape(2 * units, WIDE)
    unit = lax.broadcasted_iota(jnp.int32, (units, 2 * units), 0)
    place = lax.broadcasted_iota(jnp.int32, (units, 2 * units), 1)
    for q in range(2):
        spread = jnp.where(place == unit * 2 + q, 1.0, 0.0).astype(BF16)
        own = dot(hidden_ref[own_rows], spread).astype(BF16)
        residual = dot(own, pairs) + dot(pick, observed_ref[q], NT)
        residual = residual * weight
        for b in range(STEP):
            for side in range(2):
                start = b * BLOCK + side * LANES
                flat[pl.ds((q * 2 + side) * STEP + b, rows, stride=PLANES * STEP), :] = residual[
                    :, start : start + LANES
                ]


def residual_part(first_row, rows, hidden_t, w, observed, keep, taper):
    blocks = keep.shape[1]
    return pl.pallas_call(
        functools.partial(residual_kernel, first_row, rows),
        grid=(blocks // STEP,),
        in_specs=[
            pl.BlockSpec(hidden_t.shape, lambda g: (0, 0)),
            pl.BlockSpec((w.shape[0], 2, WIDE), lambda g: (0, 0, g)),
            pl.BlockSpec((2, WIDE, observed.shape[2]), lambda g: (0, g, 0)),
            pl.BlockSpec(keep.shape, lambda g: (0, 0)),
            pl.BlockSpec((1, WIDE), lambda g: (0, g)),
        ],
        out_specs=pl.BlockSpec((rows, PLANES, STEP, LANES), lambda g: (0, 0, g, 0)),
        out_shape=jax.ShapeDtypeStruct((rows, PLANES, blocks, LANES), F32),
        compiler_params=params(),
        cost_estimate=pl.CostEstimate(
            flops=2 * rows * 2 * blocks * BLOCK * 192, bytes_accessed=10 * 2**20, transcendentals=0
        ),
        name=f"residual_{first_row}",
    )(hidden_t, w, observed, keep, taper)


def halves_of(values):
    high = values.astype(BF16)
    return high, (values - high.astype(F32)).astype(BF16)


def dot_three(a, b):
    return dot(a[0], b[0]) + (dot(a[0], b[1]) + dot(a[1], b[0]))


def delay_kernel(pieces, x_ref, fh_ref, fl_ref, bh_ref, bl_ref, cos_ref, sin_ref, weight_ref, *outs):
    forward = (fh_ref[...], fl_ref[...])
    backward = (bh_ref[...], bl_ref[...])
    cosine, sine = cos_ref[...], sin_ref[...]
    count = x_ref.shape[1]
    members, local = x_ref.shape[0], x_ref.shape[3]
    turned = []
    for i in range(count):
        values = jnp.concatenate(
            [
                jnp.concatenate(
                    [x_ref[:, i, q * 2 + side].reshape(NBLOCKS, LANES) for side in range(2)], axis=1
                )
                for q in range(2)
            ],
            axis=0,
        )
        first = dot_three(forward, halves_of(values))
        real, imag = first[:NBLOCKS], first[NBLOCKS:]
        turned.append(
            jnp.concatenate([real * cosine + imag * sine, imag * cosine - real * sine], axis=1)
        )
    second = dot_three(halves_of(jnp.concatenate(turned, axis=0)), backward)
    factor = weight_ref[...] * (LOSS_SCALE / CHANNELS)
    factor = jnp.concatenate([jnp.concatenate([factor, factor], axis=1)] * count, axis=0)
    third = dot_three(halves_of(second * factor), forward)
    for i in range(count):
        part = third[i * NBLOCKS : (i + 1) * NBLOCKS]
        real, imag = part[:, :BLOCK], part[:, BLOCK:]
        back = jnp.concatenate([real * cosine - imag * sine, imag * cosine + real * sine], axis=0)
        fourth = dot_three(backward, halves_of(back))
        for q in range(2):
            for member in range(members):
                start = q * NBLOCKS + member * local
                for out_ref, size in zip(outs, pieces):
                    for side in range(2):
                        out_ref[member, i, q * 2 + side] = fourth[
                            start : start + size, side * LANES : (side + 1) * LANES
                        ]
                    start += size


def delay_filter(pieces, arrived, constants, weight, count=2):
    members, rows, _, local, _ = arrived.shape
    whole = lambda array: pl.BlockSpec(array.shape, lambda g: (0, 0))
    flops = rows * 4 * 3 * 2 * 512 * 512 * 256
    return pl.pallas_call(
        functools.partial(delay_kernel, pieces),
        grid=(rows // count,),
        in_specs=[
            pl.BlockSpec((members, count, PLANES, local, LANES), lambda g: (0, g, 0, 0, 0)),
            *[whole(array) for array in constants],
            whole(weight),
        ],
        out_specs=[
            pl.BlockSpec((members, count, PLANES, size, LANES), lambda g: (0, g, 0, 0, 0))
            for size in pieces
        ],
        out_shape=[
            jax.ShapeDtypeStruct((members, rows, PLANES, size, LANES), F32) for size in pieces
        ],
        compiler_params=params(),
        cost_estimate=pl.CostEstimate(flops=flops, bytes_accessed=12 * 2**20, transcendentals=0),
        name=f"delay_{len(pieces)}",
    )(arrived, *constants, weight)


def tail_kernel(first, g1_ref, g2_ref, hidden_ref, w_ref, keep_ref, taper_ref, before_ref,
                mine_ref, other_ref, hidden_grad_ref):
    step = pl.program_id(0)
    weight = weight_of(keep_ref[...], taper_ref[...], (first + step) * STEP)
    flats = [
        (ref.shape[0], ref.reshape(ref.shape[0] * PLANES * STEP, LANES)) for ref in (g1_ref, g2_ref)
    ]

    @pl.when(step == 0)
    def _():
        hidden_grad_ref[...] = before_ref[...]

    total = hidden_grad_ref[...]
    for q in range(2):
        values = jnp.concatenate(
            [
                jnp.concatenate(
                    [
                        flat[pl.ds((q * 2 + side) * STEP + b, rows, stride=PLANES * STEP), :]
                        for b in range(STEP)
                        for side in range(2)
                    ],
                    axis=1,
                )
                for rows, flat in flats
            ],
            axis=0,
        )
        grad_field = (values * weight).astype(BF16)
        grad_out = dot(hidden_ref[...], grad_field)
        units = grad_out.shape[0] // 2
        for d in range(4):
            mine_ref[d, q] = grad_out[d * 8 : (d + 1) * 8]
            other_ref[d, q] = grad_out[units + d * 8 : units + (d + 1) * 8]
        total = total + dot(w_ref[q], grad_field, NT)
    hidden_grad_ref[...] = total


def tail_part(first, count, g1, g2, hidden_order, w, keep, taper, before):
    units, total_rows = hidden_order.shape
    return pl.pallas_call(
        functools.partial(tail_kernel, first),
        grid=(count,),
        in_specs=[
            pl.BlockSpec((g1.shape[0], PLANES, STEP, LANES), lambda g: (0, 0, first + g, 0)),
            pl.BlockSpec((g2.shape[0], PLANES, STEP, LANES), lambda g: (0, 0, g, 0)),
            pl.BlockSpec((units, total_rows), lambda g: (0, 0)),
            pl.BlockSpec((2, units, WIDE), lambda g: (0, 0, first + g)),
            pl.BlockSpec(keep.shape, lambda g: (0, 0)),
            pl.BlockSpec((1, WIDE), lambda g: (0, first + g)),
            pl.BlockSpec((units, total_rows), lambda g: (0, 0)),
        ],
        out_specs=[
            pl.BlockSpec((4, 2, 8, WIDE), lambda g: (0, 0, 0, g)),
            pl.BlockSpec((4, 2, 8, WIDE), lambda g: (0, 0, 0, g)),
            pl.BlockSpec((units, total_rows), lambda g: (0, 0)),
        ],
        out_shape=[
            jax.ShapeDtypeStruct((4, 2, 8, count * WIDE), F32),
            jax.ShapeDtypeStruct((4, 2, 8, count * WIDE), F32),
            jax.ShapeDtypeStruct((units, total_rows), F32),
        ],
        compiler_params=params(),
        cost_estimate=pl.CostEstimate(
            flops=count * 2 * 2 * 2 * 64 * 128 * WIDE, bytes_accessed=count * 4 * 2**20, transcendentals=0
        ),
        name=f"tail_{first}",
    )(g1, g2, hidden_order, w, keep, taper, before)


def terms_of(values, count):
    out = []
    for _ in range(count):
        term = values.astype(BF16)
        out.append(term)
        values = values - term.astype(F32)
    return out


def member_blocks(count):
    apart = [lax.axis_index("bl") ^ m for m in range(count)]
    return [(a // 4, a % 4) for a in apart]


def rows_kernel(index_ref, table_ref, features_ref, w_in_ref, inputs_ref, slope_ref, cells_ref):
    spots = member_blocks(index_ref.shape[0] * index_ref.shape[1])
    cells = jnp.concatenate([index_ref[f, n] for f, n in spots], axis=1).astype(jnp.int32)
    cells_ref[...] = cells
    summed = []
    for which, ref in ((0, table_ref), (1, features_ref)):
        total = 0.0
        for start in range(0, ref.shape[1], 512):
            size = min(512, ref.shape[1] - start)
            picked = one_hot_rows(cells[which : which + 1] - start, size)
            total = total + dot(ref[:, start : start + size], picked)
        summed.append(total)
    inputs = (summed[0] + summed[1]).astype(BF16)
    inputs_ref[...] = inputs
    pre_act = dot(w_in_ref[...], inputs, TN)
    sigmoid = 1.0 / (1.0 + jnp.exp(-pre_act))
    slope_ref[...] = sigmoid * (1.0 + pre_act * (1.0 - sigmoid))


def all_rows(index, uvw_table, baseline_features, w_in):
    rows = index.shape[0] * index.shape[1] * index.shape[3]
    return pl.pallas_call(
        rows_kernel,
        out_shape=[
            jax.ShapeDtypeStruct((w_in.shape[0], rows), BF16),
            jax.ShapeDtypeStruct((w_in.shape[1], rows), F32),
            jax.ShapeDtypeStruct((index.shape[2], rows), jnp.int32),
        ],
        compiler_params=params(),
        cost_estimate=pl.CostEstimate(flops=6 * 10**9, bytes_accessed=2**20, transcendentals=0),
        name="all_rows",
    )(index, uvw_table, baseline_features, w_in)


def scatter_kernel(own_ref, one_ref, two_ref, three_ref, inputs_ref, slope_ref, cells_ref, w_in_ref,
                   grad_in_ref, grad_uvw_ref, grad_base_ref):
    units = w_in_ref.shape[0]
    blocks = []
    for far, n in member_blocks(16):
        block = own_ref[n]
        for k, ref in ((1, one_ref), (2, two_ref), (3, three_ref)):
            block = jnp.where(far == k, ref[n], block)
        blocks.append(block)
    pre_grad = jnp.concatenate(blocks, axis=1) * slope_ref[...]
    grad_terms = jnp.concatenate(terms_of(pre_grad, 2), axis=0)
    parts = dot(inputs_ref[...], grad_terms, NT)
    grad_in_ref[...] = parts[:, :units] + parts[:, units:]
    input_grad = dot(w_in_ref[...], grad_terms[:units]) + dot(w_in_ref[...], grad_terms[units:])
    terms = jnp.concatenate(terms_of(input_grad, 2), axis=0)
    for which, out_ref in ((0, grad_uvw_ref), (1, grad_base_ref)):
        index = cells_ref[which : which + 1, :]
        cells = out_ref.shape[1]
        half = -(-cells // 2 // LANES) * LANES
        upper = index >= half
        index = jnp.where(upper, index - half, index)
        zero = jnp.zeros_like(terms)
        sides = jnp.concatenate(
            [jnp.where(upper, zero, terms), jnp.where(upper, terms, zero)], axis=0
        )
        for start in range(0, half, 512):
            size = min(512, half - start)
            sums = dot(one_hot_rows(index - start, size), sides, NT).T
            for side in range(2):
                first = side * half + start
                wide = min(size, cells - first)
                part = sums[side * 2 * units : (side + 1) * 2 * units, :wide]
                out_ref[:, first : first + wide] = part[:units] + part[units:]


def scatter(blocks, known, w_in, cells, baselines):
    return pl.pallas_call(
        scatter_kernel,
        out_shape=[
            jax.ShapeDtypeStruct(w_in.shape, F32),
            jax.ShapeDtypeStruct((w_in.shape[0], cells), F32),
            jax.ShapeDtypeStruct((w_in.shape[0], baselines), F32),
        ],
        compiler_params=params(32 * 2**20),
        cost_estimate=pl.CostEstimate(
            flops=6 * 10**9, bytes_accessed=4 * 2**20, transcendentals=0
        ),
        name="scatter",
    )(*blocks, *known, w_in)


def swap(values, axis, distance):
    size = lax.axis_size(axis)
    return lax.ppermute(values, axis, [(i, i ^ distance) for i in range(size)])


def met(values, axis, distances):
    return [values, *[swap(values, axis, distance) for distance in distances]]


def sum_over_ch(values, *others):
    a, b, c, d = met(values, "ch", (2, 4, 6))
    total = after((a + b) + (c + d), *others)
    return total + swap(total, "ch", 1)


def sum_cores(mine, other, parts):
    return mine + swap(other, "bl", 1)


def sum_far(both):
    ring = lambda d: [(i, (i + 4 * d) % 16) for i in range(16)]
    got = [lax.ppermute(both[d], "bl", ring(d)) for d in (1, 2, 3)]
    return both[0] + got[0] + got[1] + got[2]


def sum_near(total):
    return total[:, :4] + swap(total[:, 4:], "bl", 2)


def together(*values):
    return lax.optimization_barrier(values)


def after(value, *others):
    return lax.optimization_barrier((value, *others))[0]


def body(
    uvw_index, row_baseline, flags, uvw_table, baseline_features, w_in, w_out, observed, delay_weight
):
    members = lax.axis_size("ch")
    rows = uvw_index.shape[0]
    local_blocks = flags.shape[1]
    local_channels = w_out.shape[2]
    head_rows = rows * 4 // 16

    taper = jnp.asarray(taper_table()).reshape(members, local_channels)
    hidden, hidden_t, keep, taper = trunk(
        uvw_index, row_baseline, flags, uvw_table, baseline_features, w_in, taper
    )
    constants = [jnp.asarray(table) for table in tables()]
    weight = delay_weight.reshape(BLOCK, NBLOCKS).T

    def exchange(values):
        size = values.shape[-2]
        return lax.all_to_all(
            values.reshape(members, -1, PLANES, size, LANES), "ch", 0, 0, tiled=True
        )

    def arrive(part):
        return exchange(part).reshape(-1, PLANES, part.shape[-2], LANES)

    part = residual_part(0, head_rows, hidden_t, w_out, observed, keep, taper)
    hidden_t = after(hidden_t, part)
    sent_0 = exchange(part)
    index = jnp.stack([uvw_index, row_baseline]).astype(F32)
    index = jnp.concatenate([index, jnp.zeros((6, rows), F32)], axis=0)
    index = after(index, part)
    index = jnp.stack(met(index, "bl", (4, 8, 12)))
    index = jnp.stack(met(index, "bl", (1, 2, 3)), axis=1)
    part = residual_part(head_rows, rows - head_rows, hidden_t, w_out, observed, keep, taper)
    sent_1 = exchange(after(part, index))

    me = lax.axis_index("bl")
    order = lax.broadcasted_iota(jnp.int32, hidden.shape[:1], 0)
    core, x_far, y_far, unit = order // 32, (order // 8) % 4, (order // 4) % 2, order % 4
    owner = ((me // 4 + x_far) % 4) * 4 + ((me // 2) % 2 ^ y_far) * 2 + (me % 2 ^ core)
    units = lax.broadcasted_iota(jnp.int32, (hidden.shape[0],) * 2, 1)
    turn = (units == (owner * 4 + unit)[:, None]).astype(BF16)
    hidden_order = dot(turn, hidden).astype(BF16)
    w = w_out.transpose(1, 0, 2)

    (part,) = delay_filter((local_blocks,), sent_0, constants, weight)
    known = all_rows(after(index, part), uvw_table, baseline_features, w_in)
    part = after(part, hidden_order, w, *known)
    back_0 = arrive(part)
    sizes = (local_blocks * 16 // 32, local_blocks * 16 // 32)
    counts = [size // STEP for size in sizes]
    parts = delay_filter(sizes, after(sent_1, part), constants, weight)

    piece = arrive(after(parts[0], back_0))
    late = after(parts[1], piece)
    mine, other, hidden_grad = tail_part(
        0, counts[0], back_0, piece, hidden_order, w, keep, taper, jnp.zeros(hidden.shape, F32)
    )
    both = sum_cores(mine, other, 1)
    piece = after(arrive(late), both)
    first = sum_far(both)
    mine, other, hidden_grad = tail_part(
        counts[0], counts[1], back_0, piece, hidden_order, w, keep, taper, hidden_grad
    )
    both = sum_cores(mine, other, 1)
    hidden_grad = sum_over_ch(hidden_grad, both, first)
    second = sum_far(both)
    near = after(jnp.stack(met(hidden_grad, "bl", (1, 2, 3))), second)
    blocks = met(near, "bl", (4, 8, 12))
    grad_out = sum_near(jnp.concatenate([first, second], axis=2)).transpose(1, 0, 2)
    grad_in, grad_uvw, grad_base = scatter(
        blocks, known, w_in, uvw_table.shape[1], baseline_features.shape[1]
    )
    return (grad_out, grad_in, grad_uvw, grad_base)


def solution(mesh):
    return jax.shard_map(
        body,
        mesh=mesh,
        in_specs=(
            P("bl"),
            P("bl"),
            P("bl", "ch"),
            P(),
            P(),
            P(),
            P(None, None, "ch"),
            P(None, "ch", "bl"),
            P(),
        ),
        out_specs=(P("bl", None, "ch"), P(), P(), P()),
        check_vma=False,
    )
```

```python
import functools
import math

import jax
import jax.numpy as jnp
import ml_dtypes
import numpy as np
from jax import lax
from jax.experimental import pallas as pl
from jax.experimental.pallas import tpu as pltpu
from jax.sharding import PartitionSpec as P

BLOCK = 256
NBLOCKS = 256
CHANNELS = 65536
LOSS_SCALE = 0.0625
HIGHEST = lax.Precision.HIGHEST
F32 = jnp.float32
BF16 = jnp.bfloat16
STEP = 8
WIDE = STEP * BLOCK
LANES = 128
PLANES = 4
VMEM = 63 * 2**20


def split_matrix(matrix):
    high = matrix.astype(ml_dtypes.bfloat16)
    low = (matrix - high.astype(np.float64)).astype(ml_dtypes.bfloat16)
    return high, low


def tables():
    n = np.arange(BLOCK)
    product = np.outer(n, n)
    cosine = np.cos(2 * math.pi * (product % BLOCK) / BLOCK)
    sine = np.sin(2 * math.pi * (product % BLOCK) / BLOCK)
    forward = np.block([[cosine, sine], [-sine, cosine]])
    backward = np.block([[cosine, -sine], [sine, cosine]])
    twiddle = 2 * math.pi * product / CHANNELS
    return (
        *split_matrix(forward),
        *split_matrix(backward),
        np.cos(twiddle).astype(np.float32),
        np.sin(twiddle).astype(np.float32),
    )


def taper_table():
    c = np.arange(CHANNELS)
    window = np.full((CHANNELS,), 0.35875)
    for harmonic, term in ((1, -0.48829), (2, 0.14128), (3, -0.01168)):
        window = window + term * np.cos(2 * math.pi * ((c * harmonic) % CHANNELS) / CHANNELS)
    return window.astype(np.float32)


def dot(a, b, dims=(((1,), (0,)), ((), ())), precision=None):
    return lax.dot_general(a, b, dims, precision=precision, preferred_element_type=F32)


NT = (((1,), (1,)), ((), ()))
TN = (((0,), (0,)), ((), ()))


def params(vmem=VMEM):
    return pltpu.CompilerParams(vmem_limit_bytes=vmem)


def one_hot_rows(index_row, count):
    cells = lax.broadcasted_iota(jnp.int32, (count, index_row.shape[1]), 0)
    return jnp.where(cells == index_row, 1.0, 0.0).astype(BF16)


def trunk_kernel(uvw_ref, base_ref, flags_ref, table_ref, features_ref, w_in_ref, taper_ref,
                 hidden_ref, hidden_t_ref, keep_ref, taper_here_ref):
    taper_here_ref[...] = taper_ref[pl.ds(lax.axis_index("ch"), 1), :]
    summed = dot(table_ref[...], one_hot_rows(uvw_ref[...], table_ref.shape[1]))
    summed = summed + dot(features_ref[...], one_hot_rows(base_ref[...], features_ref.shape[1]))
    inputs = summed.astype(BF16)
    pre_act = dot(w_in_ref[...], inputs, TN)
    hidden = pre_act / (1.0 + jnp.exp(-pre_act))
    hidden_ref[...] = hidden.astype(BF16)
    hidden_t_ref[...] = hidden.T.astype(BF16)
    keep_ref[...] = (1.0 - flags_ref[...].astype(F32)).T.astype(BF16)


def trunk(uvw_index, row_baseline, flags, uvw_table, baseline_features, w_in, taper):
    rows = uvw_index.shape[0]
    units = w_in.shape[1]
    return pl.pallas_call(
        trunk_kernel,
        out_shape=(
            jax.ShapeDtypeStruct((units, rows), BF16),
            jax.ShapeDtypeStruct((rows, units), BF16),
            jax.ShapeDtypeStruct(flags.shape, BF16),
            jax.ShapeDtypeStruct((1, taper.shape[1]), F32),
        ),
        compiler_params=params(),
        name="trunk",
    )(uvw_index[None], row_baseline[None], flags.T, uvw_table, baseline_features, w_in, taper)


def weight_of(keep, taper_row, first_block):
    blocks = keep.shape[1]
    block = lax.broadcasted_iota(jnp.int32, (blocks, WIDE), 0)
    lane = lax.broadcasted_iota(jnp.int32, (blocks, WIDE), 1)
    expand = jnp.where(block == first_block + (lane >> 8), 1.0, 0.0).astype(BF16)
    return dot(keep, expand) * taper_row


def residual_kernel(first_row, rows, hidden_ref, w_ref, observed_ref, keep_ref, taper_ref, out_ref):
    total = observed_ref.shape[2]
    own_rows = slice(first_row, first_row + rows)
    weight = weight_of(keep_ref[own_rows], taper_ref[...], pl.program_id(0) * STEP)
    row = lax.broadcasted_iota(jnp.int32, (rows, total), 0)
    column = lax.broadcasted_iota(jnp.int32, (rows, total), 1)
    pick = jnp.where(column == row + first_row, -1.0, 0.0).astype(BF16)
    flat = out_ref.reshape(rows * PLANES * STEP, LANES)
    units = w_ref.shape[0]
    pairs = w_ref[...].reshape(2 * units, WIDE)
    unit = lax.broadcasted_iota(jnp.int32, (units, 2 * units), 0)
    place = lax.broadcasted_iota(jnp.int32, (units, 2 * units), 1)
    spread = jnp.concatenate(
        [jnp.where(place == unit * 2 + q, 1.0, 0.0).astype(BF16) for q in range(2)], axis=1
    )
    own = dot(hidden_ref[own_rows], spread).astype(BF16)
    fields = dot(jnp.concatenate([own[:, : 2 * units], own[:, 2 * units :]], axis=0), pairs)
    for q in range(2):
        residual = fields[q * rows : (q + 1) * rows] + dot(pick, observed_ref[q], NT)
        residual = residual * weight
        for b in range(STEP):
            for side in range(2):
                start = b * BLOCK + side * LANES
                flat[pl.ds((q * 2 + side) * STEP + b, rows, stride=PLANES * STEP), :] = residual[
                    :, start : start + LANES
                ]


def residual_part(first_row, rows, hidden_t, w, observed, keep, taper):
    blocks = keep.shape[1]
    return pl.pallas_call(
        functools.partial(residual_kernel, first_row, rows),
        grid=(blocks // STEP,),
        in_specs=[
            pl.BlockSpec(hidden_t.shape, lambda g: (0, 0)),
            pl.BlockSpec((w.shape[0], 2, WIDE), lambda g: (0, 0, g)),
            pl.BlockSpec((2, WIDE, observed.shape[2]), lambda g: (0, g, 0)),
            pl.BlockSpec(keep.shape, lambda g: (0, 0)),
            pl.BlockSpec((1, WIDE), lambda g: (0, g)),
        ],
        out_specs=pl.BlockSpec((rows, PLANES, STEP, LANES), lambda g: (0, 0, g, 0)),
        out_shape=jax.ShapeDtypeStruct((rows, PLANES, blocks, LANES), F32),
        compiler_params=params(),
        cost_estimate=pl.CostEstimate(
            flops=2 * rows * 2 * blocks * BLOCK * 192, bytes_accessed=10 * 2**20, transcendentals=0
        ),
        name=f"residual_{first_row}",
    )(hidden_t, w, observed, keep, taper)


def halves_of(values):
    high = values.astype(BF16)
    return high, (values - high.astype(F32)).astype(BF16)


def dot_three(a, b):
    return dot(a[0], b[0]) + (dot(a[0], b[1]) + dot(a[1], b[0]))


def delay_kernel(pieces, x_ref, fh_ref, fl_ref, bh_ref, bl_ref, cos_ref, sin_ref, weight_ref, *outs):
    forward = (fh_ref[...], fl_ref[...])
    backward = (bh_ref[...], bl_ref[...])
    cosine, sine = cos_ref[...], sin_ref[...]
    count = x_ref.shape[1]
    members, local = x_ref.shape[0], x_ref.shape[3]
    turned = []
    for i in range(count):
        values = jnp.concatenate(
            [
                jnp.concatenate(
                    [x_ref[:, i, q * 2 + side].reshape(NBLOCKS, LANES) for side in range(2)], axis=1
                )
                for q in range(2)
            ],
            axis=0,
        )
        first = dot_three(forward, halves_of(values))
        real, imag = first[:NBLOCKS], first[NBLOCKS:]
        turned.append(
            jnp.concatenate([real * cosine + imag * sine, imag * cosine - real * sine], axis=1)
        )
    second = dot_three(halves_of(jnp.concatenate(turned, axis=0)), backward)
    factor = weight_ref[...] * (LOSS_SCALE / CHANNELS)
    factor = jnp.concatenate([jnp.concatenate([factor, factor], axis=1)] * count, axis=0)
    third = dot_three(halves_of(second * factor), forward)
    for i in range(count):
        part = third[i * NBLOCKS : (i + 1) * NBLOCKS]
        real, imag = part[:, :BLOCK], part[:, BLOCK:]
        back = jnp.concatenate([real * cosine - imag * sine, imag * cosine + real * sine], axis=0)
        fourth = dot_three(backward, halves_of(back))
        for q in range(2):
            for member in range(members):
                start = q * NBLOCKS + member * local
                for out_ref, size in zip(outs, pieces):
                    for side in range(2):
                        out_ref[member, i, q * 2 + side] = fourth[
                            start : start + size, side * LANES : (side + 1) * LANES
                        ]
                    start += size


def delay_filter(pieces, arrived, constants, weight, count=2):
    members, rows, _, local, _ = arrived.shape
    whole = lambda array: pl.BlockSpec(array.shape, lambda g: (0, 0))
    flops = rows * 4 * 3 * 2 * 512 * 512 * 256
    return pl.pallas_call(
        functools.partial(delay_kernel, pieces),
        grid=(rows // count,),
        in_specs=[
            pl.BlockSpec((members, count, PLANES, local, LANES), lambda g: (0, g, 0, 0, 0)),
            *[whole(array) for array in constants],
            whole(weight),
        ],
        out_specs=[
            pl.BlockSpec((members, count, PLANES, size, LANES), lambda g: (0, g, 0, 0, 0))
            for size in pieces
        ],
        out_shape=[
            jax.ShapeDtypeStruct((members, rows, PLANES, size, LANES), F32) for size in pieces
        ],
        compiler_params=params(),
        cost_estimate=pl.CostEstimate(flops=flops, bytes_accessed=12 * 2**20, transcendentals=0),
        name=f"delay_{len(pieces)}",
    )(arrived, *constants, weight)


def tail_kernel(first, g1_ref, g2_ref, hidden_ref, w_ref, keep_ref, taper_ref, before_ref,
                mine_ref, other_ref, hidden_grad_ref, weight_ref):
    step = pl.program_id(0)
    flats = [
        (ref.shape[0], ref.reshape(ref.shape[0] * 2 * STEP, LANES)) for ref in (g1_ref, g2_ref)
    ]

    @pl.when(pl.program_id(1) == 0)
    def _():
        weight_ref[...] = weight_of(keep_ref[...], taper_ref[...], (first + step) * STEP)

    @pl.when((step == 0) & (pl.program_id(1) == 0))
    def _():
        hidden_grad_ref[...] = before_ref[...]

    values = jnp.concatenate(
        [
            jnp.concatenate(
                [
                    flat[pl.ds(side * STEP + b, rows, stride=2 * STEP), :]
                    for b in range(STEP)
                    for side in range(2)
                ],
                axis=1,
            )
            for rows, flat in flats
        ],
        axis=0,
    )
    grad_field = (values * weight_ref[...]).astype(BF16)
    grad_out = dot(hidden_ref[...], grad_field)
    units = grad_out.shape[0] // 2
    for d in range(4):
        mine_ref[d, 0] = grad_out[d * 8 : (d + 1) * 8]
        other_ref[d, 0] = grad_out[units + d * 8 : units + (d + 1) * 8]
    hidden_grad_ref[...] += dot(w_ref[0], grad_field, NT)


def tail_part(first, count, g1, g2, hidden_order, w, keep, taper, before):
    units, total_rows = hidden_order.shape
    return pl.pallas_call(
        functools.partial(tail_kernel, first),
        grid=(count, 2),
        in_specs=[
            pl.BlockSpec((g1.shape[0], 2, STEP, LANES), lambda g, q: (0, q, first + g, 0)),
            pl.BlockSpec((g2.shape[0], 2, STEP, LANES), lambda g, q: (0, q, g, 0)),
            pl.BlockSpec((units, total_rows), lambda g, q: (0, 0)),
            pl.BlockSpec((1, units, WIDE), lambda g, q: (q, 0, first + g)),
            pl.BlockSpec(keep.shape, lambda g, q: (0, 0)),
            pl.BlockSpec((1, WIDE), lambda g, q: (0, first + g)),
            pl.BlockSpec((units, total_rows), lambda g, q: (0, 0)),
        ],
        out_specs=[
            pl.BlockSpec((4, 1, 8, WIDE), lambda g, q: (0, q, 0, g)),
            pl.BlockSpec((4, 1, 8, WIDE), lambda g, q: (0, q, 0, g)),
            pl.BlockSpec((units, total_rows), lambda g, q: (0, 0)),
        ],
        out_shape=[
            jax.ShapeDtypeStruct((4, 2, 8, count * WIDE), F32),
            jax.ShapeDtypeStruct((4, 2, 8, count * WIDE), F32),
            jax.ShapeDtypeStruct((units, total_rows), F32),
        ],
        scratch_shapes=[pltpu.VMEM((total_rows, WIDE), F32)],
        compiler_params=params(),
        cost_estimate=pl.CostEstimate(
            flops=count * 2 * 2 * 2 * 64 * 128 * WIDE, bytes_accessed=count * 4 * 2**20, transcendentals=0
        ),
        name=f"tail_{first}",
    )(g1, g2, hidden_order, w, keep, taper, before)


def terms_of(values, count):
    out = []
    for _ in range(count):
        term = values.astype(BF16)
        out.append(term)
        values = values - term.astype(F32)
    return out


def member_blocks(count):
    apart = [lax.axis_index("bl") ^ m for m in range(count)]
    return [(a // 4, a % 4) for a in apart]


def rows_kernel(index_ref, table_ref, features_ref, w_in_ref, inputs_ref, slope_ref, cells_ref):
    spots = member_blocks(index_ref.shape[0] * index_ref.shape[1])
    cells = jnp.concatenate([index_ref[f, n] for f, n in spots], axis=1).astype(jnp.int32)
    cells_ref[...] = cells
    summed = []
    for which, ref in ((0, table_ref), (1, features_ref)):
        total = 0.0
        for start in range(0, ref.shape[1], 512):
            size = min(512, ref.shape[1] - start)
            picked = one_hot_rows(cells[which : which + 1] - start, size)
            total = total + dot(ref[:, start : start + size], picked)
        summed.append(total)
    inputs = (summed[0] + summed[1]).astype(BF16)
    inputs_ref[...] = inputs
    pre_act = dot(w_in_ref[...], inputs, TN)
    sigmoid = 1.0 / (1.0 + jnp.exp(-pre_act))
    slope_ref[...] = sigmoid * (1.0 + pre_act * (1.0 - sigmoid))


def all_rows(index, uvw_table, baseline_features, w_in):
    rows = index.shape[0] * index.shape[1] * index.shape[3]
    return pl.pallas_call(
        rows_kernel,
        out_shape=[
            jax.ShapeDtypeStruct((w_in.shape[0], rows), BF16),
            jax.ShapeDtypeStruct((w_in.shape[1], rows), F32),
            jax.ShapeDtypeStruct((index.shape[2], rows), jnp.int32),
        ],
        compiler_params=params(),
        cost_estimate=pl.CostEstimate(flops=6 * 10**9, bytes_accessed=2**20, transcendentals=0),
        name="all_rows",
    )(index, uvw_table, baseline_features, w_in)


def scatter_kernel(own_ref, one_ref, two_ref, three_ref, inputs_ref, slope_ref, cells_ref, w_in_ref,
                   grad_in_ref, grad_uvw_ref, grad_base_ref):
    units = w_in_ref.shape[0]
    blocks = []
    for far, n in member_blocks(16):
        block = own_ref[n]
        for k, ref in ((1, one_ref), (2, two_ref), (3, three_ref)):
            block = jnp.where(far == k, ref[n], block)
        blocks.append(block)
    pre_grad = jnp.concatenate(blocks, axis=1) * slope_ref[...]
    grad_terms = jnp.concatenate(terms_of(pre_grad, 2), axis=0)
    parts = dot(inputs_ref[...], grad_terms, NT)
    grad_in_ref[...] = parts[:, :units] + parts[:, units:]
    input_grad = dot(w_in_ref[...], grad_terms[:units]) + dot(w_in_ref[...], grad_terms[units:])
    terms = jnp.concatenate(terms_of(input_grad, 2), axis=0)
    for which, out_ref in ((0, grad_uvw_ref), (1, grad_base_ref)):
        index = cells_ref[which : which + 1, :]
        cells = out_ref.shape[1]
        half = -(-cells // 2 // LANES) * LANES
        upper = index >= half
        index = jnp.where(upper, index - half, index)
        zero = jnp.zeros_like(terms)
        sides = jnp.concatenate(
            [jnp.where(upper, zero, terms), jnp.where(upper, terms, zero)], axis=0
        )
        for start in range(0, half, 512):
            size = min(512, half - start)
            sums = dot(one_hot_rows(index - start, size), sides, NT).T
            for side in range(2):
                first = side * half + start
                wide = min(size, cells - first)
                part = sums[side * 2 * units : (side + 1) * 2 * units, :wide]
                out_ref[:, first : first + wide] = part[:units] + part[units:]


def scatter(blocks, known, w_in, cells, baselines):
    return pl.pallas_call(
        scatter_kernel,
        out_shape=[
            jax.ShapeDtypeStruct(w_in.shape, F32),
            jax.ShapeDtypeStruct((w_in.shape[0], cells), F32),
            jax.ShapeDtypeStruct((w_in.shape[0], baselines), F32),
        ],
        compiler_params=params(32 * 2**20),
        cost_estimate=pl.CostEstimate(
            flops=6 * 10**9, bytes_accessed=4 * 2**20, transcendentals=0
        ),
        name="scatter",
    )(*blocks, *known, w_in)


def swap(values, axis, distance):
    size = lax.axis_size(axis)
    return lax.ppermute(values, axis, [(i, i ^ distance) for i in range(size)])


def met(values, axis, distances):
    return [values, *[swap(values, axis, distance) for distance in distances]]


def sum_over_ch(values, *others):
    a, b, c, d = met(values, "ch", (2, 4, 6))
    total = after((a + b) + (c + d), *others)
    return total + swap(total, "ch", 1)


def sum_cores(mine, other, parts):
    return mine + swap(other, "bl", 1)


def sum_far(both):
    ring = lambda d: [(i, (i + 4 * d) % 16) for i in range(16)]
    got = [lax.ppermute(both[d], "bl", ring(d)) for d in (1, 2, 3)]
    return both[0] + got[0] + got[1] + got[2]


def sum_near(total):
    return total[:, :4] + swap(total[:, 4:], "bl", 2)


def together(*values):
    return lax.optimization_barrier(values)


def after(value, *others):
    return lax.optimization_barrier((value, *others))[0]


def body(
    uvw_index, row_baseline, flags, uvw_table, baseline_features, w_in, w_out, observed, delay_weight
):
    members = lax.axis_size("ch")
    rows = uvw_index.shape[0]
    local_blocks = flags.shape[1]
    local_channels = w_out.shape[2]
    head_rows = rows * 6 // 16

    taper = jnp.asarray(taper_table()).reshape(members, local_channels)
    hidden, hidden_t, keep, taper = trunk(
        uvw_index, row_baseline, flags, uvw_table, baseline_features, w_in, taper
    )
    constants = [jnp.asarray(table) for table in tables()]
    weight = delay_weight.reshape(BLOCK, NBLOCKS).T

    def exchange(values):
        size = values.shape[-2]
        return lax.all_to_all(
            values.reshape(members, -1, PLANES, size, LANES), "ch", 0, 0, tiled=True
        )

    def arrive(part):
        return exchange(part).reshape(-1, PLANES, part.shape[-2], LANES)

    part = residual_part(0, head_rows, hidden_t, w_out, observed, keep, taper)
    hidden_t = after(hidden_t, part)
    index = jnp.stack([uvw_index, row_baseline]).astype(F32)
    index = jnp.concatenate([index, jnp.zeros((6, rows), F32)], axis=0)
    index = jnp.stack([index, swap(index, "bl", 2)])
    sent_0 = exchange(after(part, index))
    index = after(index, part)
    across = swap(index, "bl", 1)
    index = jnp.stack([index[0], across[0], index[1], across[1]])
    index = jnp.stack(met(index, "bl", (4, 8, 12)))
    part = residual_part(head_rows, rows - head_rows, hidden_t, w_out, observed, keep, taper)
    sent_1 = exchange(after(part, index))

    me = lax.axis_index("bl")
    order = lax.broadcasted_iota(jnp.int32, hidden.shape[:1], 0)
    core, x_far, y_far, unit = order // 32, (order // 8) % 4, (order // 4) % 2, order % 4
    owner = ((me // 4 + x_far) % 4) * 4 + ((me // 2) % 2 ^ y_far) * 2 + (me % 2 ^ core)
    units = lax.broadcasted_iota(jnp.int32, (hidden.shape[0],) * 2, 1)
    turn = (units == (owner * 4 + unit)[:, None]).astype(BF16)
    hidden_order = dot(turn, hidden).astype(BF16)
    w = w_out.transpose(1, 0, 2)

    (part,) = delay_filter((local_blocks,), sent_0, constants, weight)
    known = all_rows(after(index, part), uvw_table, baseline_features, w_in)
    part = after(part, hidden_order, w, *known)
    back_0 = arrive(part)
    sizes = (local_blocks * 16 // 32, local_blocks * 16 // 32)
    counts = [size // STEP for size in sizes]
    parts = delay_filter(sizes, after(sent_1, part), constants, weight)

    piece = arrive(after(parts[0], back_0))
    late = after(parts[1], piece)
    mine, other, hidden_grad = tail_part(
        0, counts[0], back_0, piece, hidden_order, w, keep, taper, jnp.zeros(hidden.shape, F32)
    )
    both = sum_cores(mine, other, 1)
    piece = after(arrive(late), both)
    first = sum_far(both)
    mine, other, hidden_grad = tail_part(
        counts[0], counts[1], back_0, piece, hidden_order, w, keep, taper, hidden_grad
    )
    both = sum_cores(mine, other, 1)
    hidden_grad = sum_over_ch(hidden_grad, both, first)
    second = sum_far(both)
    near = after(jnp.stack(met(hidden_grad, "bl", (1, 2, 3))), second)
    blocks = met(near, "bl", (4, 8, 12))
    grad_out = sum_near(jnp.concatenate([first, second], axis=2)).transpose(1, 0, 2)
    grad_in, grad_uvw, grad_base = scatter(
        blocks, known, w_in, uvw_table.shape[1], baseline_features.shape[1]
    )
    return (grad_out, grad_in, grad_uvw, grad_base)


def solution(mesh):
    return jax.shard_map(
        body,
        mesh=mesh,
        in_specs=(
            P("bl"),
            P("bl"),
            P("bl", "ch"),
            P(),
            P(),
            P(),
            P(None, None, "ch"),
            P(None, "ch", "bl"),
            P(),
        ),
        out_specs=(P("bl", None, "ch"), P(), P(), P()),
        check_vma=False,
    )
```

```python
import functools
import math

import jax
import jax.numpy as jnp
import ml_dtypes
import numpy as np
from jax import lax
from jax.experimental import pallas as pl
from jax.experimental.pallas import tpu as pltpu
from jax.sharding import PartitionSpec as P

BLOCK = 256
NBLOCKS = 256
CHANNELS = 65536
LOSS_SCALE = 0.0625
HIGHEST = lax.Precision.HIGHEST
F32 = jnp.float32
BF16 = jnp.bfloat16
STEP = 8
WIDE = STEP * BLOCK
LANES = 128
PLANES = 4
VMEM = 63 * 2**20


def split_matrix(matrix):
    high = matrix.astype(ml_dtypes.bfloat16)
    low = (matrix - high.astype(np.float64)).astype(ml_dtypes.bfloat16)
    return high, low


def tables():
    n = np.arange(BLOCK)
    product = np.outer(n, n)
    cosine = np.cos(2 * math.pi * (product % BLOCK) / BLOCK)
    sine = np.sin(2 * math.pi * (product % BLOCK) / BLOCK)
    forward = np.block([[cosine, sine], [-sine, cosine]])
    backward = np.block([[cosine, -sine], [sine, cosine]])
    twiddle = 2 * math.pi * product / CHANNELS
    return (
        *split_matrix(forward),
        *split_matrix(backward),
        np.cos(twiddle).astype(np.float32),
        np.sin(twiddle).astype(np.float32),
    )


def taper_table():
    c = np.arange(CHANNELS)
    window = np.full((CHANNELS,), 0.35875)
    for harmonic, term in ((1, -0.48829), (2, 0.14128), (3, -0.01168)):
        window = window + term * np.cos(2 * math.pi * ((c * harmonic) % CHANNELS) / CHANNELS)
    return window.astype(np.float32)


def dot(a, b, dims=(((1,), (0,)), ((), ())), precision=None):
    return lax.dot_general(a, b, dims, precision=precision, preferred_element_type=F32)


NT = (((1,), (1,)), ((), ()))
TN = (((0,), (0,)), ((), ()))


def params(vmem=VMEM):
    return pltpu.CompilerParams(vmem_limit_bytes=vmem)


def one_hot_rows(index_row, count):
    cells = lax.broadcasted_iota(jnp.int32, (count, index_row.shape[1]), 0)
    return jnp.where(cells == index_row, 1.0, 0.0).astype(BF16)


def trunk_kernel(uvw_ref, base_ref, flags_ref, table_ref, features_ref, w_in_ref, taper_ref,
                 hidden_ref, hidden_t_ref, keep_ref, taper_here_ref):
    taper_here_ref[...] = taper_ref[pl.ds(lax.axis_index("ch"), 1), :]
    summed = dot(table_ref[...], one_hot_rows(uvw_ref[...], table_ref.shape[1]))
    summed = summed + dot(features_ref[...], one_hot_rows(base_ref[...], features_ref.shape[1]))
    inputs = summed.astype(BF16)
    pre_act = dot(w_in_ref[...], inputs, TN)
    hidden = pre_act / (1.0 + jnp.exp(-pre_act))
    hidden_ref[...] = hidden.astype(BF16)
    hidden_t_ref[...] = hidden.T.astype(BF16)
    keep_ref[...] = (1.0 - flags_ref[...].astype(F32)).T.astype(BF16)


def trunk(uvw_index, row_baseline, flags, uvw_table, baseline_features, w_in, taper):
    rows = uvw_index.shape[0]
    units = w_in.shape[1]
    return pl.pallas_call(
        trunk_kernel,
        out_shape=(
            jax.ShapeDtypeStruct((units, rows), BF16),
            jax.ShapeDtypeStruct((rows, units), BF16),
            jax.ShapeDtypeStruct(flags.shape, BF16),
            jax.ShapeDtypeStruct((1, taper.shape[1]), F32),
        ),
        compiler_params=params(),
        name="trunk",
    )(uvw_index[None], row_baseline[None], flags.T, uvw_table, baseline_features, w_in, taper)


def weight_of(keep, taper_row, first_block):
    blocks = keep.shape[1]
    block = lax.broadcasted_iota(jnp.int32, (blocks, WIDE), 0)
    lane = lax.broadcasted_iota(jnp.int32, (blocks, WIDE), 1)
    expand = jnp.where(block == first_block + (lane >> 8), 1.0, 0.0).astype(BF16)
    return dot(keep, expand) * taper_row


def residual_kernel(first_row, rows, hidden_ref, w_ref, observed_ref, keep_ref, taper_ref, out_ref):
    total = observed_ref.shape[2]
    own_rows = slice(first_row, first_row + rows)
    weight = weight_of(keep_ref[own_rows], taper_ref[...], pl.program_id(0) * STEP)
    row = lax.broadcasted_iota(jnp.int32, (rows, total), 0)
    column = lax.broadcasted_iota(jnp.int32, (rows, total), 1)
    pick = jnp.where(column == row + first_row, -1.0, 0.0).astype(BF16)
    flat = out_ref.reshape(rows * PLANES * STEP, LANES)
    units = w_ref.shape[0]
    pairs = w_ref[...].reshape(2 * units, WIDE)
    unit = lax.broadcasted_iota(jnp.int32, (units, 2 * units), 0)
    place = lax.broadcasted_iota(jnp.int32, (units, 2 * units), 1)
    spread = jnp.concatenate(
        [jnp.where(place == unit * 2 + q, 1.0, 0.0).astype(BF16) for q in range(2)], axis=1
    )
    own = dot(hidden_ref[own_rows], spread).astype(BF16)
    fields = dot(jnp.concatenate([own[:, : 2 * units], own[:, 2 * units :]], axis=0), pairs)
    for q in range(2):
        residual = fields[q * rows : (q + 1) * rows] + dot(pick, observed_ref[q], NT)
        residual = residual * weight
        for b in range(STEP):
            for side in range(2):
                start = b * BLOCK + side * LANES
                flat[pl.ds((q * 2 + side) * STEP + b, rows, stride=PLANES * STEP), :] = residual[
                    :, start : start + LANES
                ]


def residual_part(first_row, rows, hidden_t, w, observed, keep, taper):
    blocks = keep.shape[1]
    return pl.pallas_call(
        functools.partial(residual_kernel, first_row, rows),
        grid=(blocks // STEP,),
        in_specs=[
            pl.BlockSpec(hidden_t.shape, lambda g: (0, 0)),
            pl.BlockSpec((w.shape[0], 2, WIDE), lambda g: (0, 0, g)),
            pl.BlockSpec((2, WIDE, observed.shape[2]), lambda g: (0, g, 0)),
            pl.BlockSpec(keep.shape, lambda g: (0, 0)),
            pl.BlockSpec((1, WIDE), lambda g: (0, g)),
        ],
        out_specs=pl.BlockSpec((rows, PLANES, STEP, LANES), lambda g: (0, 0, g, 0)),
        out_shape=jax.ShapeDtypeStruct((rows, PLANES, blocks, LANES), F32),
        compiler_params=params(),
        cost_estimate=pl.CostEstimate(
            flops=2 * rows * 2 * blocks * BLOCK * 192, bytes_accessed=10 * 2**20, transcendentals=0
        ),
        name=f"residual_{first_row}",
    )(hidden_t, w, observed, keep, taper)


def halves_of(values):
    high = values.astype(BF16)
    return high, (values - high.astype(F32)).astype(BF16)


def dot_three(a, b):
    return dot(a[0], b[0]) + (dot(a[0], b[1]) + dot(a[1], b[0]))


def delay_kernel(pieces, x_ref, fh_ref, fl_ref, bh_ref, bl_ref, cos_ref, sin_ref, weight_ref, *outs):
    forward = (fh_ref[...], fl_ref[...])
    backward = (bh_ref[...], bl_ref[...])
    cosine, sine = cos_ref[...], sin_ref[...]
    count = x_ref.shape[1]
    members, local = x_ref.shape[0], x_ref.shape[3]
    turned = []
    for i in range(count):
        values = jnp.concatenate(
            [
                jnp.concatenate(
                    [x_ref[:, i, q * 2 + side].reshape(NBLOCKS, LANES) for side in range(2)], axis=1
                )
                for q in range(2)
            ],
            axis=0,
        )
        first = dot_three(forward, halves_of(values))
        real, imag = first[:NBLOCKS], first[NBLOCKS:]
        turned.append(
            jnp.concatenate([real * cosine + imag * sine, imag * cosine - real * sine], axis=1)
        )
    second = dot_three(halves_of(jnp.concatenate(turned, axis=0)), backward)
    factor = weight_ref[...] * (LOSS_SCALE / CHANNELS)
    factor = jnp.concatenate([jnp.concatenate([factor, factor], axis=1)] * count, axis=0)
    third = dot_three(halves_of(second * factor), forward)
    for i in range(count):
        part = third[i * NBLOCKS : (i + 1) * NBLOCKS]
        real, imag = part[:, :BLOCK], part[:, BLOCK:]
        back = jnp.concatenate([real * cosine - imag * sine, imag * cosine + real * sine], axis=0)
        fourth = dot_three(backward, halves_of(back))
        for q in range(2):
            for member in range(members):
                start = q * NBLOCKS + member * local
                for out_ref, size in zip(outs, pieces):
                    for side in range(2):
                        out_ref[member, i, q * 2 + side] = fourth[
                            start : start + size, side * LANES : (side + 1) * LANES
                        ]
                    start += size


def delay_filter(pieces, arrived, constants, weight, count=4):
    members, rows, _, local, _ = arrived.shape
    whole = lambda array: pl.BlockSpec(array.shape, lambda g: (0, 0))
    flops = rows * 4 * 3 * 2 * 512 * 512 * 256
    return pl.pallas_call(
        functools.partial(delay_kernel, pieces),
        grid=(rows // count,),
        in_specs=[
            pl.BlockSpec((members, count, PLANES, local, LANES), lambda g: (0, g, 0, 0, 0)),
            *[whole(array) for array in constants],
            whole(weight),
        ],
        out_specs=[
            pl.BlockSpec((members, count, PLANES, size, LANES), lambda g: (0, g, 0, 0, 0))
            for size in pieces
        ],
        out_shape=[
            jax.ShapeDtypeStruct((members, rows, PLANES, size, LANES), F32) for size in pieces
        ],
        compiler_params=params(),
        cost_estimate=pl.CostEstimate(flops=flops, bytes_accessed=12 * 2**20, transcendentals=0),
        name=f"delay_{len(pieces)}",
    )(arrived, *constants, weight)


def tail_kernel(first, g1_ref, g2_ref, hidden_ref, w_ref, keep_ref, taper_ref, before_ref,
                mine_ref, other_ref, hidden_grad_ref, weight_ref):
    step = pl.program_id(0)
    flats = [
        (ref.shape[0], ref.reshape(ref.shape[0] * 2 * STEP, LANES)) for ref in (g1_ref, g2_ref)
    ]

    @pl.when(pl.program_id(1) == 0)
    def _():
        weight_ref[...] = weight_of(keep_ref[...], taper_ref[...], (first + step) * STEP)

    @pl.when((step == 0) & (pl.program_id(1) == 0))
    def _():
        hidden_grad_ref[...] = before_ref[...]

    values = jnp.concatenate(
        [
            jnp.concatenate(
                [
                    flat[pl.ds(side * STEP + b, rows, stride=2 * STEP), :]
                    for b in range(STEP)
                    for side in range(2)
                ],
                axis=1,
            )
            for rows, flat in flats
        ],
        axis=0,
    )
    grad_field = (values * weight_ref[...]).astype(BF16)
    grad_out = dot(hidden_ref[...], grad_field)
    units = grad_out.shape[0] // 2
    for d in range(4):
        mine_ref[d, 0] = grad_out[d * 8 : (d + 1) * 8]
        other_ref[d, 0] = grad_out[units + d * 8 : units + (d + 1) * 8]
    hidden_grad_ref[...] += dot(w_ref[0], grad_field, NT)


def tail_part(first, count, g1, g2, hidden_order, w, keep, taper, before):
    units, total_rows = hidden_order.shape
    return pl.pallas_call(
        functools.partial(tail_kernel, first),
        grid=(count, 2),
        in_specs=[
            pl.BlockSpec((g1.shape[0], 2, STEP, LANES), lambda g, q: (0, q, first + g, 0)),
            pl.BlockSpec((g2.shape[0], 2, STEP, LANES), lambda g, q: (0, q, g, 0)),
            pl.BlockSpec((units, total_rows), lambda g, q: (0, 0)),
            pl.BlockSpec((1, units, WIDE), lambda g, q: (q, 0, first + g)),
            pl.BlockSpec(keep.shape, lambda g, q: (0, 0)),
            pl.BlockSpec((1, WIDE), lambda g, q: (0, first + g)),
            pl.BlockSpec((units, total_rows), lambda g, q: (0, 0)),
        ],
        out_specs=[
            pl.BlockSpec((4, 1, 8, WIDE), lambda g, q: (0, q, 0, g)),
            pl.BlockSpec((4, 1, 8, WIDE), lambda g, q: (0, q, 0, g)),
            pl.BlockSpec((units, total_rows), lambda g, q: (0, 0)),
        ],
        out_shape=[
            jax.ShapeDtypeStruct((4, 2, 8, count * WIDE), F32),
            jax.ShapeDtypeStruct((4, 2, 8, count * WIDE), F32),
            jax.ShapeDtypeStruct((units, total_rows), F32),
        ],
        scratch_shapes=[pltpu.VMEM((total_rows, WIDE), F32)],
        compiler_params=params(),
        cost_estimate=pl.CostEstimate(
            flops=count * 2 * 2 * 2 * 64 * 128 * WIDE, bytes_accessed=count * 4 * 2**20, transcendentals=0
        ),
        name=f"tail_{first}",
    )(g1, g2, hidden_order, w, keep, taper, before)


def terms_of(values, count):
    out = []
    for _ in range(count):
        term = values.astype(BF16)
        out.append(term)
        values = values - term.astype(F32)
    return out


def member_blocks(count):
    apart = [lax.axis_index("bl") ^ m for m in range(count)]
    return [(a // 4, a % 4) for a in apart]


def rows_kernel(index_ref, table_ref, features_ref, w_in_ref, inputs_ref, slope_ref, cells_ref):
    spots = member_blocks(index_ref.shape[0] * index_ref.shape[1])
    cells = jnp.concatenate([index_ref[f, n] for f, n in spots], axis=1).astype(jnp.int32)
    cells_ref[...] = cells
    summed = []
    for which, ref in ((0, table_ref), (1, features_ref)):
        total = 0.0
        for start in range(0, ref.shape[1], 512):
            size = min(512, ref.shape[1] - start)
            picked = one_hot_rows(cells[which : which + 1] - start, size)
            total = total + dot(ref[:, start : start + size], picked)
        summed.append(total)
    inputs = (summed[0] + summed[1]).astype(BF16)
    inputs_ref[...] = inputs
    pre_act = dot(w_in_ref[...], inputs, TN)
    sigmoid = 1.0 / (1.0 + jnp.exp(-pre_act))
    slope_ref[...] = sigmoid * (1.0 + pre_act * (1.0 - sigmoid))


def all_rows(index, uvw_table, baseline_features, w_in):
    rows = index.shape[0] * index.shape[1] * index.shape[3]
    return pl.pallas_call(
        rows_kernel,
        out_shape=[
            jax.ShapeDtypeStruct((w_in.shape[0], rows), BF16),
            jax.ShapeDtypeStruct((w_in.shape[1], rows), F32),
            jax.ShapeDtypeStruct((index.shape[2], rows), jnp.int32),
        ],
        compiler_params=params(),
        cost_estimate=pl.CostEstimate(flops=6 * 10**9, bytes_accessed=2**20, transcendentals=0),
        name="all_rows",
    )(index, uvw_table, baseline_features, w_in)


def scatter_kernel(own_ref, one_ref, two_ref, three_ref, inputs_ref, slope_ref, cells_ref, w_in_ref,
                   grad_in_ref, grad_uvw_ref, grad_base_ref):
    units = w_in_ref.shape[0]
    blocks = []
    for far, n in member_blocks(16):
        block = own_ref[n]
        for k, ref in ((1, one_ref), (2, two_ref), (3, three_ref)):
            block = jnp.where(far == k, ref[n], block)
        blocks.append(block)
    pre_grad = jnp.concatenate(blocks, axis=1) * slope_ref[...]
    grad_terms = jnp.concatenate(terms_of(pre_grad, 2), axis=0)
    parts = dot(inputs_ref[...], grad_terms, NT)
    grad_in_ref[...] = parts[:, :units] + parts[:, units:]
    input_grad = dot(w_in_ref[...], grad_terms[:units]) + dot(w_in_ref[...], grad_terms[units:])
    terms = jnp.concatenate(terms_of(input_grad, 2), axis=0)
    for which, out_ref in ((0, grad_uvw_ref), (1, grad_base_ref)):
        index = cells_ref[which : which + 1, :]
        cells = out_ref.shape[1]
        half = -(-cells // 2 // LANES) * LANES
        upper = index >= half
        index = jnp.where(upper, index - half, index)
        zero = jnp.zeros_like(terms)
        sides = jnp.concatenate(
            [jnp.where(upper, zero, terms), jnp.where(upper, terms, zero)], axis=0
        )
        for start in range(0, half, 512):
            size = min(512, half - start)
            sums = dot(one_hot_rows(index - start, size), sides, NT).T
            for side in range(2):
                first = side * half + start
                wide = min(size, cells - first)
                part = sums[side * 2 * units : (side + 1) * 2 * units, :wide]
                out_ref[:, first : first + wide] = part[:units] + part[units:]


def scatter(blocks, known, w_in, cells, baselines):
    return pl.pallas_call(
        scatter_kernel,
        out_shape=[
            jax.ShapeDtypeStruct(w_in.shape, F32),
            jax.ShapeDtypeStruct((w_in.shape[0], cells), F32),
            jax.ShapeDtypeStruct((w_in.shape[0], baselines), F32),
        ],
        compiler_params=params(32 * 2**20),
        cost_estimate=pl.CostEstimate(
            flops=6 * 10**9, bytes_accessed=4 * 2**20, transcendentals=0
        ),
        name="scatter",
    )(*blocks, *known, w_in)


def swap(values, axis, distance):
    size = lax.axis_size(axis)
    return lax.ppermute(values, axis, [(i, i ^ distance) for i in range(size)])


def met(values, axis, distances):
    return [values, *[swap(values, axis, distance) for distance in distances]]


def sum_over_ch(values, *others):
    a, b, c, d = met(values, "ch", (2, 4, 6))
    total = after((a + b) + (c + d), *others)
    return total + swap(total, "ch", 1)


def sum_cores(mine, other, parts):
    return mine + swap(other, "bl", 1)


def sum_far(both):
    ring = lambda d: [(i, (i + 4 * d) % 16) for i in range(16)]
    got = [lax.ppermute(both[d], "bl", ring(d)) for d in (1, 2, 3)]
    return both[0] + got[0] + got[1] + got[2]


def sum_near(total):
    return total[:, :4] + swap(total[:, 4:], "bl", 2)


def together(*values):
    return lax.optimization_barrier(values)


def after(value, *others):
    return lax.optimization_barrier((value, *others))[0]


def body(
    uvw_index, row_baseline, flags, uvw_table, baseline_features, w_in, w_out, observed, delay_weight
):
    members = lax.axis_size("ch")
    rows = uvw_index.shape[0]
    local_blocks = flags.shape[1]
    local_channels = w_out.shape[2]
    head_rows = rows * 4 // 16

    taper = jnp.asarray(taper_table()).reshape(members, local_channels)
    hidden, hidden_t, keep, taper = trunk(
        uvw_index, row_baseline, flags, uvw_table, baseline_features, w_in, taper
    )
    constants = [jnp.asarray(table) for table in tables()]
    weight = delay_weight.reshape(BLOCK, NBLOCKS).T

    def exchange(values):
        size = values.shape[-2]
        return lax.all_to_all(
            values.reshape(members, -1, PLANES, size, LANES), "ch", 0, 0, tiled=True
        )

    def arrive(part):
        return exchange(part).reshape(-1, PLANES, part.shape[-2], LANES)

    part = residual_part(0, head_rows, hidden_t, w_out, observed, keep, taper)
    hidden_t = after(hidden_t, part)
    index = jnp.stack([uvw_index, row_baseline]).astype(F32)
    index = jnp.concatenate([index, jnp.zeros((6, rows), F32)], axis=0)
    index = jnp.stack([index, swap(index, "bl", 2)])
    sent_0 = exchange(after(part, index))
    index = after(index, part)
    across = swap(index, "bl", 1)
    index = jnp.stack([index[0], across[0], index[1], across[1]])
    index = jnp.stack(met(index, "bl", (4, 8, 12)))
    part = residual_part(head_rows, rows - head_rows, hidden_t, w_out, observed, keep, taper)
    sent_1 = exchange(after(part, index))

    me = lax.axis_index("bl")
    order = lax.broadcasted_iota(jnp.int32, hidden.shape[:1], 0)
    core, x_far, y_far, unit = order // 32, (order // 8) % 4, (order // 4) % 2, order % 4
    owner = ((me // 4 + x_far) % 4) * 4 + ((me // 2) % 2 ^ y_far) * 2 + (me % 2 ^ core)
    units = lax.broadcasted_iota(jnp.int32, (hidden.shape[0],) * 2, 1)
    turn = (units == (owner * 4 + unit)[:, None]).astype(BF16)
    hidden_order = dot(turn, hidden).astype(BF16)
    w = w_out.transpose(1, 0, 2)

    (part,) = delay_filter((local_blocks,), sent_0, constants, weight)
    known = all_rows(after(index, part), uvw_table, baseline_features, w_in)
    part = after(part, hidden_order, w, *known)
    back_0 = arrive(part)
    sizes = (local_blocks * 16 // 32, local_blocks * 16 // 32)
    counts = [size // STEP for size in sizes]
    parts = delay_filter(sizes, after(sent_1, part), constants, weight)

    piece = arrive(after(parts[0], back_0))
    late = after(parts[1], piece)
    mine, other, hidden_grad = tail_part(
        0, counts[0], back_0, piece, hidden_order, w, keep, taper, jnp.zeros(hidden.shape, F32)
    )
    both = sum_cores(mine, other, 1)
    piece = after(arrive(late), both)
    first = sum_far(both)
    mine, other, hidden_grad = tail_part(
        counts[0], counts[1], back_0, piece, hidden_order, w, keep, taper, hidden_grad
    )
    both = sum_cores(mine, other, 1)
    hidden_grad = sum_over_ch(hidden_grad, both, first)
    second = sum_far(both)
    near = after(jnp.stack(met(hidden_grad, "bl", (1, 2, 3))), second)
    blocks = met(near, "bl", (4, 8, 12))
    grad_out = sum_near(jnp.concatenate([first, second], axis=2)).transpose(1, 0, 2)
    grad_in, grad_uvw, grad_base = scatter(
        blocks, known, w_in, uvw_table.shape[1], baseline_features.shape[1]
    )
    return (grad_out, grad_in, grad_uvw, grad_base)


def solution(mesh):
    return jax.shard_map(
        body,
        mesh=mesh,
        in_specs=(
            P("bl"),
            P("bl"),
            P("bl", "ch"),
            P(),
            P(),
            P(),
            P(None, None, "ch"),
            P(None, "ch", "bl"),
            P(),
        ),
        out_specs=(P("bl", None, "ch"), P(), P(), P()),
        check_vma=False,
    )
```

```python
import functools
import math

import jax
import jax.numpy as jnp
import ml_dtypes
import numpy as np
from jax import lax
from jax.experimental import pallas as pl
from jax.experimental.pallas import tpu as pltpu
from jax.sharding import PartitionSpec as P

BLOCK = 256
NBLOCKS = 256
CHANNELS = 65536
LOSS_SCALE = 0.0625
HIGHEST = lax.Precision.HIGHEST
F32 = jnp.float32
BF16 = jnp.bfloat16
STEP = 8
WIDE = STEP * BLOCK
LANES = 128
PLANES = 4
VMEM = 63 * 2**20


def split_matrix(matrix):
    high = matrix.astype(ml_dtypes.bfloat16)
    low = (matrix - high.astype(np.float64)).astype(ml_dtypes.bfloat16)
    return high, low


def tables():
    n = np.arange(BLOCK)
    product = np.outer(n, n)
    cosine = np.cos(2 * math.pi * (product % BLOCK) / BLOCK)
    sine = np.sin(2 * math.pi * (product % BLOCK) / BLOCK)
    forward = np.block([[cosine, sine], [-sine, cosine]])
    backward = np.block([[cosine, -sine], [sine, cosine]])
    twiddle = 2 * math.pi * product / CHANNELS
    return (
        *split_matrix(forward),
        *split_matrix(backward),
        np.cos(twiddle).astype(np.float32),
        np.sin(twiddle).astype(np.float32),
    )


def taper_table():
    c = np.arange(CHANNELS)
    window = np.full((CHANNELS,), 0.35875)
    for harmonic, term in ((1, -0.48829), (2, 0.14128), (3, -0.01168)):
        window = window + term * np.cos(2 * math.pi * ((c * harmonic) % CHANNELS) / CHANNELS)
    return window.astype(np.float32)


def dot(a, b, dims=(((1,), (0,)), ((), ())), precision=None):
    return lax.dot_general(a, b, dims, precision=precision, preferred_element_type=F32)


NT = (((1,), (1,)), ((), ()))
TN = (((0,), (0,)), ((), ()))


def params(vmem=VMEM):
    return pltpu.CompilerParams(vmem_limit_bytes=vmem)


def one_hot_rows(index_row, count):
    cells = lax.broadcasted_iota(jnp.int32, (count, index_row.shape[1]), 0)
    return jnp.where(cells == index_row, 1.0, 0.0).astype(BF16)


def trunk_kernel(uvw_ref, base_ref, flags_ref, table_ref, features_ref, w_in_ref, taper_ref,
                 hidden_ref, hidden_t_ref, keep_ref, taper_here_ref, index_ref):
    pair = jnp.concatenate([uvw_ref[...], base_ref[...]], axis=0).astype(F32)
    index_ref[...] = jnp.concatenate([pair] * 4, axis=0)
    taper_here_ref[...] = taper_ref[pl.ds(lax.axis_index("ch"), 1), :]
    summed = dot(table_ref[...], one_hot_rows(uvw_ref[...], table_ref.shape[1]))
    summed = summed + dot(features_ref[...], one_hot_rows(base_ref[...], features_ref.shape[1]))
    inputs = summed.astype(BF16)
    pre_act = dot(w_in_ref[...], inputs, TN)
    hidden = pre_act / (1.0 + jnp.exp(-pre_act))
    hidden_ref[...] = hidden.astype(BF16)
    hidden_t_ref[...] = hidden.T.astype(BF16)
    keep_ref[...] = (1.0 - flags_ref[...].astype(F32)).T.astype(BF16)


def trunk(uvw_index, row_baseline, flags, uvw_table, baseline_features, w_in, taper):
    rows = uvw_index.shape[0]
    units = w_in.shape[1]
    return pl.pallas_call(
        trunk_kernel,
        out_shape=(
            jax.ShapeDtypeStruct((units, rows), BF16),
            jax.ShapeDtypeStruct((rows, units), BF16),
            jax.ShapeDtypeStruct(flags.shape, BF16),
            jax.ShapeDtypeStruct((1, taper.shape[1]), F32),
            jax.ShapeDtypeStruct((8, rows), F32),
        ),
        compiler_params=params(),
        name="trunk",
    )(uvw_index[None], row_baseline[None], flags.T, uvw_table, baseline_features, w_in, taper)


def weight_of(keep, taper_row, first_block):
    blocks = keep.shape[1]
    block = lax.broadcasted_iota(jnp.int32, (blocks, WIDE), 0)
    lane = lax.broadcasted_iota(jnp.int32, (blocks, WIDE), 1)
    expand = jnp.where(block == first_block + (lane >> 8), 1.0, 0.0).astype(BF16)
    return dot(keep, expand) * taper_row


def residual_kernel(first_row, rows, hidden_ref, w_ref, observed_ref, keep_ref, taper_ref, out_ref):
    total = observed_ref.shape[2]
    own_rows = slice(first_row, first_row + rows)
    weight = weight_of(keep_ref[own_rows], taper_ref[...], pl.program_id(0) * STEP)
    row = lax.broadcasted_iota(jnp.int32, (rows, total), 0)
    column = lax.broadcasted_iota(jnp.int32, (rows, total), 1)
    pick = jnp.where(column == row + first_row, -1.0, 0.0).astype(BF16)
    flat = out_ref.reshape(rows * PLANES * STEP, LANES)
    units = w_ref.shape[0]
    pairs = w_ref[...].reshape(2 * units, WIDE)
    unit = lax.broadcasted_iota(jnp.int32, (units, 2 * units), 0)
    place = lax.broadcasted_iota(jnp.int32, (units, 2 * units), 1)
    spread = jnp.concatenate(
        [jnp.where(place == unit * 2 + q, 1.0, 0.0).astype(BF16) for q in range(2)], axis=1
    )
    own = dot(hidden_ref[own_rows], spread).astype(BF16)
    fields = dot(jnp.concatenate([own[:, : 2 * units], own[:, 2 * units :]], axis=0), pairs)
    for q in range(2):
        residual = fields[q * rows : (q + 1) * rows] + dot(pick, observed_ref[q], NT)
        residual = residual * weight
        for b in range(STEP):
            for side in range(2):
                start = b * BLOCK + side * LANES
                flat[pl.ds((q * 2 + side) * STEP + b, rows, stride=PLANES * STEP), :] = residual[
                    :, start : start + LANES
                ]


def residual_part(first_row, rows, hidden_t, w, observed, keep, taper):
    blocks = keep.shape[1]
    return pl.pallas_call(
        functools.partial(residual_kernel, first_row, rows),
        grid=(blocks // STEP,),
        in_specs=[
            pl.BlockSpec(hidden_t.shape, lambda g: (0, 0)),
            pl.BlockSpec((w.shape[0], 2, WIDE), lambda g: (0, 0, g)),
            pl.BlockSpec((2, WIDE, observed.shape[2]), lambda g: (0, g, 0)),
            pl.BlockSpec(keep.shape, lambda g: (0, 0)),
            pl.BlockSpec((1, WIDE), lambda g: (0, g)),
        ],
        out_specs=pl.BlockSpec((rows, PLANES, STEP, LANES), lambda g: (0, 0, g, 0)),
        out_shape=jax.ShapeDtypeStruct((rows, PLANES, blocks, LANES), F32),
        compiler_params=params(),
        cost_estimate=pl.CostEstimate(
            flops=2 * rows * 2 * blocks * BLOCK * 192, bytes_accessed=10 * 2**20, transcendentals=0
        ),
        name=f"residual_{first_row}",
    )(hidden_t, w, observed, keep, taper)


def halves_of(values):
    high = values.astype(BF16)
    return high, (values - high.astype(F32)).astype(BF16)


def dot_three(a, b):
    return dot(a[0], b[0]) + (dot(a[0], b[1]) + dot(a[1], b[0]))


def delay_kernel(pieces, x_ref, fh_ref, fl_ref, bh_ref, bl_ref, cos_ref, sin_ref, weight_ref, *outs):
    forward = (fh_ref[...], fl_ref[...])
    backward = (bh_ref[...], bl_ref[...])
    cosine, sine = cos_ref[...], sin_ref[...]
    count = x_ref.shape[1]
    members, local = x_ref.shape[0], x_ref.shape[3]
    turned = []
    for i in range(count):
        values = jnp.concatenate(
            [
                jnp.concatenate(
                    [x_ref[:, i, q * 2 + side].reshape(NBLOCKS, LANES) for side in range(2)], axis=1
                )
                for q in range(2)
            ],
            axis=0,
        )
        first = dot_three(forward, halves_of(values))
        real, imag = first[:NBLOCKS], first[NBLOCKS:]
        turned.append(
            jnp.concatenate([real * cosine + imag * sine, imag * cosine - real * sine], axis=1)
        )
    second = dot_three(halves_of(jnp.concatenate(turned, axis=0)), backward)
    factor = weight_ref[...] * (LOSS_SCALE / CHANNELS)
    factor = jnp.concatenate([jnp.concatenate([factor, factor], axis=1)] * count, axis=0)
    third = dot_three(halves_of(second * factor), forward)
    for i in range(count):
        part = third[i * NBLOCKS : (i + 1) * NBLOCKS]
        real, imag = part[:, :BLOCK], part[:, BLOCK:]
        back = jnp.concatenate([real * cosine - imag * sine, imag * cosine + real * sine], axis=0)
        fourth = dot_three(backward, halves_of(back))
        for q in range(2):
            for member in range(members):
                start = q * NBLOCKS + member * local
                for out_ref, size in zip(outs, pieces):
                    for side in range(2):
                        out_ref[member, i, q * 2 + side] = fourth[
                            start : start + size, side * LANES : (side + 1) * LANES
                        ]
                    start += size


def delay_filter(pieces, arrived, constants, weight, count=4):
    members, rows, _, local, _ = arrived.shape
    whole = lambda array: pl.BlockSpec(array.shape, lambda g: (0, 0))
    flops = rows * 4 * 3 * 2 * 512 * 512 * 256
    return pl.pallas_call(
        functools.partial(delay_kernel, pieces),
        grid=(rows // count,),
        in_specs=[
            pl.BlockSpec((members, count, PLANES, local, LANES), lambda g: (0, g, 0, 0, 0)),
            *[whole(array) for array in constants],
            whole(weight),
        ],
        out_specs=[
            pl.BlockSpec((members, count, PLANES, size, LANES), lambda g: (0, g, 0, 0, 0))
            for size in pieces
        ],
        out_shape=[
            jax.ShapeDtypeStruct((members, rows, PLANES, size, LANES), F32) for size in pieces
        ],
        compiler_params=params(),
        cost_estimate=pl.CostEstimate(flops=flops, bytes_accessed=12 * 2**20, transcendentals=0),
        name=f"delay_{len(pieces)}",
    )(arrived, *constants, weight)


def tail_kernel(first, g1_ref, g2_ref, hidden_ref, w_ref, keep_ref, taper_ref, before_ref,
                mine_ref, other_ref, hidden_grad_ref, weight_ref):
    step = pl.program_id(0)
    flats = [
        (ref.shape[0], ref.reshape(ref.shape[0] * 2 * STEP, LANES)) for ref in (g1_ref, g2_ref)
    ]

    @pl.when(pl.program_id(1) == 0)
    def _():
        weight_ref[...] = weight_of(keep_ref[...], taper_ref[...], (first + step) * STEP)

    @pl.when((step == 0) & (pl.program_id(1) == 0))
    def _():
        hidden_grad_ref[...] = before_ref[...]

    values = jnp.concatenate(
        [
            jnp.concatenate(
                [
                    flat[pl.ds(side * STEP + b, rows, stride=2 * STEP), :]
                    for b in range(STEP)
                    for side in range(2)
                ],
                axis=1,
            )
            for rows, flat in flats
        ],
        axis=0,
    )
    grad_field = (values * weight_ref[...]).astype(BF16)
    grad_out = dot(hidden_ref[...], grad_field)
    units = grad_out.shape[0] // 2
    for d in range(4):
        mine_ref[d, 0] = grad_out[d * 8 : (d + 1) * 8]
        other_ref[d, 0] = grad_out[units + d * 8 : units + (d + 1) * 8]
    hidden_grad_ref[...] += dot(w_ref[0], grad_field, NT)


def tail_part(first, count, g1, g2, hidden_order, w, keep, taper, before):
    units, total_rows = hidden_order.shape
    return pl.pallas_call(
        functools.partial(tail_kernel, first),
        grid=(count, 2),
        in_specs=[
            pl.BlockSpec((g1.shape[0], 2, STEP, LANES), lambda g, q: (0, q, first + g, 0)),
            pl.BlockSpec((g2.shape[0], 2, STEP, LANES), lambda g, q: (0, q, g, 0)),
            pl.BlockSpec((units, total_rows), lambda g, q: (0, 0)),
            pl.BlockSpec((1, units, WIDE), lambda g, q: (q, 0, first + g)),
            pl.BlockSpec(keep.shape, lambda g, q: (0, 0)),
            pl.BlockSpec((1, WIDE), lambda g, q: (0, first + g)),
            pl.BlockSpec((units, total_rows), lambda g, q: (0, 0)),
        ],
        out_specs=[
            pl.BlockSpec((4, 1, 8, WIDE), lambda g, q: (0, q, 0, g)),
            pl.BlockSpec((4, 1, 8, WIDE), lambda g, q: (0, q, 0, g)),
            pl.BlockSpec((units, total_rows), lambda g, q: (0, 0)),
        ],
        out_shape=[
            jax.ShapeDtypeStruct((4, 2, 8, count * WIDE), F32),
            jax.ShapeDtypeStruct((4, 2, 8, count * WIDE), F32),
            jax.ShapeDtypeStruct((units, total_rows), F32),
        ],
        scratch_shapes=[pltpu.VMEM((total_rows, WIDE), F32)],
        compiler_params=params(),
        cost_estimate=pl.CostEstimate(
            flops=count * 2 * 2 * 2 * 64 * 128 * WIDE, bytes_accessed=count * 4 * 2**20, transcendentals=0
        ),
        name=f"tail_{first}",
    )(g1, g2, hidden_order, w, keep, taper, before)


def terms_of(values, count):
    out = []
    for _ in range(count):
        term = values.astype(BF16)
        out.append(term)
        values = values - term.astype(F32)
    return out


def member_blocks(count):
    apart = [lax.axis_index("bl") ^ m for m in range(count)]
    return [(a // 4, a % 4) for a in apart]


def rows_kernel(index_ref, table_ref, features_ref, w_in_ref, inputs_ref, slope_ref, cells_ref):
    spots = member_blocks(index_ref.shape[0] * index_ref.shape[1])
    cells = jnp.concatenate([index_ref[f, n] for f, n in spots], axis=1).astype(jnp.int32)
    cells_ref[...] = cells
    summed = []
    for which, ref in ((0, table_ref), (1, features_ref)):
        total = 0.0
        for start in range(0, ref.shape[1], 512):
            size = min(512, ref.shape[1] - start)
            picked = one_hot_rows(cells[which : which + 1] - start, size)
            total = total + dot(ref[:, start : start + size], picked)
        summed.append(total)
    inputs = (summed[0] + summed[1]).astype(BF16)
    inputs_ref[...] = inputs
    pre_act = dot(w_in_ref[...], inputs, TN)
    sigmoid = 1.0 / (1.0 + jnp.exp(-pre_act))
    slope_ref[...] = sigmoid * (1.0 + pre_act * (1.0 - sigmoid))


def all_rows(index, uvw_table, baseline_features, w_in):
    rows = index.shape[0] * index.shape[1] * index.shape[3]
    return pl.pallas_call(
        rows_kernel,
        out_shape=[
            jax.ShapeDtypeStruct((w_in.shape[0], rows), BF16),
            jax.ShapeDtypeStruct((w_in.shape[1], rows), F32),
            jax.ShapeDtypeStruct((index.shape[2], rows), jnp.int32),
        ],
        compiler_params=params(),
        cost_estimate=pl.CostEstimate(flops=6 * 10**9, bytes_accessed=2**20, transcendentals=0),
        name="all_rows",
    )(index, uvw_table, baseline_features, w_in)


def scatter_kernel(own_ref, one_ref, two_ref, three_ref, inputs_ref, slope_ref, cells_ref, w_in_ref,
                   grad_in_ref, grad_uvw_ref, grad_base_ref):
    units = w_in_ref.shape[0]
    blocks = []
    for far, n in member_blocks(16):
        block = own_ref[n]
        for k, ref in ((1, one_ref), (2, two_ref), (3, three_ref)):
            block = jnp.where(far == k, ref[n], block)
        blocks.append(block)
    pre_grad = jnp.concatenate(blocks, axis=1) * slope_ref[...]
    grad_terms = jnp.concatenate(terms_of(pre_grad, 2), axis=0)
    parts = dot(inputs_ref[...], grad_terms, NT)
    grad_in_ref[...] = parts[:, :units] + parts[:, units:]
    input_grad = dot(w_in_ref[...], grad_terms[:units]) + dot(w_in_ref[...], grad_terms[units:])
    terms = jnp.concatenate(terms_of(input_grad, 2), axis=0)
    for which, out_ref in ((0, grad_uvw_ref), (1, grad_base_ref)):
        index = cells_ref[which : which + 1, :]
        cells = out_ref.shape[1]
        half = -(-cells // 2 // LANES) * LANES
        upper = index >= half
        index = jnp.where(upper, index - half, index)
        zero = jnp.zeros_like(terms)
        sides = jnp.concatenate(
            [jnp.where(upper, zero, terms), jnp.where(upper, terms, zero)], axis=0
        )
        for start in range(0, half, 512):
            size = min(512, half - start)
            sums = dot(one_hot_rows(index - start, size), sides, NT).T
            for side in range(2):
                first = side * half + start
                wide = min(size, cells - first)
                part = sums[side * 2 * units : (side + 1) * 2 * units, :wide]
                out_ref[:, first : first + wide] = part[:units] + part[units:]


def scatter(blocks, known, w_in, cells, baselines):
    return pl.pallas_call(
        scatter_kernel,
        out_shape=[
            jax.ShapeDtypeStruct(w_in.shape, F32),
            jax.ShapeDtypeStruct((w_in.shape[0], cells), F32),
            jax.ShapeDtypeStruct((w_in.shape[0], baselines), F32),
        ],
        compiler_params=params(32 * 2**20),
        cost_estimate=pl.CostEstimate(
            flops=6 * 10**9, bytes_accessed=4 * 2**20, transcendentals=0
        ),
        name="scatter",
    )(*blocks, *known, w_in)


def swap(values, axis, distance):
    size = lax.axis_size(axis)
    return lax.ppermute(values, axis, [(i, i ^ distance) for i in range(size)])


def met(values, axis, distances):
    return [values, *[swap(values, axis, distance) for distance in distances]]


def sum_over_ch(values, *others):
    a, b, c, d = met(values, "ch", (2, 4, 6))
    total = after((a + b) + (c + d), *others)
    return total + swap(total, "ch", 1)


def sum_cores(mine, other, parts):
    return mine + swap(other, "bl", 1)


def sum_far(both):
    ring = lambda d: [(i, (i + 4 * d) % 16) for i in range(16)]
    got = [lax.ppermute(both[d], "bl", ring(d)) for d in (1, 2, 3)]
    return both[0] + got[0] + got[1] + got[2]


def sum_near(total):
    return total[:, :4] + swap(total[:, 4:], "bl", 2)


def together(*values):
    return lax.optimization_barrier(values)


def after(value, *others):
    return lax.optimization_barrier((value, *others))[0]


def body(
    uvw_index, row_baseline, flags, uvw_table, baseline_features, w_in, w_out, observed, delay_weight
):
    members = lax.axis_size("ch")
    rows = uvw_index.shape[0]
    local_blocks = flags.shape[1]
    local_channels = w_out.shape[2]
    head_rows = rows * 4 // 16

    taper = jnp.asarray(taper_table()).reshape(members, local_channels)
    hidden, hidden_t, keep, taper, index = trunk(
        uvw_index, row_baseline, flags, uvw_table, baseline_features, w_in, taper
    )
    constants = [jnp.asarray(table) for table in tables()]
    weight = delay_weight.reshape(BLOCK, NBLOCKS).T

    def exchange(values):
        size = values.shape[-2]
        return lax.all_to_all(
            values.reshape(members, -1, PLANES, size, LANES), "ch", 0, 0, tiled=True
        )

    def arrive(part):
        return exchange(part).reshape(-1, PLANES, part.shape[-2], LANES)

    part = residual_part(0, head_rows, hidden_t, w_out, observed, keep, taper)
    hidden_t = after(hidden_t, part)
    index = jnp.stack([index, swap(index, "bl", 2)])
    sent_0 = exchange(after(part, index))
    index = after(index, part)
    across = swap(index, "bl", 1)
    index = jnp.stack([index[0], across[0], index[1], across[1]])
    index = jnp.stack(met(index, "bl", (4, 8, 12)))
    part = residual_part(head_rows, rows - head_rows, hidden_t, w_out, observed, keep, taper)
    sent_1 = exchange(after(part, index))

    me = lax.axis_index("bl")
    order = lax.broadcasted_iota(jnp.int32, hidden.shape[:1], 0)
    core, x_far, y_far, unit = order // 32, (order // 8) % 4, (order // 4) % 2, order % 4
    owner = ((me // 4 + x_far) % 4) * 4 + ((me // 2) % 2 ^ y_far) * 2 + (me % 2 ^ core)
    units = lax.broadcasted_iota(jnp.int32, (hidden.shape[0],) * 2, 1)
    turn = (units == (owner * 4 + unit)[:, None]).astype(BF16)
    hidden_order = dot(turn, hidden).astype(BF16)
    w = w_out.transpose(1, 0, 2)

    (part,) = delay_filter((local_blocks,), sent_0, constants, weight)
    known = all_rows(after(index, part), uvw_table, baseline_features, w_in)
    part = after(part, hidden_order, w, *known)
    back_0 = arrive(part)
    sizes = (local_blocks * 16 // 32, local_blocks * 16 // 32)
    counts = [size // STEP for size in sizes]
    parts = delay_filter(sizes, after(sent_1, part), constants, weight)

    piece = arrive(after(parts[0], back_0))
    late = after(parts[1], piece)
    mine, other, hidden_grad = tail_part(
        0, counts[0], back_0, piece, hidden_order, w, keep, taper, jnp.zeros(hidden.shape, F32)
    )
    both = sum_cores(mine, other, 1)
    piece = after(arrive(late), both)
    first = sum_far(both)
    mine, other, hidden_grad = tail_part(
        counts[0], counts[1], back_0, piece, hidden_order, w, keep, taper, hidden_grad
    )
    both = sum_cores(mine, other, 1)
    hidden_grad = sum_over_ch(hidden_grad, both, first)
    second = sum_far(both)
    near = after(jnp.stack(met(hidden_grad, "bl", (1, 2, 3))), second)
    blocks = met(near, "bl", (4, 8, 12))
    grad_out = sum_near(jnp.concatenate([first, second], axis=2)).transpose(1, 0, 2)
    grad_in, grad_uvw, grad_base = scatter(
        blocks, known, w_in, uvw_table.shape[1], baseline_features.shape[1]
    )
    return (grad_out, grad_in, grad_uvw, grad_base)


def solution(mesh):
    return jax.shard_map(
        body,
        mesh=mesh,
        in_specs=(
            P("bl"),
            P("bl"),
            P("bl", "ch"),
            P(),
            P(),
            P(),
            P(None, None, "ch"),
            P(None, "ch", "bl"),
            P(),
        ),
        out_specs=(P("bl", None, "ch"), P(), P(), P()),
        check_vma=False,
    )
```

```python
import functools
import math

import jax
import jax.numpy as jnp
import ml_dtypes
import numpy as np
from jax import lax
from jax.experimental import pallas as pl
from jax.experimental.pallas import tpu as pltpu
from jax.sharding import PartitionSpec as P

BLOCK = 256
NBLOCKS = 256
CHANNELS = 65536
LOSS_SCALE = 0.0625
HIGHEST = lax.Precision.HIGHEST
F32 = jnp.float32
BF16 = jnp.bfloat16
STEP = 8
WIDE = STEP * BLOCK
LANES = 128
PLANES = 4
VMEM = 63 * 2**20


def split_matrix(matrix):
    high = matrix.astype(ml_dtypes.bfloat16)
    low = (matrix - high.astype(np.float64)).astype(ml_dtypes.bfloat16)
    return high, low


def tables():
    n = np.arange(BLOCK)
    product = np.outer(n, n)
    cosine = np.cos(2 * math.pi * (product % BLOCK) / BLOCK)
    sine = np.sin(2 * math.pi * (product % BLOCK) / BLOCK)
    forward = np.block([[cosine, sine], [-sine, cosine]])
    backward = np.block([[cosine, -sine], [sine, cosine]])
    twiddle = 2 * math.pi * product / CHANNELS
    return (
        *split_matrix(forward),
        *split_matrix(backward),
        np.cos(twiddle).astype(np.float32),
        np.sin(twiddle).astype(np.float32),
    )


def taper_table():
    c = np.arange(CHANNELS)
    window = np.full((CHANNELS,), 0.35875)
    for harmonic, term in ((1, -0.48829), (2, 0.14128), (3, -0.01168)):
        window = window + term * np.cos(2 * math.pi * ((c * harmonic) % CHANNELS) / CHANNELS)
    return window.astype(np.float32)


def dot(a, b, dims=(((1,), (0,)), ((), ())), precision=None):
    return lax.dot_general(a, b, dims, precision=precision, preferred_element_type=F32)


NT = (((1,), (1,)), ((), ()))
TN = (((0,), (0,)), ((), ()))


def params(vmem=VMEM):
    return pltpu.CompilerParams(vmem_limit_bytes=vmem)


def one_hot_rows(index_row, count):
    cells = lax.broadcasted_iota(jnp.int32, (count, index_row.shape[1]), 0)
    return jnp.where(cells == index_row, 1.0, 0.0).astype(BF16)


def trunk_kernel(uvw_ref, base_ref, flags_ref, table_ref, features_ref, w_in_ref, taper_ref,
                 hidden_ref, hidden_t_ref, keep_ref, taper_here_ref):
    taper_here_ref[...] = taper_ref[pl.ds(lax.axis_index("ch"), 1), :]
    summed = dot(table_ref[...], one_hot_rows(uvw_ref[...], table_ref.shape[1]))
    summed = summed + dot(features_ref[...], one_hot_rows(base_ref[...], features_ref.shape[1]))
    inputs = summed.astype(BF16)
    pre_act = dot(w_in_ref[...], inputs, TN)
    hidden = pre_act / (1.0 + jnp.exp(-pre_act))
    hidden_ref[...] = hidden.astype(BF16)
    hidden_t_ref[...] = hidden.T.astype(BF16)
    keep_ref[...] = (1.0 - flags_ref[...].astype(F32)).T.astype(BF16)


def trunk(uvw_index, row_baseline, flags, uvw_table, baseline_features, w_in, taper):
    rows = uvw_index.shape[0]
    units = w_in.shape[1]
    return pl.pallas_call(
        trunk_kernel,
        out_shape=(
            jax.ShapeDtypeStruct((units, rows), BF16),
            jax.ShapeDtypeStruct((rows, units), BF16),
            jax.ShapeDtypeStruct(flags.shape, BF16),
            jax.ShapeDtypeStruct((1, taper.shape[1]), F32),
        ),
        compiler_params=params(),
        name="trunk",
    )(uvw_index[None], row_baseline[None], flags.T, uvw_table, baseline_features, w_in, taper)


def weight_of(keep, taper_row, first_block):
    blocks = keep.shape[1]
    block = lax.broadcasted_iota(jnp.int32, (blocks, WIDE), 0)
    lane = lax.broadcasted_iota(jnp.int32, (blocks, WIDE), 1)
    expand = jnp.where(block == first_block + (lane >> 8), 1.0, 0.0).astype(BF16)
    return dot(keep, expand) * taper_row


def residual_kernel(first_row, rows, hidden_ref, w_ref, observed_ref, keep_ref, taper_ref, out_ref):
    total = observed_ref.shape[2]
    own_rows = slice(first_row, first_row + rows)
    weight = weight_of(keep_ref[own_rows], taper_ref[...], pl.program_id(0) * STEP)
    row = lax.broadcasted_iota(jnp.int32, (rows, total), 0)
    column = lax.broadcasted_iota(jnp.int32, (rows, total), 1)
    pick = jnp.where(column == row + first_row, -1.0, 0.0).astype(BF16)
    flat = out_ref.reshape(rows * PLANES * STEP, LANES)
    units = w_ref.shape[0]
    pairs = w_ref[...].reshape(2 * units, WIDE)
    unit = lax.broadcasted_iota(jnp.int32, (units, 2 * units), 0)
    place = lax.broadcasted_iota(jnp.int32, (units, 2 * units), 1)
    spread = jnp.concatenate(
        [jnp.where(place == unit * 2 + q, 1.0, 0.0).astype(BF16) for q in range(2)], axis=1
    )
    own = dot(hidden_ref[own_rows], spread).astype(BF16)
    fields = dot(jnp.concatenate([own[:, : 2 * units], own[:, 2 * units :]], axis=0), pairs)
    for q in range(2):
        residual = fields[q * rows : (q + 1) * rows] + dot(pick, observed_ref[q], NT)
        residual = residual * weight
        for b in range(STEP):
            for side in range(2):
                start = b * BLOCK + side * LANES
                flat[pl.ds((q * 2 + side) * STEP + b, rows, stride=PLANES * STEP), :] = residual[
                    :, start : start + LANES
                ]


def residual_part(first_row, rows, hidden_t, w, observed, keep, taper):
    blocks = keep.shape[1]
    return pl.pallas_call(
        functools.partial(residual_kernel, first_row, rows),
        grid=(blocks // STEP,),
        in_specs=[
            pl.BlockSpec(hidden_t.shape, lambda g: (0, 0)),
            pl.BlockSpec((w.shape[0], 2, WIDE), lambda g: (0, 0, g)),
            pl.BlockSpec((2, WIDE, observed.shape[2]), lambda g: (0, g, 0)),
            pl.BlockSpec(keep.shape, lambda g: (0, 0)),
            pl.BlockSpec((1, WIDE), lambda g: (0, g)),
        ],
        out_specs=pl.BlockSpec((rows, PLANES, STEP, LANES), lambda g: (0, 0, g, 0)),
        out_shape=jax.ShapeDtypeStruct((rows, PLANES, blocks, LANES), F32),
        compiler_params=params(),
        cost_estimate=pl.CostEstimate(
            flops=2 * rows * 2 * blocks * BLOCK * 192, bytes_accessed=10 * 2**20, transcendentals=0
        ),
        name=f"residual_{first_row}",
    )(hidden_t, w, observed, keep, taper)


def halves_of(values):
    high = values.astype(BF16)
    return high, (values - high.astype(F32)).astype(BF16)


def dot_three(a, b):
    return dot(a[0], b[0]) + (dot(a[0], b[1]) + dot(a[1], b[0]))


def delay_kernel(pieces, x_ref, fh_ref, fl_ref, bh_ref, bl_ref, cos_ref, sin_ref, weight_ref, *outs):
    forward = (fh_ref[...], fl_ref[...])
    backward = (bh_ref[...], bl_ref[...])
    cosine, sine = cos_ref[...], sin_ref[...]
    count = x_ref.shape[1]
    members, local = x_ref.shape[0], x_ref.shape[3]
    turned = []
    for i in range(count):
        values = jnp.concatenate(
            [
                jnp.concatenate(
                    [x_ref[:, i, q * 2 + side].reshape(NBLOCKS, LANES) for side in range(2)], axis=1
                )
                for q in range(2)
            ],
            axis=0,
        )
        first = dot_three(forward, halves_of(values))
        real, imag = first[:NBLOCKS], first[NBLOCKS:]
        turned.append(
            jnp.concatenate([real * cosine + imag * sine, imag * cosine - real * sine], axis=1)
        )
    second = dot_three(halves_of(jnp.concatenate(turned, axis=0)), backward)
    factor = weight_ref[...] * (LOSS_SCALE / CHANNELS)
    factor = jnp.concatenate([jnp.concatenate([factor, factor], axis=1)] * count, axis=0)
    third = dot_three(halves_of(second * factor), forward)
    for i in range(count):
        part = third[i * NBLOCKS : (i + 1) * NBLOCKS]
        real, imag = part[:, :BLOCK], part[:, BLOCK:]
        back = jnp.concatenate([real * cosine - imag * sine, imag * cosine + real * sine], axis=0)
        fourth = dot_three(backward, halves_of(back))
        for q in range(2):
            for member in range(members):
                start = q * NBLOCKS + member * local
                for out_ref, size in zip(outs, pieces):
                    for side in range(2):
                        out_ref[member, i, q * 2 + side] = fourth[
                            start : start + size, side * LANES : (side + 1) * LANES
                        ]
                    start += size


def delay_filter(pieces, arrived, constants, weight, count=4):
    members, rows, _, local, _ = arrived.shape
    whole = lambda array: pl.BlockSpec(array.shape, lambda g: (0, 0))
    flops = rows * 4 * 3 * 2 * 512 * 512 * 256
    return pl.pallas_call(
        functools.partial(delay_kernel, pieces),
        grid=(rows // count,),
        in_specs=[
            pl.BlockSpec((members, count, PLANES, local, LANES), lambda g: (0, g, 0, 0, 0)),
            *[whole(array) for array in constants],
            whole(weight),
        ],
        out_specs=[
            pl.BlockSpec((members, count, PLANES, size, LANES), lambda g: (0, g, 0, 0, 0))
            for size in pieces
        ],
        out_shape=[
            jax.ShapeDtypeStruct((members, rows, PLANES, size, LANES), F32) for size in pieces
        ],
        compiler_params=params(),
        cost_estimate=pl.CostEstimate(flops=flops, bytes_accessed=12 * 2**20, transcendentals=0),
        name=f"delay_{len(pieces)}",
    )(arrived, *constants, weight)


def tail_kernel(first, g1_ref, g2_ref, hidden_ref, w_ref, keep_ref, taper_ref, before_ref,
                mine_ref, other_ref, hidden_grad_ref, weight_ref):
    step = pl.program_id(0)
    flats = [
        (ref.shape[0], ref.reshape(ref.shape[0] * 2 * STEP, LANES)) for ref in (g1_ref, g2_ref)
    ]

    @pl.when(pl.program_id(1) == 0)
    def _():
        weight_ref[...] = weight_of(keep_ref[...], taper_ref[...], (first + step) * STEP)

    @pl.when((step == 0) & (pl.program_id(1) == 0))
    def _():
        hidden_grad_ref[...] = before_ref[...]

    values = jnp.concatenate(
        [
            jnp.concatenate(
                [
                    flat[pl.ds(side * STEP + b, rows, stride=2 * STEP), :]
                    for b in range(STEP)
                    for side in range(2)
                ],
                axis=1,
            )
            for rows, flat in flats
        ],
        axis=0,
    )
    grad_field = (values * weight_ref[...]).astype(BF16)
    grad_out = dot(hidden_ref[...], grad_field)
    units = grad_out.shape[0] // 2
    for d in range(4):
        mine_ref[d, 0] = grad_out[d * 8 : (d + 1) * 8]
        other_ref[d, 0] = grad_out[units + d * 8 : units + (d + 1) * 8]
    hidden_grad_ref[...] += dot(w_ref[0], grad_field, NT)


def tail_part(first, count, g1, g2, hidden_order, w, keep, taper, before):
    units, total_rows = hidden_order.shape
    return pl.pallas_call(
        functools.partial(tail_kernel, first),
        grid=(count, 2),
        in_specs=[
            pl.BlockSpec((g1.shape[0], 2, STEP, LANES), lambda g, q: (0, q, first + g, 0)),
            pl.BlockSpec((g2.shape[0], 2, STEP, LANES), lambda g, q: (0, q, g, 0)),
            pl.BlockSpec((units, total_rows), lambda g, q: (0, 0)),
            pl.BlockSpec((1, units, WIDE), lambda g, q: (q, 0, first + g)),
            pl.BlockSpec(keep.shape, lambda g, q: (0, 0)),
            pl.BlockSpec((1, WIDE), lambda g, q: (0, first + g)),
            pl.BlockSpec((units, total_rows), lambda g, q: (0, 0)),
        ],
        out_specs=[
            pl.BlockSpec((4, 1, 8, WIDE), lambda g, q: (0, q, 0, g)),
            pl.BlockSpec((4, 1, 8, WIDE), lambda g, q: (0, q, 0, g)),
            pl.BlockSpec((units, total_rows), lambda g, q: (0, 0)),
        ],
        out_shape=[
            jax.ShapeDtypeStruct((4, 2, 8, count * WIDE), F32),
            jax.ShapeDtypeStruct((4, 2, 8, count * WIDE), F32),
            jax.ShapeDtypeStruct((units, total_rows), F32),
        ],
        scratch_shapes=[pltpu.VMEM((total_rows, WIDE), F32)],
        compiler_params=params(),
        cost_estimate=pl.CostEstimate(
            flops=count * 2 * 2 * 2 * 64 * 128 * WIDE, bytes_accessed=count * 4 * 2**20, transcendentals=0
        ),
        name=f"tail_{first}",
    )(g1, g2, hidden_order, w, keep, taper, before)


def terms_of(values, count):
    out = []
    for _ in range(count):
        term = values.astype(BF16)
        out.append(term)
        values = values - term.astype(F32)
    return out


def member_blocks(count):
    apart = [lax.axis_index("bl") ^ m for m in range(count)]
    return [(a // 4, a % 4) for a in apart]


def rows_kernel(index_ref, table_ref, features_ref, w_in_ref, inputs_ref, slope_ref, cells_ref):
    spots = member_blocks(index_ref.shape[0] * index_ref.shape[1])
    cells = jnp.concatenate([index_ref[f, n] for f, n in spots], axis=1).astype(jnp.int32)
    cells_ref[...] = cells
    summed = []
    for which, ref in ((0, table_ref), (1, features_ref)):
        total = 0.0
        for start in range(0, ref.shape[1], 512):
            size = min(512, ref.shape[1] - start)
            picked = one_hot_rows(cells[which : which + 1] - start, size)
            total = total + dot(ref[:, start : start + size], picked)
        summed.append(total)
    inputs = (summed[0] + summed[1]).astype(BF16)
    inputs_ref[...] = inputs
    pre_act = dot(w_in_ref[...], inputs, TN)
    sigmoid = 1.0 / (1.0 + jnp.exp(-pre_act))
    slope_ref[...] = sigmoid * (1.0 + pre_act * (1.0 - sigmoid))


def all_rows(index, uvw_table, baseline_features, w_in):
    rows = index.shape[0] * index.shape[1] * index.shape[3]
    return pl.pallas_call(
        rows_kernel,
        out_shape=[
            jax.ShapeDtypeStruct((w_in.shape[0], rows), BF16),
            jax.ShapeDtypeStruct((w_in.shape[1], rows), F32),
            jax.ShapeDtypeStruct((index.shape[2], rows), jnp.int32),
        ],
        compiler_params=params(),
        cost_estimate=pl.CostEstimate(flops=6 * 10**9, bytes_accessed=2**20, transcendentals=0),
        name="all_rows",
    )(index, uvw_table, baseline_features, w_in)


def scatter_kernel(own_ref, one_ref, two_ref, three_ref, inputs_ref, slope_ref, cells_ref, w_in_ref,
                   grad_in_ref, grad_uvw_ref, grad_base_ref):
    units = w_in_ref.shape[0]
    blocks = []
    for far, n in member_blocks(16):
        block = own_ref[n]
        for k, ref in ((1, one_ref), (2, two_ref), (3, three_ref)):
            block = jnp.where(far == k, ref[n], block)
        blocks.append(block)
    pre_grad = jnp.concatenate(blocks, axis=1) * slope_ref[...]
    grad_terms = jnp.concatenate(terms_of(pre_grad, 2), axis=0)
    parts = dot(inputs_ref[...], grad_terms, NT)
    grad_in_ref[...] = parts[:, :units] + parts[:, units:]
    input_grad = dot(w_in_ref[...], grad_terms[:units]) + dot(w_in_ref[...], grad_terms[units:])
    terms = jnp.concatenate(terms_of(input_grad, 2), axis=0)
    for which, out_ref in ((0, grad_uvw_ref), (1, grad_base_ref)):
        index = cells_ref[which : which + 1, :]
        cells = out_ref.shape[1]
        quarter = -(-cells // 4 // LANES) * LANES
        sides = [
            (index >= side * quarter) & (index < (side + 1) * quarter) for side in range(4)
        ]
        zero = jnp.zeros_like(terms)
        apart = jnp.concatenate([jnp.where(here, terms, zero) for here in sides], axis=0)
        index = index % quarter
        for start in range(0, quarter, 512):
            size = min(512, quarter - start)
            sums = dot(one_hot_rows(index - start, size), apart, NT).T
            for side in range(4):
                first = side * quarter + start
                wide = min(size, cells - first)
                part = sums[side * 2 * units : (side + 1) * 2 * units, :wide]
                out_ref[:, first : first + wide] = part[:units] + part[units:]


def scatter(blocks, known, w_in, cells, baselines):
    return pl.pallas_call(
        scatter_kernel,
        out_shape=[
            jax.ShapeDtypeStruct(w_in.shape, F32),
            jax.ShapeDtypeStruct((w_in.shape[0], cells), F32),
            jax.ShapeDtypeStruct((w_in.shape[0], baselines), F32),
        ],
        compiler_params=params(32 * 2**20),
        cost_estimate=pl.CostEstimate(
            flops=6 * 10**9, bytes_accessed=4 * 2**20, transcendentals=0
        ),
        name="scatter",
    )(*blocks, *known, w_in)


def swap(values, axis, distance):
    size = lax.axis_size(axis)
    return lax.ppermute(values, axis, [(i, i ^ distance) for i in range(size)])


def met(values, axis, distances):
    return [values, *[swap(values, axis, distance) for distance in distances]]


def sum_over_ch(values, *others):
    a, b, c, d = met(values, "ch", (2, 4, 6))
    total = after((a + b) + (c + d), *others)
    return total + swap(total, "ch", 1)


def sum_cores(mine, other, parts):
    return mine + swap(other, "bl", 1)


def far_parts(both):
    ring = lambda d: [(i, (i + 4 * d) % 16) for i in range(16)]
    return [both[0], *[lax.ppermute(both[d], "bl", ring(d)) for d in (1, 2, 3)]]


def sum_near(total):
    return total[:, :4] + swap(total[:, 4:], "bl", 2)


def together(*values):
    return lax.optimization_barrier(values)


def after(value, *others):
    return lax.optimization_barrier((value, *others))[0]


def body(
    uvw_index, row_baseline, flags, uvw_table, baseline_features, w_in, w_out, observed, delay_weight
):
    members = lax.axis_size("ch")
    rows = uvw_index.shape[0]
    local_blocks = flags.shape[1]
    local_channels = w_out.shape[2]
    head_rows = rows * 4 // 16

    taper = jnp.asarray(taper_table()).reshape(members, local_channels)
    hidden, hidden_t, keep, taper = trunk(
        uvw_index, row_baseline, flags, uvw_table, baseline_features, w_in, taper
    )
    constants = [jnp.asarray(table) for table in tables()]
    weight = delay_weight.reshape(BLOCK, NBLOCKS).T

    def exchange(values):
        size = values.shape[-2]
        return lax.all_to_all(
            values.reshape(members, -1, PLANES, size, LANES), "ch", 0, 0, tiled=True
        )

    def arrive(part):
        return exchange(part).reshape(-1, PLANES, part.shape[-2], LANES)

    part = residual_part(0, head_rows, hidden_t, w_out, observed, keep, taper)
    hidden_t = after(hidden_t, part)
    index = jnp.stack([uvw_index, row_baseline]).astype(F32)
    index = jnp.concatenate([index, jnp.zeros((6, rows), F32)], axis=0)
    index = jnp.stack([index, swap(index, "bl", 2)])
    sent_0 = exchange(after(part, index))
    index = after(index, part)
    across = swap(index, "bl", 1)
    index = jnp.stack([index[0], across[0], index[1], across[1]])
    index = jnp.stack(met(index, "bl", (4, 8, 12)))
    part = residual_part(head_rows, rows - head_rows, hidden_t, w_out, observed, keep, taper)
    sent_1 = exchange(after(part, index))

    me = lax.axis_index("bl")
    order = lax.broadcasted_iota(jnp.int32, hidden.shape[:1], 0)
    core, x_far, y_far, unit = order // 32, (order // 8) % 4, (order // 4) % 2, order % 4
    owner = ((me // 4 + x_far) % 4) * 4 + ((me // 2) % 2 ^ y_far) * 2 + (me % 2 ^ core)
    units = lax.broadcasted_iota(jnp.int32, (hidden.shape[0],) * 2, 1)
    turn = (units == (owner * 4 + unit)[:, None]).astype(BF16)
    hidden_order = dot(turn, hidden).astype(BF16)
    w = w_out.transpose(1, 0, 2)

    (part,) = delay_filter((local_blocks,), sent_0, constants, weight)
    known = all_rows(after(index, part), uvw_table, baseline_features, w_in)
    part = after(part, hidden_order, w, *known)
    back_0 = arrive(part)
    sizes = (local_blocks * 16 // 32, local_blocks * 16 // 32)
    counts = [size // STEP for size in sizes]
    parts = delay_filter(sizes, after(sent_1, part), constants, weight)

    piece = arrive(after(parts[0], back_0))
    late = after(parts[1], piece)
    mine, other, hidden_grad = tail_part(
        0, counts[0], back_0, piece, hidden_order, w, keep, taper, jnp.zeros(hidden.shape, F32)
    )
    both = sum_cores(mine, other, 1)
    piece = after(arrive(late), both)
    first = sum(far_parts(both))
    mine, other, hidden_grad = tail_part(
        counts[0], counts[1], back_0, piece, hidden_order, w, keep, taper, hidden_grad
    )
    both = sum_cores(mine, other, 1)
    hidden_grad = sum_over_ch(hidden_grad, both, first)
    second = far_parts(both)
    near = after(jnp.stack(met(hidden_grad, "bl", (1, 2, 3))), *second[1:])
    blocks = met(near, "bl", (4, 8, 12))
    grad_out = sum_near(jnp.concatenate([first, sum(second)], axis=2)).transpose(1, 0, 2)
    grad_in, grad_uvw, grad_base = scatter(
        blocks, known, w_in, uvw_table.shape[1], baseline_features.shape[1]
    )
    return (grad_out, grad_in, grad_uvw, grad_base)


def solution(mesh):
    return jax.shard_map(
        body,
        mesh=mesh,
        in_specs=(
            P("bl"),
            P("bl"),
            P("bl", "ch"),
            P(),
            P(),
            P(),
            P(None, None, "ch"),
            P(None, "ch", "bl"),
            P(),
        ),
        out_specs=(P("bl", None, "ch"), P(), P(), P()),
        check_vma=False,
    )
```
